32 devices in a mesh: dp: 8 (over z, core), fsdp: 4 (over y, x).
Axes of the slice: x: 2, y: 2, z: 4, core: 2. Of those that a mesh axis runs over, the one named last changes fastest.
Arguments:
- tokens: bfloat16 [128, 288, 768], P(('dp', 'fsdp')), may hold values from -6 to 6
- pair_lengths: int32 [128], P(('dp', 'fsdp')), may hold values from 36 to 288, as said below
- out_cotangent: bfloat16 [128, 288, 768], P(('dp', 'fsdp')), may hold values from -6 to 6
- retr_cotangent: bfloat16 [128, 128], P(('dp', 'fsdp')), may hold values from -6 to 6
- qkv_weight: bfloat16 [768, 2304], P(('dp', 'fsdp')), may hold values from -0.21875 to 0.21875
- query_bias: bfloat16 [768], P(('dp', 'fsdp')), may hold values from -3 to 3
- value_bias: bfloat16 [768], P(('dp', 'fsdp')), may hold values from -3 to 3
- out_weight: bfloat16 [768, 768], P(('dp', 'fsdp')), may hold values from -0.875 to 0.875
- out_bias: bfloat16 [768], P(('dp', 'fsdp')), may hold values from -3 to 3
- first_gain: bfloat16 [768], P(('dp', 'fsdp')), may hold values from 0.5 to 1.5
- first_shift: bfloat16 [768], P(('dp', 'fsdp')), may hold values from -2 to 2
- up_weight: bfloat16 [768, 3072], P(('dp', 'fsdp')), may hold values from -0.21875 to 0.21875
- up_bias: bfloat16 [3072], P(('dp', 'fsdp')), may hold values from -3 to 3
- down_weight: bfloat16 [3072, 768], P(('dp', 'fsdp')), may hold values from -0.21875 to 0.21875
- down_bias: bfloat16 [768], P(('dp', 'fsdp')), may hold values from -3 to 3
- second_gain: bfloat16 [768], P(('dp', 'fsdp')), may hold values from 0.5 to 1.5
- second_shift: bfloat16 [768], P(('dp', 'fsdp')), may hold values from -2 to 2
- retr_weight: bfloat16 [768, 128], P(('dp', 'fsdp')), may hold values from -0.21875 to 0.21875
Outputs:
- layer_output: bfloat16 [128, 288, 768], P(('dp', 'fsdp'))
- grad_tokens: bfloat16 [128, 288, 768], P(('dp', 'fsdp'))
- grad_qkv: float32 [768, 2304], P(('dp', 'fsdp'))
- grad_qbias: float32 [768], P(('dp', 'fsdp'))
- grad_vbias: float32 [768], P(('dp', 'fsdp'))
- grad_outw: float32 [768, 768], P(('dp', 'fsdp'))
- grad_outb: float32 [768], P(('dp', 'fsdp'))
- grad_fgain: float32 [768], P(('dp', 'fsdp'))
- grad_fshift: float32 [768], P(('dp', 'fsdp'))
- grad_upw: float32 [768, 3072], P(('dp', 'fsdp'))
- grad_upb: float32 [3072], P(('dp', 'fsdp'))
- grad_downw: float32 [3072, 768], P(('dp', 'fsdp'))
- grad_downb: float32 [768], P(('dp', 'fsdp'))
- grad_sgain: float32 [768], P(('dp', 'fsdp'))
- grad_sshift: float32 [768], P(('dp', 'fsdp'))
- grad_retr: float32 [768, 128], P(('dp', 'fsdp'))
The draws below stay inside these ranges and needn't reach their ends.
Inputs may be any that keep to these rules, and one draw needn't show every extreme that they name: `pair_lengths`: in each aligned block of 8 pairs (one query's retrieved documents) one pair has exactly 288 tokens, one, the null-document pair, has 36 to 72, and the others have 288 // 2 or more.
All inputs are finite; a program needn't handle non-finite values.
Results may differ from the reference program's by a relative error of at most 0.015.
Values may be sent and summed in bfloat16 or wider, within the bound.
No kernel may reach another device: no remote copies, remote signals or barrier semaphores. Data moves between devices by JAX's collectives and lax.ppermute only.
A program may use at most 192 MiB of HBM per device.

```python
import jax
import jax.numpy as jnp
from jax import lax

D = 768
H = 12
DH = 64
FF = 3072
PROJ = 128
SEQ = 288
PAIRS = 128


def draw_pair_lengths(key, part):
    key = jax.random.fold_in(key, 11)
    keys = jax.random.split(key, 4)
    blocks = PAIRS // 8
    common = jax.random.randint(keys[0], (blocks, 8), SEQ // 2, SEQ + 1)
    shorter = jax.random.randint(keys[1], (blocks, 8), SEQ // 8, SEQ // 4 + 1)
    full_slot = jax.random.randint(keys[2], (blocks, 1), 0, 8)
    offset = jax.random.randint(keys[3], (blocks, 1), 1, 8)
    null_slot = (full_slot + offset) % 8
    places = jnp.arange(8, dtype=jnp.int32)[None, :]
    lengths = jnp.where(places == full_slot, SEQ, jnp.where(places == null_slot, shorter, common))
    return lengths.reshape(PAIRS).astype(jnp.int32)


def block_levels(key, extent, cuts, low, largest):
    def one(axis_at, blocks):
        steps = jax.random.uniform(jax.random.fold_in(jax.random.fold_in(key, 6), axis_at), (blocks,), jnp.float32, low / len(cuts), largest / len(cuts))
        return jnp.repeat(jnp.exp(steps), extent[axis_at] // blocks).reshape((-1,) + (1,) * (len(extent) - axis_at - 1))

    gain = one(*cuts[0])
    for cut in cuts[1:]:
        gain = gain * one(*cut)
    return gain


def gaussian(rng, shape, scale, reach, pieces=(), held_as=jnp.bfloat16):
    values = scale * jax.random.normal(rng, shape, jnp.float32)
    if pieces:
        values = values * block_levels(rng, shape, pieces, -0.22, 0.18)
    return jnp.clip(values, -reach, reach).astype(held_as)


def setup_inputs(seed: int = 0) -> dict:
    splits = jax.random.split(jax.random.key(seed), 19)
    tokens = gaussian(splits[0], (PAIRS, SEQ, D), 1.0, 6.0, ((0, 32),))
    pair_lengths = draw_pair_lengths(jax.random.fold_in(splits[18], 71), 0)
    out_cotangent = gaussian(splits[2], (PAIRS, SEQ, D), 1.0, 6.0, ((0, 32),))
    retr_cotangent = gaussian(splits[3], (PAIRS, PROJ), 1.0, 6.0, ((0, 32),))
    qkv_weight = gaussian(splits[4], (D, 3 * D), D ** -0.5, 0.21875, ((0, 32),))
    query_bias = gaussian(splits[5], (D,), 0.5, 3.0, ((0, 32),))
    value_bias = gaussian(splits[6], (D,), 0.5, 3.0, ((0, 32),))
    out_weight = gaussian(splits[7], (D, D), (D // 16) ** -0.5, 0.875, ((0, 32),))
    out_bias = gaussian(splits[8], (D,), 0.5, 3.0, ((0, 32),))
    first_gain = jnp.clip(1.0 + 0.1 * jax.random.normal(splits[9], (D,), jnp.float32), 0.5, 1.5).astype(jnp.bfloat16)
    first_shift = gaussian(splits[10], (D,), 0.3, 2.0, ((0, 32),))
    up_weight = gaussian(splits[11], (D, FF), D ** -0.5, 0.21875, ((0, 32),))
    up_bias = gaussian(splits[12], (FF,), 0.5, 3.0, ((0, 32),))
    down_weight = gaussian(splits[13], (FF, D), (FF // 4) ** -0.5, 0.21875, ((0, 32),))
    down_bias = gaussian(splits[14], (D,), 0.5, 3.0, ((0, 32),))
    second_gain = jnp.clip(1.0 + 0.1 * jax.random.normal(splits[15], (D,), jnp.float32), 0.5, 1.5).astype(jnp.bfloat16)
    second_shift = gaussian(splits[16], (D,), 0.3, 2.0, ((0, 32),))
    retr_weight = gaussian(splits[17], (D, PROJ), D ** -0.5, 0.21875, ((0, 32),))
    return dict(tokens=tokens, pair_lengths=pair_lengths, out_cotangent=out_cotangent, retr_cotangent=retr_cotangent, qkv_weight=qkv_weight, query_bias=query_bias, value_bias=value_bias, out_weight=out_weight, out_bias=out_bias, first_gain=first_gain, first_shift=first_shift, up_weight=up_weight, up_bias=up_bias, down_weight=down_weight, down_bias=down_bias, second_gain=second_gain, second_shift=second_shift, retr_weight=retr_weight)


@jax.custom_vjp
def low(v):
    return lax.optimization_barrier(v.astype(jnp.bfloat16)).astype(jnp.float32)

@jax.custom_vjp
def low_back(v):
    return v

def low_keep(v):
    return (low(v), None)

def low_pass(kept, grad):
    return (grad,)

def back_keep(v):
    return (v, None)

def back_low(kept, grad):
    return (low(grad),)
low.defvjp(low_keep, low_pass)
low_back.defvjp(back_keep, back_low)
HIGHEST = lax.Precision.HIGHEST
EPSILON = 1e-12
SCALE = 0.125

def matmul(left, right):
    return jnp.dot(left, right, precision=HIGHEST)

def layer_norm(summed, norm_gain, norm_shift):
    average = lax.optimization_barrier(jnp.mean(summed, axis=-1, keepdims=True))
    centred = summed - average
    variance = lax.optimization_barrier(jnp.mean(centred * centred, axis=-1, keepdims=True))
    return centred * lax.rsqrt(variance + EPSILON) * norm_gain + norm_shift

def layer(inputs, lengths, params):
    qkv_weight, query_bias, value_bias, out_weight, out_bias, first_gain, first_shift, up_weight, up_bias, down_weight, down_bias, second_gain, second_shift, retr_weight = params
    group, seq_len, model_width = inputs.shape
    flat_rows = inputs.reshape(group * seq_len, model_width)
    qkv_bias = jnp.concatenate([query_bias, jnp.zeros_like(query_bias), value_bias])
    joint = low(low_back(matmul(flat_rows, qkv_weight) + qkv_bias))
    joint = joint.reshape(group, seq_len, 3, H, DH)
    queries = joint[:, :, 0]
    key_rows = joint[:, :, 1]
    values = joint[:, :, 2]
    scores = low_back(jnp.einsum('pqhd,pkhd->phqk', queries, key_rows, precision=HIGHEST) * SCALE)
    key_valid = (jnp.arange(seq_len, dtype=jnp.int32)[None, :] < lengths[:, None])[:, None, None, :]
    scores = jnp.where(key_valid, scores, -1e+30)
    row_max = lax.optimization_barrier(jnp.max(scores, axis=-1, keepdims=True))
    raised = jnp.exp(scores - row_max)
    attention = raised / lax.optimization_barrier(jnp.sum(raised, axis=-1, keepdims=True))
    context = jnp.einsum('phqk,pkhd->pqhd', low(attention), values, precision=HIGHEST)
    context = low(low_back(context.reshape(group * seq_len, model_width)))
    attended = low_back(matmul(context, out_weight) + out_bias)
    first_norm = layer_norm(flat_rows + attended, first_gain, first_shift)
    pre_gelu = low_back(matmul(low(first_norm), up_weight) + up_bias)
    active = low(jax.nn.gelu(pre_gelu, approximate=False))
    output = low_back(matmul(active, down_weight) + down_bias)
    result = layer_norm(first_norm + output, second_gain, second_shift)
    result = result.reshape(group, seq_len, model_width)
    retrieval = matmul(low(result[:, 0, :]), retr_weight)
    return (result, retrieval)

def reference(tokens, pair_lengths, out_cotangent, retr_cotangent, qkv_weight, query_bias, value_bias, out_weight, out_bias, first_gain, first_shift, up_weight, up_bias, down_weight, down_bias, second_gain, second_shift, retr_weight):
    params = tuple((item.astype(jnp.float32) for item in (qkv_weight, query_bias, value_bias, out_weight, out_bias, first_gain, first_shift, up_weight, up_bias, down_weight, down_bias, second_gain, second_shift, retr_weight)))
    groups = PAIRS // 8
    inputs_all = tokens.astype(jnp.float32).reshape(groups, 8, SEQ, D)
    lengths_all = pair_lengths.reshape(groups, 8)
    cot_all = out_cotangent.astype(jnp.float32).reshape(groups, 8, SEQ, D)
    retr_all = retr_cotangent.astype(jnp.float32).reshape(groups, 8, PROJ)

    def step(totals, block):
        inputs, lengths, cot_out, cot_retr = block

        def apply_layer(values_in, weights):
            return layer(values_in, lengths, weights)
        primal, pull = jax.vjp(apply_layer, inputs, params)
        grad_inputs, grad_params = pull((cot_out, cot_retr))
        totals = jax.tree.map(lambda left, right: left + right, totals, grad_params)
        return (totals, (primal[0], grad_inputs))
    start = jax.tree.map(lambda item: jnp.zeros(item.shape, jnp.float32), params)
    totals, (results, grads_in) = lax.scan(step, start, (inputs_all, lengths_all, cot_all, retr_all))
    return (results.reshape(PAIRS, SEQ, D).astype(jnp.bfloat16), grads_in.reshape(PAIRS, SEQ, D).astype(jnp.bfloat16), totals[0], totals[1], totals[2], totals[3], totals[4], totals[5], totals[6], totals[7], totals[8], totals[9], totals[10], totals[11], totals[12], totals[13])
```

```python
import functools
import math

import jax
import jax.numpy as jnp
from jax import lax
from jax.experimental import pallas as pl
from jax.experimental.pallas import tpu as pltpu
from jax.sharding import PartitionSpec as P

H = 12
DH = 64
D = H * DH
EPSILON = 1e-12
SCALE = 0.125
LOG2E = 1.4426950408889634
AXES = ("dp", "fsdp")
SMALL_ROWS = 8
VMEM_LIMIT = 60 * 1024 * 1024
BF = jnp.bfloat16
F32 = jnp.float32


def xor_masks(size, unit):
    return [(2 * (1 << b) - 1) * unit for b in range(size.bit_length() - 1)]


class Cube:
    def __init__(self, mesh):
        dp, fsdp = mesh.shape["dp"], mesh.shape["fsdp"]
        side = 1 << ((fsdp.bit_length() - 1) // 2)
        self.n = dp * fsdp
        self.core = fsdp
        xs = xor_masks(side, 1)
        ys = xor_masks(fsdp // side, side)
        zs = xor_masks(dp // 2, 2 * fsdp)
        self.links = xs + ys + zs

    def order(self, turn):
        links = self.links
        at = turn * len(links) // 4
        return links[at:] + links[:at]

    def swap(self, x, mask):
        return lax.ppermute(x, AXES, [(i, i ^ mask) for i in range(self.n)])

    @staticmethod
    def slots(order):
        out = [0]
        for mask in order:
            out = out + [s ^ mask for s in out]
        return out


def gather_params(cube, own_a, own_b):
    parts_a, parts_b = [], []
    known = [jnp.concatenate([a, b], axis=0)[None] for a, b in zip(own_a, own_b)]
    orders = [cube.order(j) for j in range(4)]
    rows_a = [a.shape[0] for a in own_a]
    steps = len(cube.links)
    halves = [None] * 4
    for r in range(steps - 1):
        got = [cube.swap(known[j], orders[j][r]) for j in range(4)]
        if r < steps - 2:
            known = [jnp.concatenate([k, g], axis=0) for k, g in zip(known, got)]
        else:
            halves = [
                (
                    jnp.concatenate([k[:, :ra], g[:, :ra]], axis=0),
                    jnp.concatenate([k[:, ra:], g[:, ra:]], axis=0),
                )
                for k, g, ra in zip(known, got, rows_a)
            ]
    for side, out in ((0, parts_a), (1, parts_b)):
        for j in range(4):
            base = cube.slots(orders[j][:-1])
            near = halves[j][side]
            far = cube.swap(near, orders[j][-1])
            pieces = [(near, base), (far, [s ^ orders[j][-1] for s in base])]
            pieces += [(cube.swap(p, cube.core), [s ^ cube.core for s in m]) for p, m in pieces]
            out.append(pieces)
    return parts_a, parts_b


def to_natural(me, array, distances):
    n = len(distances)
    source = me ^ jnp.asarray(distances, jnp.int32)
    pick = (lax.broadcasted_iota(jnp.int32, (n, n), 0) == source[None, :]).astype(array.dtype)
    flat = array.reshape(n, -1)
    return jnp.dot(pick, flat, preferred_element_type=F32).reshape(array.shape)


def natural_piece(me, pieces, rows):
    array = jnp.concatenate([p for p, _ in pieces], axis=0)[:, :rows]
    distances = sum([list(m) for _, m in pieces], [])
    whole = to_natural(me, array, distances).astype(array.dtype)
    return [(whole.reshape(1, -1, whole.shape[-1]), [None])]


def dot_nn(a, b):
    return jnp.dot(a, b, preferred_element_type=F32)


def dot_nt(a, b):
    return lax.dot_general(a, b, (((1,), (1,)), ((), ())), preferred_element_type=F32)


def dot_tn(a, b):
    return lax.dot_general(a, b, (((0,), (0,)), ((), ())), preferred_element_type=F32)


def start_load(me, refs, distances, place, sem):
    for ref, dist in zip(refs, distances):
        for slot, d in enumerate(dist):
            to = place(0) if d is None else place(lax.bitwise_xor(me, d))
            pltpu.make_async_copy(ref.at[slot], to, sem).start()


def wait_load(buf, sem):
    pltpu.make_async_copy(buf, buf, sem).wait()


def matrix(buf, rows):
    return buf[:, :rows, :].reshape(-1, buf.shape[-1])


def head_masks():
    lane = lax.broadcasted_iota(jnp.int32, (1, 2 * DH), 1)
    first = jnp.where(lane < DH, 1.0, 0.0)
    return first.astype(BF), (1.0 - first).astype(BF)


def attn_fwd_kernel(info, rows, meta_ref, x_ref, vec_ref, *refs):
    count = sum(len(d) for d in info)
    pieces, refs = refs[:count], refs[count:]
    joint_ref, p_ref, ctx_ref, r_ref = refs[:4]
    bufs, sems = refs[4:8], refs[8]
    me = meta_ref[0]
    pair = pl.program_id(0)

    @pl.when(pair == 0)
    def _():
        at = 0
        for j in range(4):
            start_load(me, pieces[at : at + len(info[j])], info[j], lambda i, j=j: bufs[j].at[i], sems.at[j])
            at += len(info[j])
        for j in range(4):
            wait_load(bufs[j], sems.at[j])

    x = x_ref[0]
    seq = x.shape[0]
    q = (dot_nn(x, matrix(bufs[0], rows)) + vec_ref[0:1, :]).astype(BF)
    k = dot_nn(x, matrix(bufs[1], rows)).astype(BF)
    v = (dot_nn(x, matrix(bufs[2], rows)) + vec_ref[1:2, :]).astype(BF)
    joint_ref[0, :, 0:D] = q
    joint_ref[0, :, D : 2 * D] = k
    joint_ref[0, :, 2 * D : 3 * D] = v
    length = meta_ref[1 + pair]
    key = lax.broadcasted_iota(jnp.int32, (1, seq), 1)
    mask = jnp.where(key < length, 0.0, -1e30)
    sides = head_masks()
    for h2 in range(H // 2):
        cols = slice(h2 * 2 * DH, (h2 + 1) * 2 * DH)
        q2, k2, v2 = q[:, cols], k[:, cols], v[:, cols]
        acc = None
        for hh in range(2):
            s = dot_nt(q2 * sides[hh], k2) * (SCALE * LOG2E) + mask
            e = jnp.exp2(s - jnp.max(s, axis=-1, keepdims=True))
            p = (e * (1.0 / jnp.sum(e, axis=-1, keepdims=True))).astype(BF)
            p_ref[0, 2 * h2 + hh] = p
            o = dot_nn(p, v2 * sides[hh])
            acc = o if acc is None else acc + o
        ctx_ref[0, :, cols] = acc.astype(BF)
    r_ref[0] = x.astype(F32) + dot_nn(ctx_ref[0], matrix(bufs[3], rows)) + vec_ref[2:3, :]


def norm_parts(r):
    centred = r - jnp.mean(r, axis=-1, keepdims=True)
    inverse = lax.rsqrt(jnp.mean(centred * centred, axis=-1, keepdims=True) + EPSILON)
    return centred * inverse, inverse


def norm_back(e, n, inverse, gain):
    scaled = e * gain
    return inverse * (
        scaled
        - jnp.mean(scaled, axis=-1, keepdims=True)
        - n * jnp.mean(scaled * n, axis=-1, keepdims=True)
    )


def gelu_parts(u):
    gauss = jnp.exp2(u * u * (-0.5 * LOG2E))
    t = 1.0 / (1.0 + (0.3275911 * 0.7071067811865476) * jnp.abs(u))
    poly = t * (
        0.5 * 0.254829592
        + t * (-0.5 * 0.284496736 + t * (0.5 * 1.421413741 + t * (-0.5 * 1.453152027 + t * (0.5 * 1.061405429))))
    )
    tail = poly * gauss
    phi = jnp.where(u >= 0.0, 1.0 - tail, tail)
    return u * phi, phi + u * gauss * 0.3989422804014327


def ffn_kernel(info, rows, meta_ref, r_ref, cot_ref, rcot_ref, vec_ref, upb_ref, retr_ref, *refs):
    count = sum(len(d) for d in info)
    pieces, refs = refs[:count], refs[count:]
    lo_ref, first_ref, act_ref, down_ref, upl_ref, attn_ref, gone_ref, gctx_ref, sums_ref = refs[:9]
    ups, dn, wo, slope_ref, sems = refs[9:13], refs[13], refs[14], refs[15], refs[16]
    me = meta_ref[0]
    pair = pl.program_id(0)
    units = dn.shape[0]
    whole = info[0][0][0] is None

    @pl.when(pair == 0)
    def _():
        at = 0
        for j in range(9):
            if j < 4:
                place, sem = (lambda i, j=j: ups[j].at[i]), sems.at[j]
            elif j < 8:
                if whole:
                    place, sem = (lambda i: dn.at[0]), sems.at[4]
                else:
                    place, sem = (lambda i, j=j: dn.at[i * 4 + (j - 4)]), sems.at[4]
            else:
                place, sem = (lambda i: wo.at[i]), sems.at[5]
            start_load(me, pieces[at : at + len(info[j])], info[j], place, sem)
            at += len(info[j])
        for j in range(4):
            wait_load(ups[j], sems.at[j])
        wait_load(dn, sems.at[4])
        wait_load(wo, sems.at[5])
        sums_ref[...] = jnp.zeros_like(sums_ref)

    vec = lambda i: vec_ref[i : i + 1, :]
    ff = 4
    group = units // ff

    def down(c):
        if whole:
            return dn[0, c * D : (c + 1) * D, :]
        return dn[c * group : (c + 1) * group].reshape(D, D)

    n1, inv1 = norm_parts(r_ref[0])
    first_norm = n1 * vec(3) + vec(4)
    first_low = first_norm.astype(BF)
    first_ref[0] = first_low
    output = first_norm + vec(5)
    for c in range(ff):
        cols = slice(c * D, (c + 1) * D)
        pre = dot_nn(first_low, matrix(ups[c], rows)) + upb_ref[c : c + 1, :]
        active, slope = gelu_parts(pre)
        active = active.astype(BF)
        act_ref[0, :, cols] = active
        slope_ref[:, cols] = slope
        output = output + dot_nn(active, down(c))
    n2, inv2 = norm_parts(output)
    result = n2 * vec(6) + vec(7)
    lo_ref[0] = result.astype(BF)
    head = dot_nt(rcot_ref[0], retr_ref[...])
    row = lax.broadcasted_iota(jnp.int32, (n2.shape[0], 1), 0)
    e = cot_ref[0].astype(F32) + jnp.where(row == 0, head, 0.0)
    total = lambda a: jnp.sum(a, axis=0, keepdims=True)
    sums_ref[0:1, :] += total(e * n2)
    sums_ref[1:2, :] += total(e)
    g_second = norm_back(e, n2, inv2, vec(6))
    down_low = g_second.astype(BF)
    down_ref[0] = down_low
    sums_ref[2:3, :] += total(down_low.astype(F32))
    g_first = g_second
    for c in range(ff):
        cols = slice(c * D, (c + 1) * D)
        up_low = (dot_nt(down_low, down(c)) * slope_ref[:, cols]).astype(BF)
        upl_ref[0, :, cols] = up_low
        sums_ref[8 + c : 9 + c, :] += total(up_low.astype(F32))
        g_first = g_first + dot_nt(up_low, matrix(ups[c], rows))
    sums_ref[3:4, :] += total(g_first * n1)
    sums_ref[4:5, :] += total(g_first)
    g_one = norm_back(g_first, n1, inv1, vec(3))
    gone_ref[0] = g_one
    attn_low = g_one.astype(BF)
    attn_ref[0] = attn_low
    sums_ref[5:6, :] += total(attn_low.astype(F32))
    gctx_ref[0] = dot_nt(attn_low, matrix(wo, rows)).astype(BF)


def attn_bwd_kernel(info, rows, meta_ref, joint_ref, p_ref, gctx_ref, gone_ref, *refs):
    count = sum(len(d) for d in info)
    pieces, refs = refs[:count], refs[count:]
    gj_ref, gt_ref, sums_ref = refs[:3]
    bufs, sems = refs[3:6], refs[6]
    me = meta_ref[0]
    pair = pl.program_id(0)

    @pl.when(pair == 0)
    def _():
        at = 0
        for j in range(3):
            start_load(me, pieces[at : at + len(info[j])], info[j], lambda i, j=j: bufs[j].at[i], sems.at[j])
            at += len(info[j])
        for j in range(3):
            wait_load(bufs[j], sems.at[j])
        sums_ref[...] = jnp.zeros_like(sums_ref)

    sides = head_masks()
    for h2 in range(H // 2):
        cut = lambda base: slice(base + h2 * 2 * DH, base + (h2 + 1) * 2 * DH)
        q2 = joint_ref[0, :, cut(0)]
        k2 = joint_ref[0, :, cut(D)]
        v2 = joint_ref[0, :, cut(2 * D)]
        go2 = gctx_ref[0, :, cut(0)]
        gq = gk = gv = 0.0
        for hh in range(2):
            go = go2 * sides[hh]
            p = p_ref[0, 2 * h2 + hh]
            gw = dot_nt(go, v2)
            pf = p.astype(F32)
            t = gw * pf
            gs = (t - pf * jnp.sum(t, axis=-1, keepdims=True)).astype(BF)
            gv = gv + dot_tn(p, go)
            gq = gq + dot_nn(gs, k2 * sides[hh])
            gk = gk + dot_tn(gs, q2 * sides[hh])
        gj_ref[0, :, cut(0)] = (gq * SCALE).astype(BF)
        gj_ref[0, :, cut(D)] = (gk * SCALE).astype(BF)
        gj_ref[0, :, cut(2 * D)] = gv.astype(BF)
    acc = gone_ref[0]
    for j in range(3):
        acc = acc + dot_nt(gj_ref[0, :, j * D : (j + 1) * D], matrix(bufs[j], rows))
    gt_ref[0] = acc.astype(BF)
    for row, j in ((0, 0), (1, 2)):
        part = gj_ref[0, :, j * D : (j + 1) * D].astype(F32)
        sums_ref[row : row + 1, :] += jnp.sum(part, axis=0, keepdims=True)


def grad_kernel(slots, core, rows, meta_ref, a_ref, b_ref, keep_ref, send_ref, acc_ref):
    me = meta_ref[0]
    acc_ref[...] = dot_tn(a_ref[...], b_ref[...]).reshape(acc_ref.shape)
    for s, d in enumerate(slots):
        keep_ref[s, 0] = acc_ref[lax.bitwise_xor(me, d)].astype(BF)
        send_ref[s, 0] = acc_ref[lax.bitwise_xor(me, d ^ core)].astype(BF)


def grad_rows_kernel(slots, core, meta_ref, a_ref, b_ref, keep_ref, send_ref, acc_ref):
    me = meta_ref[0]
    block = pl.program_id(0)
    count = keep_ref.shape[0] * 2 // pl.num_programs(0)
    per = acc_ref.shape[0]
    acc_ref[...] = dot_tn(a_ref[...], b_ref[...]).reshape(acc_ref.shape)
    for s, d in enumerate(slots):
        for ref, extra in ((keep_ref, 0), (send_ref, core)):
            owner = lax.bitwise_xor(me, d ^ extra)
            at = owner - block * per

            @pl.when(jnp.logical_and(at >= 0, at < per))
            def _(ref=ref, at=at, s=s):
                ref[s] = acc_ref[at].astype(BF)


def grad_plain_kernel(meta_ref, a_ref, b_ref, out_ref):
    out_ref[...] = dot_tn(a_ref[...], b_ref[...]).astype(BF)


def flat(parts):
    arrays = [p for pieces in parts for p, _ in pieces]
    info = [[list(m) for _, m in pieces] for pieces in parts]
    return arrays, info


def spec_any(n):
    return [pl.BlockSpec(memory_space=pl.ANY)] * n


def params():
    return pltpu.CompilerParams(dimension_semantics=("arbitrary",), vmem_limit_bytes=VMEM_LIMIT)


def pair_spec(*shape):
    return pl.BlockSpec((1,) + shape, lambda p, *_: (p,) + (0,) * len(shape))


def full_spec(*shape):
    return pl.BlockSpec(shape, lambda p, *_: (0,) * len(shape))


def weight_buffer(pieces):
    count = sum(len(m) for _, m in pieces)
    return pltpu.VMEM((count,) + pieces[0][0].shape[1:], BF)


def attention_forward(meta, rows, tokens, vecs, parts):
    pairs, seq, _ = tokens.shape
    arrays, info = flat(parts)
    return pl.pallas_call(
        functools.partial(attn_fwd_kernel, info, rows),
        out_shape=(
            jax.ShapeDtypeStruct((pairs, seq, 3 * D), BF),
            jax.ShapeDtypeStruct((pairs, H, seq, seq), BF),
            jax.ShapeDtypeStruct((pairs, seq, D), BF),
            jax.ShapeDtypeStruct((pairs, seq, D), F32),
        ),
        grid_spec=pltpu.PrefetchScalarGridSpec(
            num_scalar_prefetch=1,
            grid=(pairs,),
            in_specs=[pair_spec(seq, D), full_spec(*vecs.shape)] + spec_any(len(arrays)),
            out_specs=(
                pair_spec(seq, 3 * D),
                pair_spec(H, seq, seq),
                pair_spec(seq, D),
                pair_spec(seq, D),
            ),
            scratch_shapes=[weight_buffer(p) for p in parts] + [pltpu.SemaphoreType.DMA((4,))],
        ),
        compiler_params=params(),
        name="attention_forward",
    )(meta, tokens, vecs, *arrays)


def feed_forward(meta, rows, r, cot, rcot, vecs, upb, retr, parts):
    pairs, seq, _ = r.shape
    arrays, info = flat(parts)
    ff = 4 * D
    down_shape = (4 * sum(len(m) for _, m in parts[4]),) + parts[4][0][0].shape[1:]
    if info[0][0][0] is None:
        down_shape = parts[4][0][0].shape
    wide = lambda n, t: jax.ShapeDtypeStruct((pairs, seq, n), t)
    return pl.pallas_call(
        functools.partial(ffn_kernel, info, rows),
        out_shape=(
            wide(D, BF),
            wide(D, BF),
            wide(ff, BF),
            wide(D, BF),
            wide(ff, BF),
            wide(D, BF),
            wide(D, F32),
            wide(D, BF),
            jax.ShapeDtypeStruct((16, D), F32),
        ),
        grid_spec=pltpu.PrefetchScalarGridSpec(
            num_scalar_prefetch=1,
            grid=(pairs,),
            in_specs=[
                pair_spec(seq, D),
                pair_spec(seq, D),
                pair_spec(1, rcot.shape[-1]),
                full_spec(*vecs.shape),
                full_spec(*upb.shape),
                full_spec(*retr.shape),
            ]
            + spec_any(len(arrays)),
            out_specs=(
                pair_spec(seq, D),
                pair_spec(seq, D),
                pair_spec(seq, ff),
                pair_spec(seq, D),
                pair_spec(seq, ff),
                pair_spec(seq, D),
                pair_spec(seq, D),
                pair_spec(seq, D),
                full_spec(16, D),
            ),
            scratch_shapes=[weight_buffer(p) for p in parts[:4]]
            + [
                pltpu.VMEM(down_shape, BF),
                weight_buffer(parts[8]),
                pltpu.VMEM((seq, ff), F32),
                pltpu.SemaphoreType.DMA((6,)),
            ],
        ),
        compiler_params=params(),
        name="feed_forward",
    )(meta, r, cot, rcot, vecs, upb, retr, *arrays)


def attention_backward(meta, rows, joint, probs, gctx, gone, parts):
    pairs, seq, _ = joint.shape
    arrays, info = flat(parts)
    return pl.pallas_call(
        functools.partial(attn_bwd_kernel, info, rows),
        out_shape=(
            jax.ShapeDtypeStruct((pairs, seq, 3 * D), BF),
            jax.ShapeDtypeStruct((pairs, seq, D), BF),
            jax.ShapeDtypeStruct((8, D), F32),
        ),
        grid_spec=pltpu.PrefetchScalarGridSpec(
            num_scalar_prefetch=1,
            grid=(pairs,),
            in_specs=[
                pair_spec(seq, 3 * D),
                pair_spec(H, seq, seq),
                pair_spec(seq, D),
                pair_spec(seq, D),
            ]
            + spec_any(len(arrays)),
            out_specs=(pair_spec(seq, 3 * D), pair_spec(seq, D), full_spec(8, D)),
            scratch_shapes=[weight_buffer(p) for p in parts] + [pltpu.SemaphoreType.DMA((3,))],
        ),
        compiler_params=params(),
        name="attention_backward",
    )(meta, joint, probs, gctx, gone, *arrays)


def weight_grad(cube, meta, order, a, b):
    total = a.shape[0]
    units = b.shape[1] // D
    shard = D // cube.n
    slots = cube.slots(order)
    if shard % 8:
        whole = pl.pallas_call(
            grad_plain_kernel,
            out_shape=jax.ShapeDtypeStruct((D, units * D), BF),
            grid_spec=pltpu.PrefetchScalarGridSpec(
                num_scalar_prefetch=1,
                grid=(units,),
                in_specs=[full_spec(total, D), pl.BlockSpec((total, D), lambda j, *_: (0, j))],
                out_specs=pl.BlockSpec((D, D), lambda j, *_: (0, j)),
            ),
            compiler_params=params(),
            name="weight_grad",
        )(meta, a, b)
        whole = whole.reshape(cube.n, shard, units, D).transpose(0, 2, 1, 3)
        at = jnp.asarray(slots, jnp.int32)
        return whole[meta[0] ^ at], whole[meta[0] ^ cube.core ^ at]
    half = cube.n // 2
    return pl.pallas_call(
        functools.partial(grad_kernel, slots, cube.core, shard),
        out_shape=(jax.ShapeDtypeStruct((half, units, shard, D), BF),) * 2,
        grid_spec=pltpu.PrefetchScalarGridSpec(
            num_scalar_prefetch=1,
            grid=(units,),
            in_specs=[full_spec(total, D), pl.BlockSpec((total, D), lambda j, *_: (0, j))],
            out_specs=(pl.BlockSpec((half, 1, shard, D), lambda j, *_: (0, j, 0, 0)),) * 2,
            scratch_shapes=[pltpu.VMEM((cube.n, shard, D), F32)],
        ),
        compiler_params=params(),
        name="weight_grad",
    )(meta, a, b)


def weight_grad_rows(cube, meta, order, a, b):
    total = a.shape[0]
    units = a.shape[1] // D
    shard = a.shape[1] // cube.n
    slots = cube.slots(order)
    if shard % 8:
        whole = pl.pallas_call(
            grad_plain_kernel,
            out_shape=jax.ShapeDtypeStruct((units * D, D), BF),
            grid_spec=pltpu.PrefetchScalarGridSpec(
                num_scalar_prefetch=1,
                grid=(units,),
                in_specs=[pl.BlockSpec((total, D), lambda j, *_: (0, j)), full_spec(total, D)],
                out_specs=pl.BlockSpec((D, D), lambda j, *_: (j, 0)),
            ),
            compiler_params=params(),
            name="weight_grad_rows",
        )(meta, a, b)
        whole = whole.reshape(cube.n, shard, D)
        at = jnp.asarray(slots, jnp.int32)
        return whole[meta[0] ^ at], whole[meta[0] ^ cube.core ^ at]
    half = cube.n // 2
    return pl.pallas_call(
        functools.partial(grad_rows_kernel, slots, cube.core),
        out_shape=(jax.ShapeDtypeStruct((half, shard, D), BF),) * 2,
        grid_spec=pltpu.PrefetchScalarGridSpec(
            num_scalar_prefetch=1,
            grid=(units,),
            in_specs=[pl.BlockSpec((total, D), lambda j, *_: (0, j)), full_spec(total, D)],
            out_specs=(full_spec(half, shard, D),) * 2,
            scratch_shapes=[pltpu.VMEM((D // shard, shard, D), F32)],
        ),
        compiler_params=params(),
        name="weight_grad_rows",
    )(meta, a, b)


def reduce_to_owner(cube, order, keep, send):
    def add(a, b):
        return a.astype(F32) + b.astype(F32)

    got = cube.swap(send, cube.core)
    for mask in reversed(order):
        half = keep.shape[0] // 2
        away = add(keep[half:], got[half:]).astype(BF)
        keep = add(keep[:half], got[:half]).astype(BF)
        got = cube.swap(away, mask)
    return add(keep[0], got[0])


def per_device(cube, tokens, pair_lengths, out_cotangent, retr_cotangent, *weights):
    (
        qkv_weight,
        query_bias,
        value_bias,
        out_weight,
        out_bias,
        first_gain,
        first_shift,
        up_weight,
        up_bias,
        down_weight,
        down_bias,
        second_gain,
        second_shift,
        retr_weight,
    ) = weights
    me = (lax.axis_index("dp") * lax.axis_size("fsdp") + lax.axis_index("fsdp")).astype(jnp.int32)
    n = cube.n
    rows = D // n
    pairs, seq, _ = tokens.shape
    proj = retr_weight.shape[1]
    meta = jnp.concatenate([me[None], pair_lengths])

    vec_list = [query_bias, value_bias, out_bias, first_gain, first_shift, down_bias, second_gain, second_shift]
    small = jnp.concatenate([retr_weight.reshape(-1)] + vec_list + [up_bias])
    small = jnp.pad(small, (0, SMALL_ROWS * D - small.shape[0])).reshape(SMALL_ROWS, D)
    own_a = [qkv_weight[:, j * D : (j + 1) * D] for j in range(3)]
    own_a.append(jnp.concatenate([out_weight, small], axis=0))
    own_b = [
        jnp.concatenate([up_weight[:, j * D : (j + 1) * D], down_weight[j * rows : (j + 1) * rows]], axis=0)
        for j in range(4)
    ]
    parts_a, parts_b = gather_params(cube, own_a, own_b)

    small_all = jnp.concatenate([p[:, rows:] for p, _ in parts_a[3]], axis=0)
    distances = sum([list(m) for _, m in parts_a[3]], [])
    small_all = to_natural(me, small_all, distances).reshape(n, SMALL_ROWS * D)
    cut = rows * proj
    retr_full = small_all[:, :cut].reshape(D, proj).astype(BF)
    vecs = small_all[:, cut : cut + 8 * rows].reshape(n, 8, rows).transpose(1, 0, 2).reshape(8, D)
    upb = small_all[:, cut + 8 * rows : cut + 12 * rows].reshape(4, D)

    if rows % 8:
        units_a = [natural_piece(me, p, rows) for p in parts_a]
        ups = [natural_piece(me, [(a[:, :rows], m) for a, m in p], rows) for p in parts_b]
        four = [[(a[:, rows:], m) for a, m in p] for p in parts_b]
        four = [natural_piece(me, p, rows)[0][0].reshape(n, rows, D) for p in four]
        whole = jnp.stack(four, axis=1).reshape(1, 4 * D, D)
        downs = [[(whole, [None])]] + [[]] * 3
        kernel_rows = D
    else:
        units_a = parts_a
        ups = [[(a[:, :rows], m) for a, m in p] for p in parts_b]
        downs = [[(a[:, rows:], m) for a, m in p] for p in parts_b]
        kernel_rows = rows

    joint, probs, ctx, r = attention_forward(meta, kernel_rows, tokens, vecs, units_a)
    rcot = retr_cotangent[:, None, :]
    (layer_output, first_low, active, down_low, up_low, attn_low, g_one, g_ctx, sums) = feed_forward(
        meta, kernel_rows, r, out_cotangent, rcot, vecs, upb, retr_full, ups + downs + [units_a[3]]
    )
    rows_of = lambda a: a.reshape(pairs * seq, a.shape[-1])
    grad_retr = lax.dot_general(
        layer_output[:, 0, :], retr_cotangent, (((0,), (0,)), ((), ())), preferred_element_type=F32
    )

    orders = [cube.order(j) for j in range(4)]
    down_keep, down_send = weight_grad_rows(cube, meta, orders[0], rows_of(active), rows_of(down_low))
    grad_downw = reduce_to_owner(cube, orders[0], down_keep, down_send)
    up_keep, up_send = weight_grad(cube, meta, orders[2], rows_of(first_low), rows_of(up_low))
    grad_upw = reduce_to_owner(cube, orders[2], up_keep, up_send)
    out_keep, out_send = weight_grad(cube, meta, orders[3], rows_of(ctx), rows_of(attn_low))

    g_joint, grad_tokens, sums_qv = attention_backward(
        meta, kernel_rows, joint, probs, g_ctx, g_one, units_a[:3]
    )

    by_owner = lambda v: v.reshape(n, -1)
    small_grad = jnp.concatenate(
        [
            by_owner(grad_retr),
            by_owner(sums_qv[0]),
            by_owner(sums_qv[1]),
            by_owner(sums[5]),
            by_owner(sums[3]),
            by_owner(sums[4]),
            by_owner(sums[2]),
            by_owner(sums[0]),
            by_owner(sums[1]),
            by_owner(sums[8:12]),
        ],
        axis=1,
    )
    small_grad = jnp.pad(small_grad, ((0, 0), (0, SMALL_ROWS * D - small_grad.shape[1])))
    small_grad = small_grad.astype(BF).reshape(n, SMALL_ROWS, D)
    slots = jnp.asarray(cube.slots(orders[3]), jnp.int32)
    source = jnp.concatenate([me ^ slots, me ^ cube.core ^ slots])
    pick = (lax.broadcasted_iota(jnp.int32, (n, n), 1) == source[:, None]).astype(BF)
    small_grad = (
        jnp.dot(pick, small_grad.reshape(n, -1), preferred_element_type=F32)
        .astype(BF)
        .reshape(n, 1, SMALL_ROWS, D)
    )
    half = n // 2
    qkv_terms = [
        weight_grad(cube, meta, orders[j], rows_of(tokens), rows_of(g_joint)[:, j * D : (j + 1) * D])
        for j in range(3)
    ]
    grad_qkv = [reduce_to_owner(cube, orders[j], *qkv_terms[j])[0] for j in range(3)]
    last = reduce_to_owner(
        cube,
        orders[3],
        jnp.concatenate([out_keep, small_grad[:half]], axis=2),
        jnp.concatenate([out_send, small_grad[half:]], axis=2),
    )[0]
    grad_outw = last[:rows]
    own = last[rows:].reshape(-1)
    take = lambda i, k=1: own[cut + i * rows : cut + (i + k) * rows]
    return (
        layer_output,
        grad_tokens,
        jnp.concatenate(grad_qkv, axis=1),
        take(0),
        take(1),
        grad_outw,
        take(2),
        take(3),
        take(4),
        jnp.concatenate([grad_upw[j] for j in range(4)], axis=1),
        take(8, 4),
        grad_downw,
        take(5),
        take(6),
        take(7),
        own[:cut].reshape(rows, proj),
    )


def solution(mesh):
    row = P(AXES)
    in_specs = (row,) * 18
    out_specs = (row,) * 16
    return jax.shard_map(
        functools.partial(per_device, Cube(mesh)),
        mesh=mesh,
        in_specs=in_specs,
        out_specs=out_specs,
        check_vma=False,
    )
```

```python
import functools

import jax
import jax.numpy as jnp
from jax import lax
from jax.experimental import pallas as pl
from jax.experimental.pallas import tpu as pltpu
from jax.sharding import PartitionSpec as P

H = 12
DH = 64
D = H * DH
EPSILON = 1e-12
SCALE = 0.125
LOG2E = 1.4426950408889634
AXES = ("dp", "fsdp")
GROUPS = 3
FEW, MANY = 2, 4
VMEM_LIMIT = 60 * 1024 * 1024
BF = jnp.bfloat16
F32 = jnp.float32


def xor_masks(size, unit):
    return [(2 * (1 << b) - 1) * unit for b in range(size.bit_length() - 1)]


class Cube:
    def __init__(self, mesh):
        dp, fsdp = mesh.shape["dp"], mesh.shape["fsdp"]
        side = 1 << ((fsdp.bit_length() - 1) // 2)
        self.n = dp * fsdp
        self.core = fsdp
        self.core_bit = fsdp.bit_length() - 1
        self.flat = xor_masks(side, 1) + xor_masks(fsdp // side, side)
        self.deep = xor_masks(dp // 2, 2 * fsdp)
        self.rounds = len(self.flat) + len(self.deep)
        self.rows = D // self.n
        self.sub = self.rows // GROUPS
        self.small = -(-8 // self.sub)
        self.tiled = self.sub % 8 == 0

    def half(self, i):
        return (i >> self.core_bit) & 1

    def order(self, part):
        turn = -1 if part >= 2 else 1
        flat, deep = self.flat[::turn], self.deep[::turn]
        return deep + flat if part % 2 else flat + deep

    def dist(self, part):
        out = [0]
        for mask in [self.core] + self.order(part):
            out = out + [s ^ mask for s in out]
        return out

    def slot(self, part):
        table = [0] * self.n
        for at, d in enumerate(self.dist(part)):
            table[d] = at
        return table

    def swap_core(self, x):
        return lax.ppermute(x, AXES, [(i, i ^ self.core) for i in range(self.n)])

    def swap(self, x, role, r):
        return lax.ppermute(x, AXES, [(i, i ^ self.order(2 * self.half(i) + role)[r]) for i in range(self.n)])


class Gather:
    def __init__(self, cube, mine, send):
        self.cube = cube
        got = cube.swap_core(send)
        cut = 3 * FEW
        known = [jnp.stack([a, b]) for a, b in ((mine[:cut], got[:cut]), (mine[cut:], got[cut:]))]
        first = [FEW, MANY + cube.small]
        for r in range(cube.rounds - 1):
            got = [cube.swap(known[role], role, r) for role in range(2)]
            known, got = lax.optimization_barrier((known, got))
            if r < cube.rounds - 2:
                known = [jnp.concatenate([a, b], axis=0) for a, b in zip(known, got)]
        self.near_a = [jnp.concatenate([a[:, :f], b[:, :f]], axis=0) for a, b, f in zip(known, got, first)]
        self.rest = [(a[:, f:], b[:, f:]) for a, b, f in zip(known, got, first)]

    def link(self, near):
        return [self.cube.swap(near[role], role, self.cube.rounds - 1) for role in range(2)]

    def pieces(self, near, far, near_other, far_other):
        half = self.cube.n // 2
        out = []
        for role in range(2):
            out += [(near[role], role, 0, 0), (far[role], role, 0, half)]
            out += [(near_other[role], role, 1, 0), (far_other[role], role, 1, half)]
        return out

    def side_a(self):
        core = self.cube.swap_core
        near_a = self.near_a
        far = self.link(near_a)
        near_b = [jnp.concatenate(pair, axis=0) for pair in self.rest]
        near_a, far, near_b = lax.optimization_barrier((near_a, far, near_b))
        self.near_b = near_b
        out = self.pieces(near_a, far, [core(x) for x in near_a], [core(x) for x in far])
        self.far_b = self.link(near_b)
        return out

    def side_b(self, after):
        after, self.near_b, self.far_b = lax.optimization_barrier((after, self.near_b, self.far_b))
        other = [[self.cube.swap_core(x) for x in side] for side in (self.near_b, self.far_b)]
        return after, self.pieces(self.near_b, self.far_b, *other)


def half_blocks(cube, me, core, pieces, half):
    out = []
    for role in range(2):
        mine, other = [
            jnp.concatenate([p for p, r, w, _ in pieces if r == role and w == whose], axis=0) for whose in range(2)
        ]
        array = jnp.where(core == half, mine, other)
        base = jnp.where(core == half, me, me ^ cube.core)
        table = jnp.asarray(cube.slot(2 * half + role), jnp.int32)
        out.append(jnp.take(array, table[jnp.arange(cube.n, dtype=jnp.int32) ^ base], axis=0))
    return out


def two_units(few, many):
    return jnp.concatenate([few, many[:, :1]], axis=1), many[:, 1:]


class Meta:
    def __init__(self, cube, pairs):
        self.lengths = 2
        self.dist = 2 + pairs
        self.slot = self.dist + 4 * cube.n

    @staticmethod
    def build(cube, me, core, pair_lengths):
        tables = [cube.dist(p) for p in range(4)] + [cube.slot(p) for p in range(4)]
        tables = jnp.asarray(sum(tables, []), jnp.int32)
        return jnp.concatenate([me[None], core[None], pair_lengths, tables])


def dot_nn(a, b):
    return jnp.dot(a, b, preferred_element_type=F32)


def dot_nt(a, b):
    return lax.dot_general(a, b, (((1,), (1,)), ((), ())), preferred_element_type=F32)


def dot_tn(a, b):
    return lax.dot_general(a, b, (((0,), (0,)), ((), ())), preferred_element_type=F32)


def params():
    return pltpu.CompilerParams(dimension_semantics=("arbitrary",), vmem_limit_bytes=VMEM_LIMIT)


def cost(macs, moved):
    return pl.CostEstimate(flops=2 * macs, bytes_accessed=moved, transcendentals=0)


def pair_spec(*shape, first=0):
    return pl.BlockSpec((1,) + shape, lambda p, *_: (p + first,) + (0,) * len(shape))


def full_spec(*shape):
    return pl.BlockSpec(shape, lambda p, *_: (0,) * len(shape))


def any_specs(n):
    return [pl.BlockSpec(memory_space=pl.ANY)] * n


class Weights:
    def __init__(self, cube, layout, pieces=(), natural=()):
        self.cube, self.layout = cube, layout
        self.arrays = list(natural) if natural else [p[0] for p in pieces]
        self.what = [p[1:] for p in pieces]

    def copies(self, refs, meta, place):
        cube = self.cube
        me, core = meta[0], meta[1]
        for ref, (role, whose, first) in zip(refs, self.what):
            half = lax.bitwise_xor(core, whose)
            base = lax.bitwise_xor(me, whose * cube.core)
            table = self.layout.dist + (2 * half + role) * cube.n + first
            for at in range(ref.shape[0]):
                device = lax.bitwise_xor(base, meta[table + at])
                for source, target, sem in place(ref, at, role, half, device):
                    pltpu.make_async_copy(source, target, sem).start()


def runs(role, first=0):
    if role == 0:
        return [(slice(first, first + FEW), 0, slice(0, FEW))]
    return [
        (slice(first, first + 1), 0, slice(FEW, GROUPS)),
        (slice(first + 1, first + MANY), 1, slice(0, GROUPS)),
    ]


def wait_load(buf, sem):
    pltpu.make_async_copy(buf, buf, sem).wait()


def square(cube, slabs):
    return slabs.reshape(D, D) if cube.tiled else slabs


def pack_kernel(cube, meta, qkv, out, up, down, retr, vec, upb, mine, send):
    sub, rows = cube.sub, cube.rows

    def blocks(half):
        return [(2 * half + i // GROUPS, i % GROUPS * sub) for i in range(2 * GROUPS)]

    def put(ref, half):
        at = 0
        for chosen, extra in ((blocks(half)[:FEW], 0), (blocks(half)[FEW:], cube.small)):
            for unit, row in chosen:
                part = slice(unit * D, (unit + 1) * D)
                ref[at] = qkv[row : row + sub, part] if unit < 3 else out[row : row + sub, :]
                at += 1
            if extra:
                ref[at] = jnp.zeros((sub, D), BF)
                if half == 0:
                    ref[at, 0:8, 0:rows] = vec[...]
                    ref[at, 0:1, 128 : 128 + 4 * rows] = upb[...]
                else:
                    for i in range(GROUPS):
                        ref[at, :, 128 * i : 128 * (i + 1)] = retr[i * sub : (i + 1) * sub, :]
                at += 1
            for unit, row in chosen:
                ref[at] = up[row : row + sub, unit * D : (unit + 1) * D]
                at += 1
            for unit, row in chosen:
                ref[at] = down[unit * rows + row : unit * rows + row + sub, :]
                at += 1

    for core in range(2):

        @pl.when(meta[1] == core)
        def _(core=core):
            put(mine, core)
            put(send, 1 - core)


def pack_own(cube, meta, qkv, out, up, down, retr, vec, upb):
    sub, rows = cube.sub, cube.rows
    total = 6 * GROUPS + cube.small
    if cube.tiled:
        args = (qkv, out, up, down, retr, vec, upb)
        return pl.pallas_call(
            functools.partial(pack_kernel, cube),
            out_shape=(jax.ShapeDtypeStruct((total, sub, D), BF),) * 2,
            grid_spec=pltpu.PrefetchScalarGridSpec(
                num_scalar_prefetch=1,
                grid=(1,),
                in_specs=[full_spec(*a.shape) for a in args],
                out_specs=(full_spec(total, sub, D),) * 2,
            ),
            compiler_params=params(),
            name="pack_own",
        )(meta, *args)
    wide = cube.small * sub
    tiny = jnp.pad(vec, ((0, wide - 8), (0, D - rows)))
    tiny = tiny.at[0, 128 : 128 + 4 * rows].set(upb[0])
    tail = jnp.pad(retr.reshape(1, -1), ((0, wide - 1), (0, D - retr.size)))
    halves = []
    for half, small in ((0, tiny), (1, tail)):
        units = (2 * half, 2 * half + 1)
        a = jnp.concatenate([qkv[:, j * D : (j + 1) * D] if j < 3 else out for j in units])
        b = jnp.concatenate([up[:, j * D : (j + 1) * D] for j in units])
        c = jnp.concatenate([down[j * rows : (j + 1) * rows] for j in units])
        cut = FEW * sub
        halves.append(jnp.concatenate([a[:cut], b[:cut], c[:cut], a[cut:], small, b[cut:], c[cut:]]))
    low, high = [x.reshape(-1, sub, D) for x in halves]
    first = meta[1] == 0
    return jnp.where(first, low, high), jnp.where(first, high, low)


def spread_vectors(cube, slabs, width, count):
    n = slabs.shape[0] // 8
    lane = lax.broadcasted_iota(jnp.int32, (128, D), 1).astype(F32)
    row = lax.broadcasted_iota(jnp.int32, (128, D), 0).astype(F32)
    inside = lane - jnp.floor((lane + 0.5) * (1.0 / width)) * width
    pick = jnp.where(jnp.abs(inside - row) < 0.5, 1.0, 0.0).astype(BF)
    full = dot_nn(slabs, pick).reshape(n, 8, D)
    at = lax.broadcasted_iota(jnp.int32, (n, 8, D), 2) - lax.broadcasted_iota(jnp.int32, (n, 8, D), 0) * width
    return jnp.sum(jnp.where((at >= 0) & (at < width), full, 0.0), axis=0)


def head_masks():
    lane = lax.broadcasted_iota(jnp.int32, (1, 2 * DH), 1)
    first = jnp.where(lane < DH, 1.0, 0.0)
    return first.astype(BF), (1.0 - first).astype(BF)


def load_a(cube, weights, meta, refs, squares, small, sems, units=(0, 1, 2, 3)):
    if not cube.tiled:
        for u in units:
            pltpu.make_async_copy(refs[u], squares.at[u], sems.at[0]).start()
        return

    def place(ref, at, role, half, device):
        out = []
        for blocks, unit, groups in runs(role):
            out.append((ref.at[at, blocks], squares.at[2 * half + unit, device, groups], sems.at[0]))
        if role == 1 and small is not None:
            out.append((ref.at[at, MANY], small.at[half, device], sems.at[1]))
        return out

    weights.copies(refs, meta, place)


def a_buffer(cube):
    return pltpu.VMEM((4, cube.n, GROUPS, cube.sub, D) if cube.tiled else (4, D, D), BF)


def attn_fwd_kernel(cube, weights, layout, meta, x_ref, *refs):
    count = len(weights.arrays)
    if not cube.tiled:
        vec_ref, refs = refs[0], refs[1:]
    pieces, refs = refs[:count], refs[count:]
    joint_ref, p_ref, ctx_ref, r_ref = refs[:4]
    refs = refs[4:]
    small = None
    if cube.tiled:
        vec_ref, upb_ref, retr_ref = refs[:3]
        small, refs = refs[3], refs[:3] + refs[4:]
        refs = refs[3:]
    squares, sems = refs
    pair = pl.program_id(0)

    @pl.when(pair == 0)
    def _():
        load_a(cube, weights, meta, pieces, squares, small, sems)
        if cube.tiled:
            n = cube.n
            per = n // 4
            wait_load(small, sems.at[1])
            vec_ref[...] = spread_vectors(cube, small[0, :, :, 0:128].reshape(n * 8, 128), cube.rows, n)
            for c in range(4):
                slabs = small[0, c * per : (c + 1) * per, :, 128:256].reshape(per * 8, 128)
                upb_ref[0:1, c * D : (c + 1) * D] = spread_vectors(cube, slabs, 4 * cube.rows, per)[0:1, :]
            for i in range(GROUPS):
                retr_ref[:, i] = small[1, :, :, 128 * i : 128 * (i + 1)]
        wait_load(squares, sems.at[0])

    weight = lambda u: square(cube, squares[u])
    x = x_ref[0]
    seq = x.shape[0]
    q = (dot_nn(x, weight(0)) + vec_ref[0:1, :]).astype(BF)
    k = dot_nn(x, weight(1)).astype(BF)
    v = (dot_nn(x, weight(2)) + vec_ref[1:2, :]).astype(BF)
    joint_ref[0, :, 0:D] = q
    joint_ref[0, :, D : 2 * D] = k
    joint_ref[0, :, 2 * D : 3 * D] = v
    length = meta[layout.lengths + pair]
    key = lax.broadcasted_iota(jnp.int32, (1, seq), 1)
    mask = jnp.where(key < length, 0.0, -1e30)
    sides = head_masks()
    for h2 in range(H // 2):
        cols = slice(h2 * 2 * DH, (h2 + 1) * 2 * DH)
        q2, k2, v2 = q[:, cols], k[:, cols], v[:, cols]
        acc = None
        for hh in range(2):
            s = dot_nt(q2 * sides[hh], k2) * (SCALE * LOG2E) + mask
            e = jnp.exp2(s - jnp.max(s, axis=-1, keepdims=True))
            p = (e * (1.0 / jnp.sum(e, axis=-1, keepdims=True))).astype(BF)
            p_ref[0, 2 * h2 + hh] = p
            o = dot_nn(p, v2 * sides[hh])
            acc = o if acc is None else acc + o
        ctx_ref[0, :, cols] = acc.astype(BF)
    r_ref[0] = x.astype(F32) + dot_nn(ctx_ref[0], weight(3)) + vec_ref[2:3, :]


def attention_forward(cube, layout, meta, tokens, weights, vecs=None):
    pairs, seq, _ = tokens.shape
    shapes = [
        jax.ShapeDtypeStruct((pairs, seq, 3 * D), BF),
        jax.ShapeDtypeStruct((pairs, H, seq, seq), BF),
        jax.ShapeDtypeStruct((pairs, seq, D), BF),
        jax.ShapeDtypeStruct((pairs, seq, D), F32),
    ]
    out_specs = [pair_spec(seq, 3 * D), pair_spec(H, seq, seq), pair_spec(seq, D), pair_spec(seq, D)]
    args = [tokens]
    in_specs = [pair_spec(seq, D)]
    if cube.tiled:
        extra = [((8, D), F32), ((1, 4 * D), F32), ((cube.n, GROUPS, cube.sub, 128), BF)]
        shapes += [jax.ShapeDtypeStruct(s, t) for s, t in extra]
        out_specs += [full_spec(*s) for s, _ in extra]
    else:
        args.append(vecs)
        in_specs.append(full_spec(*vecs.shape))
    return pl.pallas_call(
        functools.partial(attn_fwd_kernel, cube, weights, layout),
        out_shape=shapes,
        grid_spec=pltpu.PrefetchScalarGridSpec(
            num_scalar_prefetch=1,
            grid=(pairs,),
            in_specs=in_specs + any_specs(len(weights.arrays)),
            out_specs=out_specs,
            scratch_shapes=([pltpu.VMEM((2, cube.n, cube.sub, D), BF)] if cube.tiled else [])
            + [a_buffer(cube), pltpu.SemaphoreType.DMA((2,))],
        ),
        compiler_params=params(),
        cost_estimate=cost(pairs * seq * D * (4 * D + 8 * seq), 30 * pairs * seq * D),
        name="attention_forward",
    )(meta, *args, *weights.arrays)


def norm_parts(r):
    centred = r - jnp.mean(r, axis=-1, keepdims=True)
    inverse = lax.rsqrt(jnp.mean(centred * centred, axis=-1, keepdims=True) + EPSILON)
    return centred * inverse, inverse


def norm_back(e, n, inverse, gain):
    scaled = e * gain
    return inverse * (
        scaled
        - jnp.mean(scaled, axis=-1, keepdims=True)
        - n * jnp.mean(scaled * n, axis=-1, keepdims=True)
    )


def gelu_parts(u):
    gauss = jnp.exp2(u * u * (-0.5 * LOG2E))
    t = 1.0 / (1.0 + (0.3275911 * 0.7071067811865476) * jnp.abs(u))
    poly = t * (
        0.5 * 0.254829592
        + t * (-0.5 * 0.284496736 + t * (0.5 * 1.421413741 + t * (-0.5 * 1.453152027 + t * (0.5 * 1.061405429))))
    )
    tail = poly * gauss
    phi = jnp.where(u >= 0.0, 1.0 - tail, tail)
    return u * phi, phi + u * gauss * 0.3989422804014327


def load_b(cube, b_weights, b_refs, a_weights, a_refs, meta, ups, dn, wo, sems):
    if not cube.tiled:
        pltpu.make_async_copy(b_refs[0], ups, sems.at[0]).start()
        pltpu.make_async_copy(b_refs[1], dn, sems.at[1]).start()
        pltpu.make_async_copy(a_refs[0], wo.at[1], sems.at[2]).start()
        return

    def place_b(ref, at, role, half, device):
        out = []
        for blocks, unit, groups in runs(role):
            out.append((ref.at[at, blocks], ups.at[2 * half + unit, device, groups], sems.at[0]))
        for blocks, unit, groups in runs(role, (FEW, MANY)[role]):
            out.append((ref.at[at, blocks], dn.at[device * 4 + 2 * half + unit, groups], sems.at[1]))
        return out

    def place_a(ref, at, role, half, device):
        return [
            (ref.at[at, blocks], wo.at[half, device, groups], sems.at[2])
            for blocks, unit, groups in runs(role)
            if unit == 1
        ]

    b_weights.copies(b_refs, meta, place_b)
    a_weights.copies(a_refs, meta, place_a)


def ffn_kernel(cube, b_weights, a_weights, meta, r_ref, cot_ref, rcot_ref, vec_ref, upb_ref, retr_ref, *refs):
    nb, na = len(b_weights.arrays), len(a_weights.arrays)
    b_refs, a_refs, refs = refs[:nb], refs[nb : nb + na], refs[nb + na :]
    lo_ref, first_ref, act_ref, down_ref, upl_ref, attn_ref, gone_ref, gctx_ref, sums_ref, gretr_ref = refs[:10]
    ups, dn, wo, slope_ref, sems = refs[10:]
    pair = pl.program_id(0)
    first_step = pair == 0

    @pl.when(first_step)
    def _():
        load_b(cube, b_weights, b_refs, a_weights, a_refs, meta, ups, dn, wo, sems)
        sums_ref[...] = jnp.zeros_like(sums_ref)
        gretr_ref[...] = jnp.zeros_like(gretr_ref)

    vec = lambda i: vec_ref[i : i + 1, :]
    n = cube.n
    up = lambda c: square(cube, ups[c])
    down = lambda c: dn[c * n : (c + 1) * n].reshape(D, D) if cube.tiled else dn[c]

    n1, inv1 = norm_parts(r_ref[0])
    first_norm = n1 * vec(3) + vec(4)
    first_low = first_norm.astype(BF)
    first_ref[0] = first_low

    @pl.when(first_step)
    def _():
        wait_load(ups, sems.at[0])
        wait_load(dn, sems.at[1])

    output = first_norm + vec(5)
    ahead = dot_nn(first_low, up(0))
    for c in range(4):
        cols = slice(c * D, (c + 1) * D)
        pre = ahead + upb_ref[0:1, cols]
        if c < 3:
            ahead = dot_nn(first_low, up(c + 1))
        active, slope = gelu_parts(pre)
        active = active.astype(BF)
        act_ref[0, :, cols] = active
        slope_ref[:, cols] = slope
        output = output + dot_nn(active, down(c))
    n2, inv2 = norm_parts(output)
    result = n2 * vec(6) + vec(7)
    lo_ref[0] = result.astype(BF)
    head = dot_nt(rcot_ref[0], retr_ref[...].reshape(D, -1))
    row = lax.broadcasted_iota(jnp.int32, (n2.shape[0], 1), 0)
    e = cot_ref[0].astype(F32) + jnp.where(row == 0, head, 0.0)
    top = jnp.where(row[:8] == 0, result[:8], 0.0).astype(BF)
    gretr_ref[...] += dot_tn(top, jnp.broadcast_to(rcot_ref[0], (8, rcot_ref.shape[-1])))
    total = lambda a: jnp.sum(a, axis=0, keepdims=True)
    sums_ref[4:5, 0:D] += total(e * n2)
    sums_ref[5:6, 0:D] += total(e)
    g_second = norm_back(e, n2, inv2, vec(6))
    down_low = g_second.astype(BF)
    down_ref[0] = down_low
    sums_ref[3:4, 0:D] += total(down_low.astype(F32))
    g_first = g_second
    ahead = dot_nt(down_low, down(0))
    for c in range(4):
        cols = slice(c * D, (c + 1) * D)
        up_low = (ahead * slope_ref[:, cols]).astype(BF)
        if c < 3:
            ahead = dot_nt(down_low, down(c + 1))
        upl_ref[0, :, cols] = up_low
        sums_ref[6:7, cols] += total(up_low.astype(F32))
        g_first = g_first + dot_nt(up_low, up(c))
    sums_ref[1:2, 0:D] += total(g_first * n1)
    sums_ref[2:3, 0:D] += total(g_first)
    g_one = norm_back(g_first, n1, inv1, vec(3))
    gone_ref[0] = g_one
    attn_low = g_one.astype(BF)
    attn_ref[0] = attn_low
    sums_ref[0:1, 0:D] += total(attn_low.astype(F32))

    @pl.when(first_step)
    def _():
        wait_load(wo if cube.tiled else wo.at[1], sems.at[2])

    gctx_ref[0] = dot_nt(attn_low, square(cube, wo[1])).astype(BF)


def feed_forward(cube, meta, r, cot, rcot, vecs, upb, retr, b_weights, a_weights):
    pairs, seq, _ = r.shape
    ff = 4 * D
    n, sub = cube.n, cube.sub
    wide = lambda k, t: jax.ShapeDtypeStruct((pairs, seq, k), t)
    if cube.tiled:
        square_shape = (n, GROUPS, sub, D)
        buffers = [(4,) + square_shape, (4 * n, GROUPS, sub, D), (2,) + square_shape]
    else:
        buffers = [(4, D, D), (4, D, D), (2, D, D)]
    return pl.pallas_call(
        functools.partial(ffn_kernel, cube, b_weights, a_weights),
        out_shape=(
            wide(D, BF),
            wide(D, BF),
            wide(ff, BF),
            wide(D, BF),
            wide(ff, BF),
            wide(D, BF),
            wide(D, F32),
            wide(D, BF),
            jax.ShapeDtypeStruct((8, ff), F32),
            jax.ShapeDtypeStruct((D, rcot.shape[-1]), F32),
        ),
        grid_spec=pltpu.PrefetchScalarGridSpec(
            num_scalar_prefetch=1,
            grid=(pairs,),
            in_specs=[
                pair_spec(seq, D),
                pair_spec(seq, D),
                pair_spec(1, rcot.shape[-1]),
                full_spec(*vecs.shape),
                full_spec(*upb.shape),
                full_spec(*retr.shape),
            ]
            + any_specs(len(b_weights.arrays) + len(a_weights.arrays)),
            out_specs=(
                pair_spec(seq, D),
                pair_spec(seq, D),
                pair_spec(seq, ff),
                pair_spec(seq, D),
                pair_spec(seq, ff),
                pair_spec(seq, D),
                pair_spec(seq, D),
                pair_spec(seq, D),
                full_spec(8, ff),
                full_spec(D, rcot.shape[-1]),
            ),
            scratch_shapes=[pltpu.VMEM(b, BF) for b in buffers]
            + [pltpu.VMEM((seq, ff), F32), pltpu.SemaphoreType.DMA((3,))],
        ),
        compiler_params=params(),
        cost_estimate=cost(pairs * seq * D * 17 * D, 40 * pairs * seq * D),
        name="feed_forward",
    )(meta, r, cot, rcot, vecs, upb, retr, *b_weights.arrays, *a_weights.arrays)


def attn_bwd_kernel(first, joint_ref, p_ref, gctx_ref, *refs):
    if first:
        gj_ref, sums_ref = refs
        sums = jnp.zeros(sums_ref.shape, F32)
    else:
        _, before_ref, gj_ref, sums_ref = refs
        sums = before_ref[...]

    @pl.when(pl.program_id(0) == 0)
    def _():
        sums_ref[...] = sums

    sides = head_masks()
    for h2 in range(H // 2):
        cut = lambda base: slice(base + h2 * 2 * DH, base + (h2 + 1) * 2 * DH)
        q2 = joint_ref[0, :, cut(0)]
        k2 = joint_ref[0, :, cut(D)]
        v2 = joint_ref[0, :, cut(2 * D)]
        go2 = gctx_ref[0, :, cut(0)]
        gq = gk = gv = 0.0
        for hh in range(2):
            go = go2 * sides[hh]
            p = p_ref[0, 2 * h2 + hh]
            gw = dot_nt(go, v2)
            pf = p.astype(F32)
            t = gw * pf
            gs = (t - pf * jnp.sum(t, axis=-1, keepdims=True)).astype(BF)
            gv = gv + dot_tn(p, go)
            gq = gq + dot_nn(gs, k2 * sides[hh])
            gk = gk + dot_tn(gs, q2 * sides[hh])
        gj_ref[0, :, cut(0)] = (gq * SCALE).astype(BF)
        gj_ref[0, :, cut(D)] = (gk * SCALE).astype(BF)
        gj_ref[0, :, cut(2 * D)] = gv.astype(BF)
    for row, j in ((0, 0), (1, 2)):
        part = gj_ref[0, :, j * D : (j + 1) * D].astype(F32)
        sums_ref[row : row + 1, :] += jnp.sum(part, axis=0, keepdims=True)


def attention_backward(joint, probs, gctx, at, count, before=None):
    pairs, seq, _ = joint.shape
    in_specs = [
        pair_spec(seq, 3 * D, first=at),
        pair_spec(H, seq, seq, first=at),
        pair_spec(seq, D, first=at),
    ]
    args = [joint, probs, gctx]
    aliases = {}
    if before is not None:
        in_specs += any_specs(1) + [full_spec(8, D)]
        args += list(before)
        aliases = {3: 0}
    return pl.pallas_call(
        functools.partial(attn_bwd_kernel, before is None),
        out_shape=(jax.ShapeDtypeStruct((pairs, seq, 3 * D), BF), jax.ShapeDtypeStruct((8, D), F32)),
        grid=(count,),
        in_specs=in_specs,
        out_specs=(pair_spec(seq, 3 * D, first=at), full_spec(8, D)),
        input_output_aliases=aliases,
        compiler_params=params(),
        cost_estimate=cost(count * seq * D * 16 * seq, 40 * count * seq * D),
        name="attention_backward",
    )(*args)


def token_grad_kernel(cube, weights, meta, gj_ref, gone_ref, *refs):
    count = len(weights.arrays)
    pieces, refs = refs[:count], refs[count:]
    gt_ref, squares, sems = refs

    @pl.when(pl.program_id(0) == 0)
    def _():
        load_a(cube, weights, meta, pieces, squares, None, sems)
        wait_load(squares, sems.at[0])

    acc = gone_ref[0]
    for j in range(3):
        acc = acc + dot_nt(gj_ref[0, :, j * D : (j + 1) * D], square(cube, squares[j]))
    gt_ref[0] = acc.astype(BF)


def token_grad(cube, meta, g_joint, g_one, weights):
    pairs, seq, _ = g_joint.shape
    return pl.pallas_call(
        functools.partial(token_grad_kernel, cube, weights),
        out_shape=jax.ShapeDtypeStruct((pairs, seq, D), BF),
        grid_spec=pltpu.PrefetchScalarGridSpec(
            num_scalar_prefetch=1,
            grid=(pairs,),
            in_specs=[pair_spec(seq, 3 * D), pair_spec(seq, D)] + any_specs(len(weights.arrays)),
            out_specs=pair_spec(seq, D),
            scratch_shapes=[a_buffer(cube), pltpu.SemaphoreType.DMA((2,))],
        ),
        compiler_params=params(),
        cost_estimate=cost(pairs * seq * D * 3 * D, 12 * pairs * seq * D),
        name="token_grad",
    )(meta, g_joint, g_one, *weights.arrays)


def unit_at(step, meta):
    return 2 * lax.bitwise_xor(meta[1], 1 - step // 2) + step % 2


def small_block(cube, half, device, sums_qv, sums, gretr, tmp):
    rows = cube.rows
    if half == 1:
        block = gretr[device * rows : (device + 1) * rows, :].astype(BF)
        block = block.reshape(GROUPS, cube.sub, 128)
        parts = [block[i] for i in range(GROUPS)] + [jnp.zeros((cube.sub, D - 128 * GROUPS), BF)]
        return jnp.concatenate(parts, axis=1)
    tmp[0:2, 0:rows] = sums_qv[0:2, device * rows : (device + 1) * rows]
    tmp[2:8, 0:rows] = sums[0:6, device * rows : (device + 1) * rows]
    tmp[0:1, 128 : 128 + 4 * rows] = sums[6:7, device * 4 * rows : (device + 1) * 4 * rows]
    return tmp[...].astype(BF)


def unit_grad_kernel(cube, layout, tail, aliased, meta, *refs):
    if tail:
        a_ref, b_ref, a2_ref, b2_ref, qv_ref, sums_ref, gretr_ref = refs[:7]
        refs = refs[7:]
    else:
        a_ref, b_ref = refs[:2]
        refs = refs[2 + aliased :]
    sends, keeps, acc_ref = refs[0:2], refs[2:4], refs[4]
    step = pl.program_id(0)
    me, core = meta[0], meta[1]
    unit = unit_at(step, meta)
    n = cube.n

    def make(left, right):
        acc_ref[...] = dot_tn(left[...], right[...]).astype(BF).reshape(acc_ref.shape)

    if tail:
        pl.when(unit < 3)(lambda: make(a_ref, b_ref))
        pl.when(unit == 3)(lambda: make(a2_ref, b2_ref))
    else:
        make(a_ref, b_ref)

    for side, (out, base, half) in enumerate(
        ((sends, lax.bitwise_xor(me, cube.core), 1 - core), (keeps, me, core))
    ):
        slot = lambda role, i: meta[layout.slot + (2 * half + role) * n + lax.bitwise_xor(base, i)]

        @pl.when(step == 2 * side)
        def _(out=out, slot=slot):
            for i in range(n):
                out[0][slot(0, i), 0:FEW] = acc_ref[i, 0:FEW]
                out[1][slot(1, i), 0:1] = acc_ref[i, FEW:GROUPS]

        @pl.when(step == 2 * side + 1)
        def _(out=out, slot=slot):
            for i in range(n):
                out[1][slot(1, i), 1:MANY] = acc_ref[i]

        if tail:
            tmp = refs[5]
            for h in range(2):

                @pl.when((step == 2 * side) & (half == h))
                def _(out=out, slot=slot, h=h):
                    tmp[...] = jnp.zeros_like(tmp)
                    for i in range(n):
                        out[1][slot(1, i), MANY] = small_block(cube, h, i, qv_ref, sums_ref, gretr_ref, tmp)


def by_distance(cube, meta, units):
    me, core = meta[0], meta[1]
    dist = jnp.asarray([cube.dist(p) for p in range(4)], jnp.int32)
    halves = []
    for half in range(2):
        blocks = [units[2 * half + k].reshape(cube.n, GROUPS, cube.sub, D) for k in range(2)]
        blocks = jnp.concatenate(blocks, axis=1)
        halves.append([blocks[:, :FEW], blocks[:, FEW:]])
    out = []
    for whose in (1, 0):
        base = me ^ (cube.core * whose)
        half = core ^ whose
        roles = []
        for role in range(2):
            block = jnp.where(half == 0, halves[0][role], halves[1][role])
            roles.append(jnp.take(block, base ^ dist[2 * half + role], axis=0))
        out.append(roles)
    return out


def grad_plain_kernel(a_ref, b_ref, out_ref):
    out_ref[...] = dot_tn(a_ref[...], b_ref[...]).astype(BF)


def plain_grad(a, b):
    return pl.pallas_call(
        grad_plain_kernel,
        out_shape=jax.ShapeDtypeStruct((D, D), BF),
        grid=(1,),
        in_specs=[full_spec(*a.shape), full_spec(*b.shape)],
        out_specs=full_spec(D, D),
        compiler_params=params(),
        name="plain_grad",
    )(a, b)


def grad_shapes(cube, sets, small):
    few = (cube.n, sets * FEW, cube.sub, D)
    many = (cube.n, sets * MANY + small, cube.sub, D)
    return [jax.ShapeDtypeStruct(s, BF) for s in (few, many, few, many)]


def grad_specs(cube, at, small):
    few = pl.BlockSpec((cube.n, FEW, cube.sub, D), lambda s, *_: (0, at, 0, 0))
    many = pl.BlockSpec((cube.n, MANY + small, cube.sub, D), lambda s, *_: (0, at, 0, 0))
    return [few, many, few, many]


def unit_grads(cube, layout, meta, a, b, before=None, tail=None):
    n = cube.n
    total = a.shape[0]
    if not cube.tiled:
        pairs = [(a, b[:, j * D : (j + 1) * D]) for j in range(b.shape[1] // D)]
        pairs += [tail[:2]] if tail else []
        send, keep = by_distance(cube, meta, [plain_grad(x, y).reshape(n, -1, D) for x, y in pairs])
        if before:
            return [jnp.concatenate(pair, axis=1) for pair in zip(before, send + keep)]
        if tail:
            small = small_by_distance(cube, meta, *tail[2:])
            send[1] = jnp.concatenate([send[1], small[0]], axis=1)
            keep[1] = jnp.concatenate([keep[1], small[1]], axis=1)
        return send + keep
    top = b.shape[1] // D - 1
    args = [a, b]
    in_specs = [
        full_spec(total, D),
        pl.BlockSpec((total, D), lambda s, meta: (0, jnp.minimum(unit_at(s, meta), top))),
    ]
    aliases = {}
    if tail:
        args += list(tail)
        in_specs += [full_spec(*t.shape) for t in tail]
    if before:
        aliases = {3 + i: i for i in range(4)}
        args += list(before)
        in_specs += any_specs(4)
    small = cube.small if tail else 0
    scratch = [pltpu.VMEM((n, GROUPS, cube.sub, D), BF)]
    scratch += [pltpu.VMEM((8, D), F32)] if tail else []
    return pl.pallas_call(
        functools.partial(unit_grad_kernel, cube, layout, tail is not None, len(aliases)),
        out_shape=grad_shapes(cube, 2 if before else 1, small),
        grid_spec=pltpu.PrefetchScalarGridSpec(
            num_scalar_prefetch=1,
            grid=(4,),
            in_specs=in_specs,
            out_specs=grad_specs(cube, 1 if before else 0, small),
            scratch_shapes=scratch,
        ),
        input_output_aliases=aliases,
        compiler_params=params(),
        cost_estimate=cost(total * D * 4 * D, 40 * D * D),
        name="unit_grads",
    )(meta, *args)


def down_grad_kernel(cube, layout, meta, a_ref, b_ref, send0, send1, keep0, keep1, acc_ref):
    me, core = meta[0], meta[1]
    n = cube.n
    per = n // 4
    step = pl.program_id(0)
    acc_ref[...] = dot_tn(a_ref[...], b_ref[...]).astype(BF).reshape(acc_ref.shape)

    def emit(out, half, base):
        for i in range(per):
            slot = lambda role: meta[layout.slot + (2 * half + role) * n + lax.bitwise_xor(base, step * per + i)]
            out[0][slot(0), 0:FEW] = acc_ref[4 * i + 2 * half, 0:FEW]
            out[1][slot(1), 0:1] = acc_ref[4 * i + 2 * half, FEW:GROUPS]
            out[1][slot(1), 1:MANY] = acc_ref[4 * i + 2 * half + 1]

    for half in range(2):

        @pl.when(core == half)
        def _(half=half):
            emit((keep0, keep1), half, me)
            emit((send0, send1), 1 - half, lax.bitwise_xor(me, cube.core))


def down_grads(cube, layout, meta, a, b):
    n = cube.n
    total = a.shape[0]
    if not cube.tiled:
        blocks = [plain_grad(a[:, j * D : (j + 1) * D], b) for j in range(4)]
        whole = jnp.concatenate(blocks, axis=0).reshape(n, 4, -1, D)
        send, keep = by_distance(cube, meta, [whole[:, j] for j in range(4)])
        return send + keep
    return pl.pallas_call(
        functools.partial(down_grad_kernel, cube, layout),
        out_shape=grad_shapes(cube, 2, 0),
        grid_spec=pltpu.PrefetchScalarGridSpec(
            num_scalar_prefetch=1,
            grid=(4,),
            in_specs=[pl.BlockSpec((total, D), lambda s, *_: (0, s)), full_spec(total, D)],
            out_specs=grad_specs(cube, 0, 0),
            scratch_shapes=[pltpu.VMEM((n, GROUPS, cube.sub, D), BF)],
        ),
        compiler_params=params(),
        cost_estimate=cost(total * D * 4 * D, 40 * D * D),
        name="down_grads",
    )(meta, a, b)


class Reduce:
    def __init__(self, cube, core, terms):
        self.cube, self.core = cube, core
        self.terms = terms[2:]
        self.flight = [cube.swap_core(s) for s in terms[:2]]
        self.r = cube.rounds

    @staticmethod
    def add(a, b):
        return a.astype(F32) + b.astype(F32)

    def tie(self, *values):
        out, self.flight = lax.optimization_barrier((values, self.flight))
        return out[0] if len(out) == 1 else out

    def step(self):
        self.r -= 1
        pairs = list(zip(self.terms, self.flight))
        half = self.terms[0].shape[0] // 2
        away = [self.add(a[half:], b[half:]).astype(BF) for a, b in pairs]
        self.terms = [self.add(a[:half], b[:half]).astype(BF) for a, b in pairs]
        self.flight = [self.cube.swap(away[role], role, self.r) for role in range(2)]

    def last(self):
        pairs = list(zip(self.terms, self.flight))
        self.mine = jnp.concatenate([self.add(a[0], b[0]) for a, b in pairs], axis=0)
        theirs = jnp.concatenate([self.add(a[1], b[1]).astype(BF) for a, b in pairs], axis=0)
        self.flight = [self.cube.swap_core(theirs)]

    def result(self):
        theirs = self.flight[0].astype(F32)
        first = self.core == 0
        return [jnp.where(first == (h == 0), self.mine, theirs) for h in range(2)]


def small_by_distance(cube, meta, sums_qv, sums, gretr):
    n, rows = cube.n, cube.rows
    me, core = meta[0], meta[1]
    wide = cube.small * cube.sub
    vec = jnp.concatenate([sums_qv[:2], sums[:6, :D]], axis=0)
    vec = jnp.pad(vec.reshape(8, n, rows).transpose(1, 0, 2), ((0, 0), (0, wide - 8), (0, 128 - rows)))
    upb = jnp.pad(sums[6].reshape(n, 1, 4 * rows), ((0, 0), (0, wide - 1), (0, D - 128 - 4 * rows)))
    low = jnp.concatenate([vec, upb], axis=2)
    high = jnp.pad(gretr.reshape(n, 1, -1), ((0, 0), (0, wide - 1), (0, D - rows * gretr.shape[1])))
    dist = jnp.asarray([cube.dist(1), cube.dist(3)], jnp.int32)
    out = []
    for whose in (1, 0):
        half = core ^ whose
        block = jnp.where(half == 0, low, high).astype(BF)
        block = jnp.take(block, (me ^ (cube.core * whose)) ^ dist[half], axis=0)
        out.append(block.reshape(n, cube.small, cube.sub, D))
    return out


def per_device(cube, tokens, pair_lengths, out_cotangent, retr_cotangent, *weights):
    (
        qkv_weight,
        query_bias,
        value_bias,
        out_weight,
        out_bias,
        first_gain,
        first_shift,
        up_weight,
        up_bias,
        down_weight,
        down_bias,
        second_gain,
        second_shift,
        retr_weight,
    ) = weights
    me = (lax.axis_index("dp") * lax.axis_size("fsdp") + lax.axis_index("fsdp")).astype(jnp.int32)
    n, rows = cube.n, cube.rows
    core = cube.half(me)
    pairs, seq, _ = tokens.shape
    proj = retr_weight.shape[1]
    layout = Meta(cube, pairs)
    meta = Meta.build(cube, me, core, pair_lengths)

    own_vec = jnp.stack(
        [query_bias, value_bias, out_bias, first_gain, first_shift, down_bias, second_gain, second_shift]
    )
    mine, send = pack_own(
        cube, meta, qkv_weight, out_weight, up_weight, down_weight, retr_weight, own_vec, up_bias[None]
    )
    gather = Gather(cube, mine, send)
    pieces_a = gather.side_a()
    rcot = retr_cotangent[:, None, :]
    if cube.tiled:
        a_weights = Weights(cube, layout, pieces_a)
        odd_weights = Weights(cube, layout, [p for p in pieces_a if p[1] == 1])
        joint, probs, ctx, r, vecs, upb, retr = attention_forward(cube, layout, meta, tokens, a_weights)
        r, pieces_b = gather.side_b(r)
        b_weights = Weights(cube, layout, pieces_b)
    else:
        natural, small = [], []
        for half in range(2):
            few, many = half_blocks(cube, me, core, pieces_a, half)
            natural += [u.reshape(D, D) for u in two_units(few, many[:, :MANY])]
            small.append(many[:, MANY:].reshape(n, -1, D))
        tiny = small[0].astype(F32)
        vecs = tiny[:, :8, :rows].transpose(1, 0, 2).reshape(8, D)
        upb = tiny[:, 0, 128 : 128 + 4 * rows].reshape(1, 4 * D)
        retr = small[1][:, 0, : rows * proj].reshape(D, proj)
        a_weights = Weights(cube, layout, natural=natural)
        odd_weights = Weights(cube, layout, natural=natural[3:])
        joint, probs, ctx, r = attention_forward(cube, layout, meta, tokens, a_weights, vecs)
        r, pieces_b = gather.side_b(r)
        ups, downs = [], []
        for half in range(2):
            few, many = half_blocks(cube, me, core, pieces_b, half)
            ups += [u.reshape(D, D) for u in two_units(few[:, :FEW], many[:, :MANY])]
            downs += [u.reshape(n, rows, D) for u in two_units(few[:, FEW:], many[:, MANY:])]
        downs = jnp.stack(downs, axis=1).reshape(4, D, D)
        b_weights = Weights(cube, layout, natural=[jnp.stack(ups), downs])

    (layer_output, first_low, active, down_low, up_low, attn_low, g_one, g_ctx, sums, g_retr) = feed_forward(
        cube, meta, r, out_cotangent, rcot, vecs, upb, retr, b_weights, odd_weights
    )
    flat = lambda a: a.reshape(pairs * seq, a.shape[-1])
    terms = down_grads(cube, layout, meta, flat(active), flat(down_low))
    terms = unit_grads(cube, layout, meta, flat(first_low), flat(up_low), before=terms)
    g_ctx, terms = lax.optimization_barrier((g_ctx, terms))
    ffn = Reduce(cube, core, terms)

    calls = [1, 2, 1] if pairs == 4 else [1] * pairs
    state, at = None, 0
    for count in calls:
        state = ffn.tie(attention_backward(joint, probs, g_ctx, at, count, state))
        at += count
        if ffn.r:
            ffn.step()
    g_joint, sums_qv = state
    tail_args = (flat(ctx), flat(attn_low), sums_qv, sums, g_retr)
    terms = unit_grads(cube, layout, meta, flat(tokens), flat(g_joint), tail=tail_args)
    terms = ffn.tie(terms)
    tail = Reduce(cube, core, terms)
    while ffn.r:
        ffn.step()
    g_joint = tail.tie(g_joint)
    tail.step()
    grad_tokens = token_grad(cube, meta, g_joint, g_one, a_weights)
    grad_tokens = tail.tie(grad_tokens)
    ffn.flight = tail.tie(ffn.flight)
    ffn.last()
    while tail.r:
        tail.step()
    tail.last()

    units = []
    for half in tail.result():
        units += [half[:GROUPS].reshape(rows, D), half[GROUPS : 2 * GROUPS].reshape(rows, D)]
        units.append(half[2 * GROUPS :].reshape(-1, D))
    grad_q, grad_k, own_vec, grad_v, grad_o, own_retr = units
    downs, ups = [], []
    for half in ffn.result():
        cuts = [0, FEW, 2 * FEW, 2 * FEW + MANY, 2 * (FEW + MANY)]
        down0, up0, down1, up1 = [half[i:j] for i, j in zip(cuts, cuts[1:])]
        downs.append(jnp.concatenate([down0, down1], axis=0).reshape(2 * rows, D))
        up = jnp.concatenate([up0, up1], axis=0).reshape(2, rows, D)
        ups += [up[0], up[1]]
    take = lambda i: own_vec[i, :rows]
    if cube.tiled:
        own_retr = own_retr[:8, : GROUPS * proj].reshape(8, GROUPS, proj).transpose(1, 0, 2).reshape(rows, proj)
    else:
        own_retr = own_retr[0, : rows * proj].reshape(rows, proj)
    return (
        layer_output,
        grad_tokens,
        jnp.concatenate([grad_q, grad_k, grad_v], axis=1),
        take(0),
        take(1),
        grad_o,
        take(2),
        take(3),
        take(4),
        jnp.concatenate(ups, axis=1),
        own_vec[0, 128 : 128 + 4 * rows],
        jnp.concatenate(downs, axis=0),
        take(5),
        take(6),
        take(7),
        own_retr,
    )


def solution(mesh):
    row = P(AXES)
    return jax.shard_map(
        functools.partial(per_device, Cube(mesh)),
        mesh=mesh,
        in_specs=(row,) * 18,
        out_specs=(row,) * 16,
        check_vma=False,
    )
```

```python
import functools

import jax
import jax.numpy as jnp
from jax import lax
from jax.experimental import pallas as pl
from jax.experimental.pallas import tpu as pltpu
from jax.sharding import PartitionSpec as P

H = 12
DH = 64
D = H * DH
EPSILON = 1e-12
SCALE = 0.125
LOG2E = 1.4426950408889634
AXES = ("dp", "fsdp")
GROUPS = 3
FEW, MANY = 4, 8
BLOCKS = FEW + MANY
VMEM_LIMIT = 60 * 1024 * 1024
BF = jnp.bfloat16
F32 = jnp.float32


def xor_masks(size, unit):
    return [(2 * (1 << b) - 1) * unit for b in range(size.bit_length() - 1)]


class Cube:
    def __init__(self, mesh):
        dp, fsdp = mesh.shape["dp"], mesh.shape["fsdp"]
        side = 1 << ((fsdp.bit_length() - 1) // 2)
        self.n = dp * fsdp
        self.core = fsdp
        self.core_bit = fsdp.bit_length() - 1
        self.flat = xor_masks(side, 1) + xor_masks(fsdp // side, side)
        self.deep = xor_masks(dp // 2, 2 * fsdp)
        self.rounds = len(self.flat) + len(self.deep)
        self.rows = D // self.n
        self.sub = self.rows // GROUPS
        self.slots = self.n // 2
        self.small = -(-8 // self.sub)
        self.tiled = self.sub % 8 == 0 and self.n // 4 % (2 * self.core) == 0

    def order(self, part):
        turn = -1 if part >= 2 else 1
        flat, deep = self.flat[::turn], self.deep[::turn]
        return deep + flat if part % 2 else flat + deep

    def dist(self, part):
        out = [0]
        for mask in self.order(part):
            out = out + [s ^ mask for s in out]
        return out

    def slot(self, part):
        table = [0] * self.n
        for at, d in enumerate(self.dist(part)):
            table[d] = at
        return table

    def swap_core(self, x):
        return lax.ppermute(x, AXES, [(i, i ^ self.core) for i in range(self.n)])

    def swap(self, x, role, r):
        core = lambda i: (i >> self.core_bit) & 1
        return lax.ppermute(x, AXES, [(i, i ^ self.order(2 * core(i) + role)[r]) for i in range(self.n)])


class Gather:
    def __init__(self, cube, own):
        self.cube = cube
        known = list(own)
        first = [FEW, MANY + 2 * cube.small]
        for r in range(cube.rounds - 1):
            got = [cube.swap(known[role], role, r) for role in range(2)]
            known, got = lax.optimization_barrier((known, got))
            if r < cube.rounds - 2:
                known = [jnp.concatenate([a, b], axis=0) for a, b in zip(known, got)]
        self.near_a = [jnp.concatenate([a[:, :f], b[:, :f]], axis=0) for a, b, f in zip(known, got, first)]
        self.rest = [(a[:, f:], b[:, f:]) for a, b, f in zip(known, got, first)]

    def link(self, near):
        return [self.cube.swap(near[role], role, self.cube.rounds - 1) for role in range(2)]

    def pieces(self, near, far, near_other, far_other):
        half = self.cube.slots // 2
        out = []
        for role in range(2):
            out += [(near[role], role, 0, 0), (far[role], role, 0, half)]
            out += [(near_other[role], role, 1, 0), (far_other[role], role, 1, half)]
        return out

    def side_a(self):
        core = self.cube.swap_core
        near_a = self.near_a
        far = self.link(near_a)
        near_b = [jnp.concatenate(pair, axis=0) for pair in self.rest]
        near_a, far, near_b = lax.optimization_barrier((near_a, far, near_b))
        self.near_b = near_b
        out = self.pieces(near_a, far, [core(x) for x in near_a], [core(x) for x in far])
        self.far_b = self.link(near_b)
        self.near_b_other = [core(x) for x in near_b]
        return out

    def side_b(self, after):
        after, self.far_b = lax.optimization_barrier((after, self.far_b))
        other = [self.cube.swap_core(x) for x in self.far_b]
        return after, self.pieces(self.near_b, self.far_b, self.near_b_other, other)


def natural_blocks(cube, me, core, pieces):
    out = []
    at = jnp.arange(cube.n, dtype=jnp.int32)
    for role in range(2):
        arrays = [
            jnp.concatenate([p for p, r, w, _ in pieces if r == role and w == whose], axis=0) for whose in range(2)
        ]
        table = jnp.asarray([cube.slot(role), cube.slot(2 + role)], jnp.int32)
        source = at ^ me
        whose = (source >> cube.core_bit) & 1
        slot = table[core ^ whose, source ^ (whose * cube.core)]
        out.append(jnp.take(jnp.concatenate(arrays, axis=0), slot + whose * cube.slots, axis=0))
    return out


def four_units(cube, blocks):
    return [blocks[:, u * GROUPS : (u + 1) * GROUPS].reshape(cube.n, cube.rows, D) for u in range(4)]


class Meta:
    def __init__(self, cube, pairs):
        self.lengths = 2
        self.dist = 2 + pairs
        self.slot = self.dist + 4 * cube.slots

    @staticmethod
    def build(cube, me, core, pair_lengths):
        tables = [cube.dist(p) for p in range(4)] + [cube.slot(p) for p in range(4)]
        tables = jnp.asarray(sum(tables, []), jnp.int32)
        return jnp.concatenate([me[None], core[None], pair_lengths, tables])


def dot_nn(a, b):
    return jnp.dot(a, b, preferred_element_type=F32)


def dot_nt(a, b):
    return lax.dot_general(a, b, (((1,), (1,)), ((), ())), preferred_element_type=F32)


def dot_tn(a, b):
    return lax.dot_general(a, b, (((0,), (0,)), ((), ())), preferred_element_type=F32)


def params():
    return pltpu.CompilerParams(dimension_semantics=("arbitrary",), vmem_limit_bytes=VMEM_LIMIT)


def cost(macs, moved):
    return pl.CostEstimate(flops=2 * macs, bytes_accessed=moved, transcendentals=0)


def pair_spec(*shape, first=0):
    return pl.BlockSpec((1,) + shape, lambda p, *_: (p + first,) + (0,) * len(shape))


def full_spec(*shape):
    return pl.BlockSpec(shape, lambda p, *_: (0,) * len(shape))


def any_specs(n):
    return [pl.BlockSpec(memory_space=pl.ANY)] * n


class Weights:
    def __init__(self, cube, layout, pieces=(), natural=()):
        self.cube, self.layout = cube, layout
        self.arrays = list(natural) if natural else [p[0] for p in pieces]
        self.what = [p[1:] for p in pieces]

    def copies(self, refs, meta, place):
        cube = self.cube
        me, core = meta[0], meta[1]
        for ref, (role, whose, first) in zip(refs, self.what):
            base = lax.bitwise_xor(me, whose * cube.core)
            table = self.layout.dist + (2 * lax.bitwise_xor(core, whose) + role) * cube.slots + first
            for at in range(ref.shape[0]):
                device = lax.bitwise_xor(base, meta[table + at])
                for source, target, sem in place(ref, at, role, device):
                    pltpu.make_async_copy(source, target, sem).start()


def wait_load(buf, sem):
    pltpu.make_async_copy(buf, buf, sem).wait()


def square(cube, blocks, unit):
    return blocks[:, unit * GROUPS : (unit + 1) * GROUPS].reshape(D, D) if cube.tiled else blocks[unit]


def pack_kernel(cube, qkv, out, up, down, retr, vec, upb, few, many):
    sub, rows = cube.sub, cube.rows
    blocks = [(i // GROUPS, i % GROUPS * sub) for i in range(BLOCKS)]
    for role, chosen in enumerate((blocks[:FEW], blocks[FEW:])):
        at, own = 0, (few, many)[role].at[0]
        for unit, row in chosen:
            part = slice(unit * D, (unit + 1) * D)
            own[at] = qkv[row : row + sub, part] if unit < 3 else out[row : row + sub, :]
            at += 1
        if role:
            own[at] = jnp.zeros((sub, D), BF)
            own[at, 0:8, 0:rows] = vec[...]
            own[at, 0:1, 128 : 128 + 4 * rows] = upb[...]
            own[at + 1] = jnp.zeros((sub, D), BF)
            for i in range(GROUPS):
                own[at + 1, :, 128 * i : 128 * (i + 1)] = retr[i * sub : (i + 1) * sub, :]
            at += 2
        for unit, row in chosen:
            own[at] = up[row : row + sub, unit * D : (unit + 1) * D]
            at += 1
        for unit, row in chosen:
            own[at] = down[unit * rows + row : unit * rows + row + sub, :]
            at += 1


def pack_own(cube, qkv, out, up, down, retr, vec, upb):
    sub, rows = cube.sub, cube.rows
    if cube.tiled:
        args = (qkv, out, up, down, retr, vec, upb)
        shapes = [(1, 3 * FEW, sub, D), (1, 3 * MANY + 2, sub, D)]
        return pl.pallas_call(
            functools.partial(pack_kernel, cube),
            out_shape=[jax.ShapeDtypeStruct(x, BF) for x in shapes],
            grid=(1,),
            in_specs=[full_spec(*a.shape) for a in args],
            out_specs=[full_spec(*x) for x in shapes],
            compiler_params=params(),
            name="pack_own",
        )(*args)
    wide = cube.small * sub
    tiny = jnp.pad(vec, ((0, wide - 8), (0, D - rows)))
    tiny = tiny.at[0, 128 : 128 + 4 * rows].set(upb[0])
    tail = jnp.pad(retr.reshape(1, -1), ((0, wide - 1), (0, D - retr.size)))
    a = jnp.concatenate([qkv[:, j * D : (j + 1) * D] for j in range(3)] + [out])
    b = jnp.concatenate([up[:, j * D : (j + 1) * D] for j in range(4)])
    cut = FEW * sub
    roles = [a[:cut], b[:cut], down[:cut]], [a[cut:], tiny, tail, b[cut:], down[cut:]]
    return [jnp.concatenate(x).reshape(1, -1, sub, D) for x in roles]


def spread_vectors(cube, slabs, width, count):
    n = slabs.shape[0] // 8
    lane = lax.broadcasted_iota(jnp.int32, (128, D), 1).astype(F32)
    row = lax.broadcasted_iota(jnp.int32, (128, D), 0).astype(F32)
    inside = lane - jnp.floor((lane + 0.5) * (1.0 / width)) * width
    pick = jnp.where(jnp.abs(inside - row) < 0.5, 1.0, 0.0).astype(BF)
    full = dot_nn(slabs, pick).reshape(n, 8, D)
    at = lax.broadcasted_iota(jnp.int32, (n, 8, D), 2) - lax.broadcasted_iota(jnp.int32, (n, 8, D), 0) * width
    return jnp.sum(jnp.where((at >= 0) & (at < width), full, 0.0), axis=0)


def head_masks():
    lane = lax.broadcasted_iota(jnp.int32, (1, 2 * DH), 1)
    first = jnp.where(lane < DH, 1.0, 0.0)
    return first.astype(BF), (1.0 - first).astype(BF)


def load_a(cube, weights, meta, refs, blocks, sem, count=4):
    if not cube.tiled:
        for u in range(count):
            pltpu.make_async_copy(refs[u], blocks.at[u], sem).start()
        return

    def place(ref, at, role, device):
        if role == 0:
            return [(ref.at[at], blocks.at[device, 0:FEW], sem)]
        many = ref.shape[1] if count == 4 else count * GROUPS - FEW
        return [(ref.at[at, 0:many], blocks.at[device, FEW : FEW + many], sem)]

    weights.copies(refs, meta, place)


def a_buffer(cube, count=4):
    many = BLOCKS + 2 if count == 4 else count * GROUPS
    return pltpu.VMEM((cube.n, many, cube.sub, D) if cube.tiled else (count, D, D), BF)


def attn_fwd_kernel(cube, weights, layout, meta, x_ref, *refs):
    count = len(weights.arrays)
    if not cube.tiled:
        vec_ref, refs = refs[0], refs[1:]
    pieces, refs = refs[:count], refs[count:]
    joint_ref, p_ref, ctx_ref, r_ref = refs[:4]
    refs = refs[4:]
    if cube.tiled:
        vec_ref, upb_ref, retr_ref = refs[:3]
        refs = refs[3:]
    blocks, sem = refs
    pair = pl.program_id(0)

    @pl.when(pair == 0)
    def _():
        load_a(cube, weights, meta, pieces, blocks, sem)
        wait_load(blocks, sem)
        if cube.tiled:
            n = cube.n
            per = n // 4
            vec_ref[...] = spread_vectors(cube, blocks[:, BLOCKS, :, 0:128].reshape(n * 8, 128), cube.rows, n)
            for c in range(4):
                slabs = blocks[c * per : (c + 1) * per, BLOCKS, :, 128:256].reshape(per * 8, 128)
                upb_ref[0:1, c * D : (c + 1) * D] = spread_vectors(cube, slabs, 4 * cube.rows, per)[0:1, :]
            for i in range(GROUPS):
                retr_ref[:, i] = blocks[:, BLOCKS + 1, :, 128 * i : 128 * (i + 1)]

    weight = lambda u: square(cube, blocks, u)
    x = x_ref[0]
    seq = x.shape[0]
    q = (dot_nn(x, weight(0)) + vec_ref[0:1, :]).astype(BF)
    k = dot_nn(x, weight(1)).astype(BF)
    v = (dot_nn(x, weight(2)) + vec_ref[1:2, :]).astype(BF)
    joint_ref[0, :, 0:D] = q
    joint_ref[0, :, D : 2 * D] = k
    joint_ref[0, :, 2 * D : 3 * D] = v
    length = meta[layout.lengths + pair]
    key = lax.broadcasted_iota(jnp.int32, (1, seq), 1)
    mask = jnp.where(key < length, 0.0, -1e30)
    sides = head_masks()
    for h2 in range(H // 2):
        cols = slice(h2 * 2 * DH, (h2 + 1) * 2 * DH)
        q2, k2, v2 = q[:, cols], k[:, cols], v[:, cols]
        acc = None
        for hh in range(2):
            s = dot_nt(q2 * sides[hh], k2) * (SCALE * LOG2E) + mask
            e = jnp.exp2(s - jnp.max(s, axis=-1, keepdims=True))
            p = (e * (1.0 / jnp.sum(e, axis=-1, keepdims=True))).astype(BF)
            p_ref[0, 2 * h2 + hh] = p
            o = dot_nn(p, v2 * sides[hh])
            acc = o if acc is None else acc + o
        ctx_ref[0, :, cols] = acc.astype(BF)
    r_ref[0] = x.astype(F32) + dot_nn(ctx_ref[0], weight(3)) + vec_ref[2:3, :]


def attention_forward(cube, layout, meta, tokens, weights, vecs=None):
    pairs, seq, _ = tokens.shape
    shapes = [
        jax.ShapeDtypeStruct((pairs, seq, 3 * D), BF),
        jax.ShapeDtypeStruct((pairs, H, seq, seq), BF),
        jax.ShapeDtypeStruct((pairs, seq, D), BF),
        jax.ShapeDtypeStruct((pairs, seq, D), F32),
    ]
    out_specs = [pair_spec(seq, 3 * D), pair_spec(H, seq, seq), pair_spec(seq, D), pair_spec(seq, D)]
    args = [tokens]
    in_specs = [pair_spec(seq, D)]
    if cube.tiled:
        extra = [((8, D), F32), ((1, 4 * D), F32), ((cube.n, GROUPS, cube.sub, 128), BF)]
        shapes += [jax.ShapeDtypeStruct(s, t) for s, t in extra]
        out_specs += [full_spec(*s) for s, _ in extra]
    else:
        args.append(vecs)
        in_specs.append(full_spec(*vecs.shape))
    return pl.pallas_call(
        functools.partial(attn_fwd_kernel, cube, weights, layout),
        out_shape=shapes,
        grid_spec=pltpu.PrefetchScalarGridSpec(
            num_scalar_prefetch=1,
            grid=(pairs,),
            in_specs=in_specs + any_specs(len(weights.arrays)),
            out_specs=out_specs,
            scratch_shapes=[a_buffer(cube), pltpu.SemaphoreType.DMA],
        ),
        compiler_params=params(),
        cost_estimate=cost(pairs * seq * D * (4 * D + 8 * seq), 30 * pairs * seq * D),
        name="attention_forward",
    )(meta, *args, *weights.arrays)


def norm_parts(r):
    centred = r - jnp.mean(r, axis=-1, keepdims=True)
    inverse = lax.rsqrt(jnp.mean(centred * centred, axis=-1, keepdims=True) + EPSILON)
    return centred * inverse, inverse


def norm_back(e, n, inverse, gain):
    scaled = e * gain
    return inverse * (
        scaled
        - jnp.mean(scaled, axis=-1, keepdims=True)
        - n * jnp.mean(scaled * n, axis=-1, keepdims=True)
    )


def gelu_parts(u):
    gauss = jnp.exp2(u * u * (-0.5 * LOG2E))
    t = 1.0 / (1.0 + (0.3275911 * 0.7071067811865476) * jnp.abs(u))
    poly = t * (
        0.5 * 0.254829592
        + t * (-0.5 * 0.284496736 + t * (0.5 * 1.421413741 + t * (-0.5 * 1.453152027 + t * (0.5 * 1.061405429))))
    )
    tail = poly * gauss
    phi = jnp.where(u >= 0.0, 1.0 - tail, tail)
    return u * phi, phi + u * gauss * 0.3989422804014327


def load_b(cube, b_weights, b_refs, a_weights, a_refs, meta, ups, dn, wo, sems):
    if not cube.tiled:
        pltpu.make_async_copy(b_refs[0], ups, sems.at[0]).start()
        pltpu.make_async_copy(b_refs[1], dn, sems.at[1]).start()
        pltpu.make_async_copy(a_refs[0], wo, sems.at[2]).start()
        return

    def place_b(kind, ref, at, role, device):
        count, first = ((FEW, 0), (MANY, FEW))[role]
        source = ref.at[at, kind * count : (kind + 1) * count]
        return [(source, (ups, dn)[kind].at[device, first : first + count], sems.at[kind])]

    def place_a(ref, at, role, device):
        last = 3 * GROUPS - FEW
        return [(ref.at[at, last : last + GROUPS], wo.at[device], sems.at[2])]

    b_weights.copies(b_refs, meta, functools.partial(place_b, 0))
    b_weights.copies(b_refs, meta, functools.partial(place_b, 1))
    a_weights.copies(a_refs, meta, place_a)


def ffn_kernel(
    cube, layout, pairs, b_weights, a_weights, meta, r_ref, cot_ref, rcot_ref, vec_ref, upb_ref, retr_ref, *refs
):
    nb, na = len(b_weights.arrays), len(a_weights.arrays)
    b_refs, a_refs, refs = refs[:nb], refs[nb : nb + na], refs[nb + na :]
    lo_ref, attn_ref, gone_ref, gctx_ref, sums_ref, gretr_ref = refs[:6]
    outs, refs = refs[6:10], refs[10:]
    ups, dn, wo, slope_ref, sems = refs[:5]
    step = pl.program_id(0)
    seq = r_ref.shape[1]
    if cube.tiled:
        first_ref, act_ref, down_ref, upl_ref = refs[5:9]
        here = pl.ds(pl.multiple_of(step * seq, seq), seq)
    else:
        first_ref, act_ref, down_ref, upl_ref = [o.at[0] for o in outs]
        here = slice(0, seq)
    first_step = step == 0

    @pl.when(first_step)
    def _():
        load_b(cube, b_weights, b_refs, a_weights, a_refs, meta, ups, dn, wo, sems)
        sums_ref[...] = jnp.zeros_like(sums_ref)
        gretr_ref[...] = jnp.zeros_like(gretr_ref)

    vec = lambda i: vec_ref[i : i + 1, :]
    n = cube.n

    def up(c):
        return square(cube, ups, c)

    def down(c):
        return dn[c * n // 4 : (c + 1) * n // 4].reshape(D, D) if cube.tiled else dn[c]

    def pair():
        n1, inv1 = norm_parts(r_ref[0])
        first_norm = n1 * vec(3) + vec(4)
        first_low = first_norm.astype(BF)
        first_ref[here, :] = first_low
        pl.when(first_step)(lambda: wait_load(ups, sems.at[0]))
        output = first_norm + vec(5)
        ahead = dot_nn(first_low, up(0))
        for c in range(4):
            cols = slice(c * D, (c + 1) * D)
            pre = ahead + upb_ref[0:1, cols]
            if c < 3:
                ahead = dot_nn(first_low, up(c + 1))
            active, slope = gelu_parts(pre)
            active = active.astype(BF)
            act_ref[here, cols] = active
            slope_ref[:, cols] = slope
            if c == 0:
                pl.when(first_step)(lambda: wait_load(dn, sems.at[1]))
            output = output + dot_nn(active, down(c))
        n2, inv2 = norm_parts(output)
        result = n2 * vec(6) + vec(7)
        lo_ref[0] = result.astype(BF)
        head = dot_nt(rcot_ref[0], retr_ref[...].reshape(D, -1))
        row = lax.broadcasted_iota(jnp.int32, (seq, 1), 0)
        e = cot_ref[0].astype(F32) + jnp.where(row == 0, head, 0.0)
        top = jnp.where(row[:8] == 0, result[:8], 0.0).astype(BF)
        gretr_ref[...] += dot_tn(top, jnp.broadcast_to(rcot_ref[0], (8, rcot_ref.shape[-1])))
        total = lambda a: jnp.sum(a, axis=0, keepdims=True)
        sums_ref[4:5, 0:D] += total(e * n2)
        sums_ref[5:6, 0:D] += total(e)
        g_second = norm_back(e, n2, inv2, vec(6))
        down_low = g_second.astype(BF)
        down_ref[here, :] = down_low
        sums_ref[3:4, 0:D] += total(down_low.astype(F32))
        g_first = g_second
        ahead = dot_nt(down_low, down(0))
        for c in range(4):
            cols = slice(c * D, (c + 1) * D)
            up_low = (ahead * slope_ref[:, cols]).astype(BF)
            if c < 3:
                ahead = dot_nt(down_low, down(c + 1))
            upl_ref[here, cols] = up_low
            sums_ref[6:7, cols] += total(up_low.astype(F32))
            g_first = g_first + dot_nt(up_low, up(c))
        sums_ref[1:2, 0:D] += total(g_first * n1)
        sums_ref[2:3, 0:D] += total(g_first)
        g_one = norm_back(g_first, n1, inv1, vec(3))
        gone_ref[0] = g_one
        attn_low = g_one.astype(BF)
        attn_ref[0] = attn_low
        sums_ref[0:1, 0:D] += total(attn_low.astype(F32))
        pl.when(first_step)(lambda: wait_load(wo, sems.at[2]))
        gctx_ref[0] = dot_nt(attn_low, wo[...].reshape(D, D)).astype(BF)

    if not cube.tiled:
        pair()
        return
    pl.when(step < pairs)(pair)

    stage, acc_ref, tmp, out_sems = refs[9:13], *refs[13:16]
    me, core = meta[0], meta[1]
    per = n // 4

    def cols(block):
        return pl.ds(pl.multiple_of(block * D, D), D)

    @pl.when((step >= pairs) & (step < pairs + 4))
    def _():
        block = step - pairs
        acc_ref[...] = dot_tn(act_ref[:, cols(block)], down_ref[...]).astype(BF).reshape(acc_ref.shape)
        for half in range(2):

            @pl.when(core == half)
            def _(half=half):
                for i in range(per):
                    owner = (i >> cube.core_bit) & 1
                    out = stage[2:4] if owner == half else stage[0:2]
                    distance = lax.bitwise_xor(me, block * per + i ^ (0 if owner == half else cube.core))
                    slots = [meta[layout.slot + (2 * owner + role) * n + distance] for role in range(2)]
                    for k in range(4):
                        put_unit(out, slots, k, acc_ref.at[4 * i + k], 0)

    @pl.when(step >= pairs + 4)
    def _():
        unit = step - pairs - 4
        acc_ref[...] = dot_tn(first_ref[...], upl_ref[:, cols(unit)]).astype(BF).reshape(acc_ref.shape)
        emit_unit(cube, layout, meta, unit, acc_ref, stage, 1)
        for half in range(2):

            @pl.when((unit == 0) & (core == half))
            def _(half=half):
                rows = cube.rows
                tmp[...] = jnp.zeros_like(tmp)
                for i in range(n):
                    near, slot = small_slot(cube, layout, meta, half, i)
                    out = stage[3 if near else 1]
                    tmp[2:8, 0:rows] = sums_ref[0:6, i * rows : (i + 1) * rows]
                    tmp[0:1, 128 : 128 + 4 * rows] = sums_ref[6:7, i * 4 * rows : (i + 1) * 4 * rows]
                    out[slot, 2 * MANY] = tmp[...].astype(BF)
                    block = gretr_ref[i * rows : (i + 1) * rows, :].astype(BF).reshape(GROUPS, cube.sub, 128)
                    parts = [block[k] for k in range(GROUPS)] + [jnp.zeros((cube.sub, D - 128 * GROUPS), BF)]
                    out[slot, 2 * MANY + 1] = jnp.concatenate(parts, axis=1)

        @pl.when(unit == 3)
        def _():
            copies = [pltpu.make_async_copy(stage[k], outs[k], out_sems.at[k]) for k in range(4)]
            for copy in copies:
                copy.start()
            for copy in copies:
                copy.wait()


def put_unit(out, slots, unit, block, at):
    first = unit * GROUPS
    few = min(max(FEW - first, 0), GROUPS)
    if few:
        out[0][slots[0], at * FEW + first : at * FEW + first + few] = block[0:few]
    if few < GROUPS:
        start = at * MANY + first + few - FEW
        out[1][slots[1], start : start + GROUPS - few] = block[few:GROUPS]


def emit_unit(cube, layout, meta, unit, acc_ref, outs, at):
    me, core = meta[0], meta[1]
    for k in range(4):

        @pl.when(unit == k)
        def _(k=k):
            for side, base, whose in ((outs[0:2], lax.bitwise_xor(me, cube.core), 1 - core), (outs[2:4], me, core)):
                for role in range(2):
                    if (role == 0 and k * GROUPS >= FEW) or (role == 1 and (k + 1) * GROUPS <= FEW):
                        continue
                    first = k * GROUPS
                    few = min(max(FEW - first, 0), GROUPS)
                    for s in range(cube.slots):
                        owner = lax.bitwise_xor(base, meta[layout.dist + (2 * whose + role) * cube.slots + s])
                        if role == 0:
                            side[0][s, at * FEW + first : at * FEW + first + few] = acc_ref[owner, 0:few]
                        else:
                            start = at * MANY + first + few - FEW
                            side[1][s, start : start + GROUPS - few] = acc_ref[owner, few:GROUPS]


def feed_forward(cube, layout, meta, r, cot, rcot, vecs, upb, retr, b_weights, a_weights):
    pairs, seq, _ = r.shape
    ff = 4 * D
    n, sub = cube.n, cube.sub
    wide = lambda k, t: jax.ShapeDtypeStruct((pairs, seq, k), t)
    at = lambda *shape: pl.BlockSpec((1,) + shape, lambda p, *_: (jnp.minimum(p, pairs - 1),) + (0,) * len(shape))
    if cube.tiled:
        square_shape = (n, GROUPS, sub, D)
        buffers = [(n, BLOCKS, sub, D), (n, BLOCKS, sub, D), square_shape]
        terms = grad_shapes(cube, 2, 2)
        term_specs = any_specs(4)
        total = pairs * seq
        more = [pltpu.VMEM((total, k), BF) for k in (D, ff, D, ff)]
        more += [pltpu.VMEM(t.shape, BF) for t in terms]
        more += [pltpu.VMEM(square_shape, BF), pltpu.VMEM((8, D), F32), pltpu.SemaphoreType.DMA((4,))]
    else:
        buffers = [(4, D, D), (4, D, D), (D, D)]
        terms = [wide(k, BF) for k in (D, ff, D, ff)]
        term_specs = [at(seq, k) for k in (D, ff, D, ff)]
        more = []
    return pl.pallas_call(
        functools.partial(ffn_kernel, cube, layout, pairs, b_weights, a_weights),
        out_shape=[
            wide(D, BF),
            wide(D, BF),
            wide(D, F32),
            wide(D, BF),
            jax.ShapeDtypeStruct((8, ff), F32),
            jax.ShapeDtypeStruct((D, rcot.shape[-1]), F32),
        ]
        + terms,
        grid_spec=pltpu.PrefetchScalarGridSpec(
            num_scalar_prefetch=1,
            grid=(pairs + 8 if cube.tiled else pairs,),
            in_specs=[
                at(seq, D),
                at(seq, D),
                at(1, rcot.shape[-1]),
                full_spec(*vecs.shape),
                full_spec(*upb.shape),
                full_spec(*retr.shape),
            ]
            + any_specs(len(b_weights.arrays) + len(a_weights.arrays)),
            out_specs=[
                at(seq, D),
                at(seq, D),
                at(seq, D),
                at(seq, D),
                full_spec(8, ff),
                full_spec(D, rcot.shape[-1]),
            ]
            + term_specs,
            scratch_shapes=[pltpu.VMEM(b, BF) for b in buffers]
            + [pltpu.VMEM((seq, ff), F32), pltpu.SemaphoreType.DMA((3,))]
            + more,
        ),
        compiler_params=params(),
        cost_estimate=cost(pairs * seq * D * 25 * D, 40 * pairs * seq * D),
        name="feed_forward",
    )(meta, r, cot, rcot, vecs, upb, retr, *b_weights.arrays, *a_weights.arrays)


def attn_bwd_kernel(first, joint_ref, p_ref, gctx_ref, *refs):
    if first:
        gj_ref, sums_ref = refs
        sums = jnp.zeros(sums_ref.shape, F32)
    else:
        _, before_ref, gj_ref, sums_ref = refs
        sums = before_ref[...]

    @pl.when(pl.program_id(0) == 0)
    def _():
        sums_ref[...] = sums

    sides = head_masks()
    for h2 in range(H // 2):
        cut = lambda base: slice(base + h2 * 2 * DH, base + (h2 + 1) * 2 * DH)
        q2 = joint_ref[0, :, cut(0)]
        k2 = joint_ref[0, :, cut(D)]
        v2 = joint_ref[0, :, cut(2 * D)]
        go2 = gctx_ref[0, :, cut(0)]
        gq = gk = gv = 0.0
        for hh in range(2):
            go = go2 * sides[hh]
            p = p_ref[0, 2 * h2 + hh]
            gw = dot_nt(go, v2)
            pf = p.astype(F32)
            t = gw * pf
            gs = (t - pf * jnp.sum(t, axis=-1, keepdims=True)).astype(BF)
            gv = gv + dot_tn(p, go)
            gq = gq + dot_nn(gs, k2 * sides[hh])
            gk = gk + dot_tn(gs, q2 * sides[hh])
        gj_ref[0, :, cut(0)] = (gq * SCALE).astype(BF)
        gj_ref[0, :, cut(D)] = (gk * SCALE).astype(BF)
        gj_ref[0, :, cut(2 * D)] = gv.astype(BF)
    for row, j in ((0, 0), (1, 2)):
        part = gj_ref[0, :, j * D : (j + 1) * D].astype(F32)
        sums_ref[row : row + 1, :] += jnp.sum(part, axis=0, keepdims=True)


def attention_backward(joint, probs, gctx, at, count, before=None):
    pairs, seq, _ = joint.shape
    in_specs = [
        pair_spec(seq, 3 * D, first=at),
        pair_spec(H, seq, seq, first=at),
        pair_spec(seq, D, first=at),
    ]
    args = [joint, probs, gctx]
    aliases = {}
    if before is not None:
        in_specs += any_specs(1) + [full_spec(8, D)]
        args += list(before)
        aliases = {3: 0}
    return pl.pallas_call(
        functools.partial(attn_bwd_kernel, before is None),
        out_shape=(jax.ShapeDtypeStruct((pairs, seq, 3 * D), BF), jax.ShapeDtypeStruct((8, D), F32)),
        grid=(count,),
        in_specs=in_specs,
        out_specs=(pair_spec(seq, 3 * D, first=at), full_spec(8, D)),
        input_output_aliases=aliases,
        compiler_params=params(),
        cost_estimate=cost(count * seq * D * 16 * seq, 40 * count * seq * D),
        name="attention_backward",
    )(*args)


def token_grad_kernel(cube, weights, meta, gj_ref, gone_ref, *refs):
    count = len(weights.arrays)
    pieces, refs = refs[:count], refs[count:]
    gt_ref, blocks, sem = refs

    @pl.when(pl.program_id(0) == 0)
    def _():
        load_a(cube, weights, meta, pieces, blocks, sem, 3)
        wait_load(blocks, sem)

    acc = gone_ref[...].reshape(-1, D)
    for j in range(3):
        acc = acc + dot_nt(gj_ref[:, :, j * D : (j + 1) * D].reshape(-1, D), square(cube, blocks, j))
    gt_ref[...] = acc.astype(BF).reshape(gt_ref.shape)


def token_grad(cube, meta, g_joint, g_one, weights):
    pairs, seq, _ = g_joint.shape
    per = 2 if pairs % 2 == 0 else 1
    block = lambda width: pl.BlockSpec((per, seq, width), lambda p, *_: (p, 0, 0))
    return pl.pallas_call(
        functools.partial(token_grad_kernel, cube, weights),
        out_shape=jax.ShapeDtypeStruct((pairs, seq, D), BF),
        grid_spec=pltpu.PrefetchScalarGridSpec(
            num_scalar_prefetch=1,
            grid=(pairs // per,),
            in_specs=[block(3 * D), block(D)] + any_specs(len(weights.arrays)),
            out_specs=block(D),
            scratch_shapes=[a_buffer(cube, 3), pltpu.SemaphoreType.DMA],
        ),
        compiler_params=params(),
        cost_estimate=cost(pairs * seq * D * 3 * D, 12 * pairs * seq * D),
        name="token_grad",
    )(meta, g_joint, g_one, *weights.arrays)


def small_slot(cube, layout, meta, half, i):
    owner = (i >> cube.core_bit) & 1
    distance = lax.bitwise_xor(meta[0], i ^ (0 if owner == half else cube.core))
    return owner == half, meta[layout.slot + (2 * owner + 1) * cube.n + distance]


def unit_grad_kernel(cube, layout, meta, a_ref, b_ref, qv_ref, a2_ref, b2_ref, *refs):
    outs, acc_ref, tmp, left2, right2, sems = refs[0:4], *refs[4:9]
    unit = pl.program_id(0)
    core = meta[1]
    late = [pltpu.make_async_copy(a2_ref, left2, sems.at[0]), pltpu.make_async_copy(b2_ref, right2, sems.at[1])]

    def make(left, right):
        acc_ref[...] = dot_tn(left[...], right[...]).astype(BF).reshape(acc_ref.shape)

    @pl.when(unit == 0)
    def _():
        for copy in late:
            copy.start()

    pl.when(unit < 3)(lambda: make(a_ref, b_ref))

    @pl.when(unit == 3)
    def _():
        for copy in late:
            copy.wait()
        make(left2, right2)

    emit_unit(cube, layout, meta, unit, acc_ref, outs, 0)
    for half in range(2):

        @pl.when((unit == 0) & (core == half))
        def _(half=half):
            tmp[...] = jnp.zeros_like(tmp)
            for i in range(cube.n):
                near, slot = small_slot(cube, layout, meta, half, i)
                tmp[0:2, 0 : cube.rows] = qv_ref[0:2, i * cube.rows : (i + 1) * cube.rows]
                outs[3 if near else 1][slot, MANY] = tmp[...].astype(BF)


def by_distance(cube, meta, units):
    me, core = meta[0], meta[1]
    dist = jnp.asarray([cube.dist(p) for p in range(4)], jnp.int32)
    blocks = jnp.concatenate([u.reshape(cube.n, GROUPS, cube.sub, D) for u in units], axis=1)
    parts = [blocks[:, :FEW], blocks[:, FEW:]]
    out = []
    for whose in (1, 0):
        base = me ^ (cube.core * whose)
        out.append([jnp.take(parts[role], base ^ dist[2 * (core ^ whose) + role], axis=0) for role in range(2)])
    return out


def grad_plain_kernel(a_ref, b_ref, out_ref):
    out_ref[...] = dot_tn(a_ref[...], b_ref[...]).astype(BF)


def plain_grad(a, b):
    return pl.pallas_call(
        grad_plain_kernel,
        out_shape=jax.ShapeDtypeStruct((D, D), BF),
        grid=(1,),
        in_specs=[full_spec(*a.shape), full_spec(*b.shape)],
        out_specs=full_spec(D, D),
        compiler_params=params(),
        name="plain_grad",
    )(a, b)


def grad_shapes(cube, sets, small):
    few = (cube.slots, sets * FEW, cube.sub, D)
    many = (cube.slots, sets * MANY + small, cube.sub, D)
    return [jax.ShapeDtypeStruct(s, BF) for s in (few, many, few, many)]


def plain_terms(cube, meta, sums, gretr, first_low, active, down_low, up_low):
    n = cube.n
    blocks = [plain_grad(active[:, j * D : (j + 1) * D], down_low) for j in range(4)]
    whole = jnp.concatenate(blocks, axis=0).reshape(n, 4, -1, D)
    down = sum(by_distance(cube, meta, [whole[:, j] for j in range(4)]), [])
    ups = [plain_grad(first_low, up_low[:, j * D : (j + 1) * D]).reshape(n, -1, D) for j in range(4)]
    up = sum(by_distance(cube, meta, ups), [])
    terms = [jnp.concatenate(pair, axis=1) for pair in zip(down, up)]
    small = small_by_distance(cube, meta, jnp.zeros((2, D), F32), sums, gretr)
    for k in range(2):
        terms[2 * k + 1] = jnp.concatenate([terms[2 * k + 1], small[k]], axis=1)
    return terms


def unit_grads(cube, layout, meta, a, b, tail):
    n = cube.n
    total = a.shape[0]
    if not cube.tiled:
        pairs = [(a, b[:, j * D : (j + 1) * D]) for j in range(b.shape[1] // D)] + [tail[:2]]
        send, keep = by_distance(cube, meta, [plain_grad(x, y).reshape(n, -1, D) for x, y in pairs])
        small = small_by_distance(cube, meta, tail[2], None, None)
        send[1] = jnp.concatenate([send[1], small[0]], axis=1)
        keep[1] = jnp.concatenate([keep[1], small[1]], axis=1)
        return send + keep
    top = b.shape[1] // D - 1
    args = [a, b]
    in_specs = [
        full_spec(total, D),
        pl.BlockSpec((total, D), lambda s, *_: (0, jnp.minimum(s, top))),
    ]
    args += [tail[2], tail[0], tail[1]]
    in_specs += [full_spec(*tail[2].shape)] + any_specs(2)
    return pl.pallas_call(
        functools.partial(unit_grad_kernel, cube, layout),
        out_shape=grad_shapes(cube, 1, 1),
        grid_spec=pltpu.PrefetchScalarGridSpec(
            num_scalar_prefetch=1,
            grid=(4,),
            in_specs=in_specs,
            out_specs=[full_spec(*t.shape) for t in grad_shapes(cube, 1, 1)],
            scratch_shapes=[pltpu.VMEM((n, GROUPS, cube.sub, D), BF), pltpu.VMEM((8, D), F32)]
            + [pltpu.VMEM((total, D), BF)] * 2
            + [pltpu.SemaphoreType.DMA((2,))],
        ),
        compiler_params=params(),
        cost_estimate=cost(total * D * 4 * D, 40 * D * D),
        name="unit_grads",
    )(meta, *args)


class Reduce:
    def __init__(self, cube, terms):
        self.cube = cube
        self.terms = terms[2:]
        self.flight = [cube.swap_core(s) for s in terms[:2]]
        self.r = cube.rounds

    @staticmethod
    def add(a, b):
        return a.astype(F32) + b.astype(F32)

    def tie(self, *values):
        out, self.flight = lax.optimization_barrier((values, self.flight))
        return out[0] if len(out) == 1 else out

    def step(self):
        self.r -= 1
        pairs = list(zip(self.terms, self.flight))
        half = self.terms[0].shape[0] // 2
        away = [self.add(a[half:], b[half:]).astype(BF) for a, b in pairs]
        self.terms = [self.add(a[:half], b[:half]).astype(BF) for a, b in pairs]
        self.flight = [self.cube.swap(away[role], role, self.r) for role in range(2)]

    def result(self):
        return [self.add(a[0], b[0]) for a, b in zip(self.terms, self.flight)]


def small_by_distance(cube, meta, sums_qv, sums, gretr):
    n, rows = cube.n, cube.rows
    me, core = meta[0], meta[1]
    wide = cube.small * cube.sub
    vec = jnp.zeros((6, D), F32) if sums is None else sums[:6, :D]
    upb = jnp.zeros((4 * D,), F32) if sums is None else sums[6]
    vec = jnp.concatenate([sums_qv[:2], vec], axis=0)
    vec = jnp.pad(vec.reshape(8, n, rows).transpose(1, 0, 2), ((0, 0), (0, wide - 8), (0, 128 - rows)))
    upb = jnp.pad(upb.reshape(n, 1, 4 * rows), ((0, 0), (0, wide - 1), (0, D - 128 - 4 * rows)))
    block = jnp.concatenate([vec, upb], axis=2)
    if gretr is not None:
        more = jnp.pad(gretr.reshape(n, 1, -1), ((0, 0), (0, wide - 1), (0, D - rows * gretr.shape[1])))
        block = jnp.concatenate([block, more], axis=1)
    dist = jnp.asarray([cube.dist(1), cube.dist(3)], jnp.int32)
    out = []
    for whose in (1, 0):
        part = jnp.take(block.astype(BF), (me ^ (cube.core * whose)) ^ dist[core ^ whose], axis=0)
        out.append(part.reshape(cube.slots, -1, cube.sub, D))
    return out


def per_device(cube, tokens, pair_lengths, out_cotangent, retr_cotangent, *weights):
    (
        qkv_weight,
        query_bias,
        value_bias,
        out_weight,
        out_bias,
        first_gain,
        first_shift,
        up_weight,
        up_bias,
        down_weight,
        down_bias,
        second_gain,
        second_shift,
        retr_weight,
    ) = weights
    me = (lax.axis_index("dp") * lax.axis_size("fsdp") + lax.axis_index("fsdp")).astype(jnp.int32)
    n, rows = cube.n, cube.rows
    core = (me >> cube.core_bit) & 1
    pairs, seq, _ = tokens.shape
    proj = retr_weight.shape[1]
    layout = Meta(cube, pairs)
    meta = Meta.build(cube, me, core, pair_lengths)

    own_vec = jnp.stack(
        [query_bias, value_bias, out_bias, first_gain, first_shift, down_bias, second_gain, second_shift]
    )
    own = pack_own(cube, qkv_weight, out_weight, up_weight, down_weight, retr_weight, own_vec, up_bias[None])
    gather = Gather(cube, own)
    pieces_a = gather.side_a()
    rcot = retr_cotangent[:, None, :]
    if cube.tiled:
        a_weights = Weights(cube, layout, pieces_a)
        odd_weights = Weights(cube, layout, [p for p in pieces_a if p[1] == 1])
        joint, probs, ctx, r, vecs, upb, retr = attention_forward(cube, layout, meta, tokens, a_weights)
        r, pieces_b = gather.side_b(r)
        b_weights = Weights(cube, layout, pieces_b)
    else:
        few, many = natural_blocks(cube, me, core, pieces_a)
        natural = four_units(cube, jnp.concatenate([few, many[:, :MANY]], axis=1))
        natural = [u.reshape(D, D) for u in natural]
        tiny, retr = [
            many[:, at : at + cube.small].reshape(n, -1, D) for at in (MANY, MANY + cube.small)
        ]
        tiny = tiny.astype(F32)
        vecs = tiny[:, :8, :rows].transpose(1, 0, 2).reshape(8, D)
        upb = tiny[:, 0, 128 : 128 + 4 * rows].reshape(1, 4 * D)
        retr = retr[:, 0, : rows * proj].reshape(D, proj)
        a_weights = Weights(cube, layout, natural=natural)
        odd_weights = Weights(cube, layout, natural=natural[3:])
        joint, probs, ctx, r = attention_forward(cube, layout, meta, tokens, a_weights, vecs)
        r, pieces_b = gather.side_b(r)
        few, many = natural_blocks(cube, me, core, pieces_b)
        ups = four_units(cube, jnp.concatenate([few[:, :FEW], many[:, :MANY]], axis=1))
        ups = jnp.stack([u.reshape(D, D) for u in ups])
        downs = jnp.concatenate([few[:, FEW:], many[:, MANY:]], axis=1).reshape(4, D, D)
        b_weights = Weights(cube, layout, natural=[ups, downs])

    layer_output, attn_low, g_one, g_ctx, sums, g_retr, *terms = feed_forward(
        cube, layout, meta, r, out_cotangent, rcot, vecs, upb, retr, b_weights, odd_weights
    )
    flat = lambda a: a.reshape(pairs * seq, a.shape[-1])
    if not cube.tiled:
        terms = plain_terms(cube, meta, sums, g_retr, *[flat(t) for t in terms])
    g_ctx, terms = lax.optimization_barrier((g_ctx, terms))
    ffn = Reduce(cube, terms)

    calls = [1, pairs - 1]
    state, at = None, 0
    for count in calls:
        state = ffn.tie(attention_backward(joint, probs, g_ctx, at, count, state))
        at += count
        if ffn.r:
            ffn.step()
    g_joint, sums_qv = state
    tail_args = (flat(ctx), flat(attn_low), sums_qv)
    terms = unit_grads(cube, layout, meta, flat(tokens), flat(g_joint), tail_args)
    terms = ffn.tie(terms)
    tail = Reduce(cube, terms)
    ffn.step()
    g_joint = tail.tie(g_joint)
    tail.step()
    grad_tokens = token_grad(cube, meta, g_joint, g_one, a_weights)
    grad_tokens = tail.tie(grad_tokens)
    ffn.flight = tail.tie(ffn.flight)
    tail.step()
    ffn.flight = tail.tie(ffn.flight)
    tail.step()
    ffn.step()
    while tail.r:
        ffn.flight = tail.tie(ffn.flight)
        tail.step()
    while ffn.r:
        ffn.step()

    few, many = tail.result()
    grad_q, grad_k, grad_v, grad_o = jnp.concatenate([few, many[:MANY]], axis=0).reshape(4, rows, D)
    own_qv = many[MANY:].reshape(-1, D)
    few, many = ffn.result()
    grad_down = jnp.concatenate([few[:FEW], many[:MANY]], axis=0).reshape(4 * rows, D)
    ups = jnp.concatenate([few[FEW:], many[MANY : 2 * MANY]], axis=0).reshape(4, rows, D)
    own_vec, own_retr = many[2 * MANY :].reshape(2, -1, D)
    take = lambda i: own_vec[i, :rows]
    if cube.tiled:
        own_retr = own_retr[:8, : GROUPS * proj].reshape(8, GROUPS, proj).transpose(1, 0, 2).reshape(rows, proj)
    else:
        own_retr = own_retr[0, : rows * proj].reshape(rows, proj)
    return (
        layer_output,
        grad_tokens,
        jnp.concatenate([grad_q, grad_k, grad_v], axis=1),
        own_qv[0, :rows],
        own_qv[1, :rows],
        grad_o,
        take(2),
        take(3),
        take(4),
        jnp.concatenate(list(ups), axis=1),
        own_vec[0, 128 : 128 + 4 * rows],
        grad_down,
        take(5),
        take(6),
        take(7),
        own_retr,
    )


def solution(mesh):
    row = P(AXES)
    return jax.shard_map(
        functools.partial(per_device, Cube(mesh)),
        mesh=mesh,
        in_specs=(row,) * 18,
        out_specs=(row,) * 16,
        check_vma=False,
    )
```

```python
import functools

import jax
import jax.numpy as jnp
from jax import lax
from jax.experimental import pallas as pl
from jax.experimental.pallas import tpu as pltpu
from jax.sharding import PartitionSpec as P

H = 12
DH = 64
D = H * DH
EPSILON = 1e-12
SCALE = 0.125
LOG2E = 1.4426950408889634
AXES = ("dp", "fsdp")
GROUPS = 3
FEW, MANY = 4, 8
BLOCKS = FEW + MANY
VMEM_LIMIT = 60 * 1024 * 1024
BF = jnp.bfloat16
F32 = jnp.float32


def xor_masks(size, unit):
    return [(2 * (1 << b) - 1) * unit for b in range(size.bit_length() - 1)]


class Cube:
    def __init__(self, mesh):
        dp, fsdp = mesh.shape["dp"], mesh.shape["fsdp"]
        side = 1 << ((fsdp.bit_length() - 1) // 2)
        self.n = dp * fsdp
        self.core = fsdp
        self.core_bit = fsdp.bit_length() - 1
        self.x, self.y = xor_masks(side, 1), xor_masks(fsdp // side, side)
        self.z = xor_masks(dp // 2, 2 * fsdp)
        self.rounds = len(self.x + self.y + self.z)
        self.rows = D // self.n
        self.sub = self.rows // GROUPS
        self.slots = self.n // 2
        self.small = -(-8 // self.sub)
        self.tiled = self.sub % 8 == 0 and self.n // 4 % (2 * self.core) == 0

    def order(self, part):
        turn = -1 if part >= 2 else 1
        flat, deep = (self.x + self.y)[::turn], self.z[::turn]
        return deep + flat if part % 2 else flat + deep

    def dist(self, part):
        out = [0]
        for mask in self.order(part):
            out = out + [s ^ mask for s in out]
        return out

    def slot(self, part):
        table = [0] * self.n
        for at, d in enumerate(self.dist(part)):
            table[d] = at
        return table

    def swap_core(self, x):
        return lax.ppermute(x, AXES, [(i, i ^ self.core) for i in range(self.n)])

    def swap(self, x, role, r):
        return self.swap_rounds(x, role, [r])

    def swap_rounds(self, x, role, rounds):
        pairs = []
        for i in range(self.n):
            order = self.order(2 * ((i >> self.core_bit) & 1) + role)
            to = i
            for r in rounds:
                to ^= order[r]
            pairs.append((i, to))
        return lax.ppermute(x, AXES, pairs)


class Gather:
    def __init__(self, cube, own):
        self.cube = cube
        known = list(own)
        first = [FEW, MANY + 2 * cube.small]
        for r in range(cube.rounds - 1):
            got = [cube.swap(known[role], role, r) for role in range(2)]
            known, got = lax.optimization_barrier((known, got))
            if r < cube.rounds - 2:
                known = [jnp.concatenate([a, b], axis=0) for a, b in zip(known, got)]
        self.near_a = [jnp.concatenate([a[:, :f], b[:, :f]], axis=0) for a, b, f in zip(known, got, first)]
        self.rest = [(a[:, f:], b[:, f:]) for a, b, f in zip(known, got, first)]

    def link(self, near):
        return [self.cube.swap(near[role], role, self.cube.rounds - 1) for role in range(2)]

    def pieces(self, near, far, near_other, far_other):
        half = self.cube.slots // 2
        out = []
        for role in range(2):
            out += [(near[role], role, 0, 0), (far[role], role, 0, half)]
            out += [(near_other[role], role, 1, 0), (far_other[role], role, 1, half)]
        return out

    def side_a(self):
        core = self.cube.swap_core
        near_a = self.near_a
        far = self.link(near_a)
        near_b = [jnp.concatenate(pair, axis=0) for pair in self.rest]
        near_a, far, near_b = lax.optimization_barrier((near_a, far, near_b))
        self.near_b = near_b
        out = self.pieces(near_a, far, [core(x) for x in near_a], [core(x) for x in far])
        self.far_b = self.link(near_b)
        self.near_b_other = [core(x) for x in near_b]
        return out

    def side_b(self, after):
        after, self.far_b = lax.optimization_barrier((after, self.far_b))
        other = [self.cube.swap_core(x) for x in self.far_b]
        return after, self.pieces(self.near_b, self.far_b, self.near_b_other, other)


def natural_blocks(cube, me, core, pieces):
    out = []
    at = jnp.arange(cube.n, dtype=jnp.int32)
    for role in range(2):
        arrays = [
            jnp.concatenate([p for p, r, w, _ in pieces if r == role and w == whose], axis=0) for whose in range(2)
        ]
        table = jnp.asarray([cube.slot(role), cube.slot(2 + role)], jnp.int32)
        source = at ^ me
        whose = (source >> cube.core_bit) & 1
        slot = table[core ^ whose, source ^ (whose * cube.core)]
        out.append(jnp.take(jnp.concatenate(arrays, axis=0), slot + whose * cube.slots, axis=0))
    return out


def four_units(cube, blocks):
    return [blocks[:, u * GROUPS : (u + 1) * GROUPS].reshape(cube.n, cube.rows, D) for u in range(4)]


class Meta:
    def __init__(self, cube, pairs):
        self.lengths = 2
        self.dist = 2 + pairs
        self.slot = self.dist + 4 * cube.slots

    @staticmethod
    def build(cube, me, core, pair_lengths):
        tables = [cube.dist(p) for p in range(4)] + [cube.slot(p) for p in range(4)]
        tables = jnp.asarray(sum(tables, []), jnp.int32)
        return jnp.concatenate([me[None], core[None], pair_lengths, tables])


def dot_nn(a, b):
    return jnp.dot(a, b, preferred_element_type=F32)


def dot_nt(a, b):
    return lax.dot_general(a, b, (((1,), (1,)), ((), ())), preferred_element_type=F32)


def dot_tn(a, b):
    return lax.dot_general(a, b, (((0,), (0,)), ((), ())), preferred_element_type=F32)


def params():
    return pltpu.CompilerParams(dimension_semantics=("arbitrary",), vmem_limit_bytes=VMEM_LIMIT)


def cost(macs, moved):
    return pl.CostEstimate(flops=2 * macs, bytes_accessed=moved, transcendentals=0)


def pair_spec(*shape, first=0):
    return pl.BlockSpec((1,) + shape, lambda p, *_: (p + first,) + (0,) * len(shape))


def full_spec(*shape):
    return pl.BlockSpec(shape, lambda p, *_: (0,) * len(shape))


def any_specs(n):
    return [pl.BlockSpec(memory_space=pl.ANY)] * n


class Weights:
    def __init__(self, cube, layout, pieces=(), natural=()):
        self.cube, self.layout = cube, layout
        self.arrays = list(natural) if natural else [p[0] for p in pieces]
        self.what = [p[1:] for p in pieces]

    def copies(self, refs, meta, place):
        cube = self.cube
        me, core = meta[0], meta[1]
        for ref, (role, whose, first) in zip(refs, self.what):
            base = lax.bitwise_xor(me, whose * cube.core)
            table = self.layout.dist + (2 * lax.bitwise_xor(core, whose) + role) * cube.slots + first
            for at in range(ref.shape[0]):
                device = lax.bitwise_xor(base, meta[table + at])
                for source, target, sem in place(ref, at, role, device):
                    pltpu.make_async_copy(source, target, sem).start()


def wait_load(buf, sem):
    pltpu.make_async_copy(buf, buf, sem).wait()


def square(cube, blocks, unit):
    return blocks[:, unit * GROUPS : (unit + 1) * GROUPS].reshape(D, D) if cube.tiled else blocks[unit]


def pack_kernel(cube, qkv, out, up, down, retr, vec, upb, few, many):
    sub, rows = cube.sub, cube.rows
    blocks = [(i // GROUPS, i % GROUPS * sub) for i in range(BLOCKS)]
    for role, chosen in enumerate((blocks[:FEW], blocks[FEW:])):
        at, own = 0, (few, many)[role].at[0]
        for unit, row in chosen:
            part = slice(unit * D, (unit + 1) * D)
            own[at] = qkv[row : row + sub, part] if unit < 3 else out[row : row + sub, :]
            at += 1
        if role:
            own[at] = jnp.zeros((sub, D), BF)
            own[at, 0:8, 0:rows] = vec[...]
            own[at, 0:1, 128 : 128 + 4 * rows] = upb[...]
            own[at + 1] = jnp.zeros((sub, D), BF)
            for i in range(GROUPS):
                own[at + 1, :, 128 * i : 128 * (i + 1)] = retr[i * sub : (i + 1) * sub, :]
            at += 2
        for unit, row in chosen:
            own[at] = up[row : row + sub, unit * D : (unit + 1) * D]
            at += 1
        for unit, row in chosen:
            own[at] = down[unit * rows + row : unit * rows + row + sub, :]
            at += 1


def pack_own(cube, qkv, out, up, down, retr, vec, upb):
    sub, rows = cube.sub, cube.rows
    if cube.tiled:
        args = (qkv, out, up, down, retr, vec, upb)
        shapes = [(1, 3 * FEW, sub, D), (1, 3 * MANY + 2, sub, D)]
        return pl.pallas_call(
            functools.partial(pack_kernel, cube),
            out_shape=[jax.ShapeDtypeStruct(x, BF) for x in shapes],
            grid=(1,),
            in_specs=[full_spec(*a.shape) for a in args],
            out_specs=[full_spec(*x) for x in shapes],
            compiler_params=params(),
            name="pack_own",
        )(*args)
    wide = cube.small * sub
    tiny = jnp.pad(vec, ((0, wide - 8), (0, D - rows)))
    tiny = tiny.at[0, 128 : 128 + 4 * rows].set(upb[0])
    tail = jnp.pad(retr.reshape(1, -1), ((0, wide - 1), (0, D - retr.size)))
    a = jnp.concatenate([qkv[:, j * D : (j + 1) * D] for j in range(3)] + [out])
    b = jnp.concatenate([up[:, j * D : (j + 1) * D] for j in range(4)])
    cut = FEW * sub
    roles = [a[:cut], b[:cut], down[:cut]], [a[cut:], tiny, tail, b[cut:], down[cut:]]
    return [jnp.concatenate(x).reshape(1, -1, sub, D) for x in roles]


def spread_vectors(cube, slabs, width, count):
    n = slabs.shape[0] // 8
    lane = lax.broadcasted_iota(jnp.int32, (128, D), 1).astype(F32)
    row = lax.broadcasted_iota(jnp.int32, (128, D), 0).astype(F32)
    inside = lane - jnp.floor((lane + 0.5) * (1.0 / width)) * width
    pick = jnp.where(jnp.abs(inside - row) < 0.5, 1.0, 0.0).astype(BF)
    full = dot_nn(slabs, pick).reshape(n, 8, D)
    at = lax.broadcasted_iota(jnp.int32, (n, 8, D), 2) - lax.broadcasted_iota(jnp.int32, (n, 8, D), 0) * width
    return jnp.sum(jnp.where((at >= 0) & (at < width), full, 0.0), axis=0)


def head_masks():
    lane = lax.broadcasted_iota(jnp.int32, (1, 2 * DH), 1)
    first = jnp.where(lane < DH, 1.0, 0.0)
    return first.astype(BF), (1.0 - first).astype(BF)


def stack_heads(two, sides):
    return jnp.concatenate([two * sides[0], two * sides[1]], axis=0)


def join_heads(stacked):
    half = stacked.shape[0] // 2
    lane = lax.broadcasted_iota(jnp.int32, (1, 2 * DH), 1)
    return jnp.where(lane < DH, stacked[:half], stacked[half:])


def load_a(cube, weights, meta, refs, blocks, sem, count=4):
    if not cube.tiled:
        for u in range(count):
            pltpu.make_async_copy(refs[u], blocks.at[u], sem).start()
        return

    def place(ref, at, role, device):
        if role == 0:
            return [(ref.at[at], blocks.at[device, 0:FEW], sem)]
        many = ref.shape[1] if count == 4 else count * GROUPS - FEW
        return [(ref.at[at, 0:many], blocks.at[device, FEW : FEW + many], sem)]

    weights.copies(refs, meta, place)


def a_buffer(cube, count=4):
    many = BLOCKS + 2 if count == 4 else count * GROUPS
    return pltpu.VMEM((cube.n, many, cube.sub, D) if cube.tiled else (count, D, D), BF)


def attn_fwd_kernel(cube, weights, layout, meta, x_ref, *refs):
    count = len(weights.arrays)
    if not cube.tiled:
        vec_ref, refs = refs[0], refs[1:]
    pieces, refs = refs[:count], refs[count:]
    joint_ref, p_ref, ctx_ref, r_ref = refs[:4]
    refs = refs[4:]
    if cube.tiled:
        vec_ref, upb_ref, retr_ref = refs[:3]
        refs = refs[3:]
    blocks, sem = refs
    pair = pl.program_id(0)

    @pl.when(pair == 0)
    def _():
        load_a(cube, weights, meta, pieces, blocks, sem)
        wait_load(blocks, sem)
        if cube.tiled:
            n = cube.n
            per = n // 4
            vec_ref[...] = spread_vectors(cube, blocks[:, BLOCKS, :, 0:128].reshape(n * 8, 128), cube.rows, n)
            for c in range(4):
                slabs = blocks[c * per : (c + 1) * per, BLOCKS, :, 128:256].reshape(per * 8, 128)
                upb_ref[0:1, c * D : (c + 1) * D] = spread_vectors(cube, slabs, 4 * cube.rows, per)[0:1, :]
            for i in range(GROUPS):
                retr_ref[:, i] = blocks[:, BLOCKS + 1, :, 128 * i : 128 * (i + 1)]

    weight = lambda u: square(cube, blocks, u)
    x = x_ref[0]
    seq = x.shape[0]
    q = (dot_nn(x, weight(0)) + vec_ref[0:1, :]).astype(BF)
    k = dot_nn(x, weight(1)).astype(BF)
    v = (dot_nn(x, weight(2)) + vec_ref[1:2, :]).astype(BF)
    joint_ref[0, :, 0:D] = q
    joint_ref[0, :, D : 2 * D] = k
    joint_ref[0, :, 2 * D : 3 * D] = v
    length = meta[layout.lengths + pair]
    key = lax.broadcasted_iota(jnp.int32, (1, seq), 1)
    mask = jnp.where(key < length, 0.0, -1e30)
    sides = head_masks()
    for h2 in range(H // 2):
        cols = slice(h2 * 2 * DH, (h2 + 1) * 2 * DH)
        s = dot_nt(stack_heads(q[:, cols], sides), k[:, cols]) * (SCALE * LOG2E) + mask
        e = jnp.exp2(s - jnp.max(s, axis=-1, keepdims=True))
        p = (e * (1.0 / jnp.sum(e, axis=-1, keepdims=True))).astype(BF)
        p_ref[0, h2] = p
        ctx_ref[0, :, cols] = join_heads(dot_nn(p, v[:, cols])).astype(BF)
    r_ref[0] = x.astype(F32) + dot_nn(ctx_ref[0], weight(3)) + vec_ref[2:3, :]


def attention_forward(cube, layout, meta, tokens, weights, vecs=None):
    pairs, seq, _ = tokens.shape
    shapes = [
        jax.ShapeDtypeStruct((pairs, seq, 3 * D), BF),
        jax.ShapeDtypeStruct((pairs, H // 2, 2 * seq, seq), BF),
        jax.ShapeDtypeStruct((pairs, seq, D), BF),
        jax.ShapeDtypeStruct((pairs, seq, D), F32),
    ]
    out_specs = [pair_spec(seq, 3 * D), pair_spec(H // 2, 2 * seq, seq), pair_spec(seq, D), pair_spec(seq, D)]
    args = [tokens]
    in_specs = [pair_spec(seq, D)]
    if cube.tiled:
        extra = [((8, D), F32), ((1, 4 * D), F32), ((cube.n, GROUPS, cube.sub, 128), BF)]
        shapes += [jax.ShapeDtypeStruct(s, t) for s, t in extra]
        out_specs += [full_spec(*s) for s, _ in extra]
    else:
        args.append(vecs)
        in_specs.append(full_spec(*vecs.shape))
    return pl.pallas_call(
        functools.partial(attn_fwd_kernel, cube, weights, layout),
        out_shape=shapes,
        grid_spec=pltpu.PrefetchScalarGridSpec(
            num_scalar_prefetch=1,
            grid=(pairs,),
            in_specs=in_specs + any_specs(len(weights.arrays)),
            out_specs=out_specs,
            scratch_shapes=[a_buffer(cube), pltpu.SemaphoreType.DMA],
        ),
        compiler_params=params(),
        cost_estimate=cost(pairs * seq * D * (4 * D + 8 * seq), 30 * pairs * seq * D),
        name="attention_forward",
    )(meta, *args, *weights.arrays)


def norm_parts(r):
    centred = r - jnp.mean(r, axis=-1, keepdims=True)
    inverse = lax.rsqrt(jnp.mean(centred * centred, axis=-1, keepdims=True) + EPSILON)
    return centred * inverse, inverse


def norm_back(e, n, inverse, gain):
    scaled = e * gain
    return inverse * (
        scaled
        - jnp.mean(scaled, axis=-1, keepdims=True)
        - n * jnp.mean(scaled * n, axis=-1, keepdims=True)
    )


def gelu_parts(u):
    gauss = jnp.exp2(u * u * (-0.5 * LOG2E))
    t = 1.0 / (1.0 + (0.3275911 * 0.7071067811865476) * jnp.abs(u))
    poly = t * (
        0.5 * 0.254829592
        + t * (-0.5 * 0.284496736 + t * (0.5 * 1.421413741 + t * (-0.5 * 1.453152027 + t * (0.5 * 1.061405429))))
    )
    tail = poly * gauss
    phi = jnp.where(u >= 0.0, 1.0 - tail, tail)
    return u * phi, phi + u * gauss * 0.3989422804014327


def load_b(cube, b_weights, b_refs, a_weights, a_refs, meta, ups, dn, wo, sems):
    if not cube.tiled:
        pltpu.make_async_copy(b_refs[0], ups, sems.at[0]).start()
        pltpu.make_async_copy(b_refs[1], dn, sems.at[1]).start()
        pltpu.make_async_copy(a_refs[0], wo, sems.at[2]).start()
        return

    def place_b(kind, ref, at, role, device):
        count, first = ((FEW, 0), (MANY, FEW))[role]
        source = ref.at[at, kind * count : (kind + 1) * count]
        return [(source, (ups, dn)[kind].at[device, first : first + count], sems.at[kind])]

    def place_a(ref, at, role, device):
        last = 3 * GROUPS - FEW
        return [(ref.at[at, last : last + GROUPS], wo.at[device], sems.at[2])]

    b_weights.copies(b_refs, meta, functools.partial(place_b, 0))
    b_weights.copies(b_refs, meta, functools.partial(place_b, 1))
    a_weights.copies(a_refs, meta, place_a)


def ffn_kernel(
    cube, layout, pairs, b_weights, a_weights, meta, r_ref, cot_ref, rcot_ref, vec_ref, upb_ref, retr_ref, *refs
):
    nb, na = len(b_weights.arrays), len(a_weights.arrays)
    b_refs, a_refs, refs = refs[:nb], refs[nb : nb + na], refs[nb + na :]
    lo_ref, attn_ref, gone_ref, gctx_ref, sums_ref, gretr_ref = refs[:6]
    outs, refs = refs[6:10], refs[10:]
    ups, dn, wo, slope_ref, sems = refs[:5]
    step = pl.program_id(0)
    seq = r_ref.shape[1]
    if cube.tiled:
        first_ref, act_ref, down_ref, upl_ref = refs[5:9]
        here = pl.ds(pl.multiple_of(step * seq, seq), seq)
    else:
        first_ref, act_ref, down_ref, upl_ref = [o.at[0] for o in outs]
        here = slice(0, seq)
    first_step = step == 0

    @pl.when(first_step)
    def _():
        load_b(cube, b_weights, b_refs, a_weights, a_refs, meta, ups, dn, wo, sems)
        sums_ref[...] = jnp.zeros_like(sums_ref)
        gretr_ref[...] = jnp.zeros_like(gretr_ref)

    vec = lambda i: vec_ref[i : i + 1, :]
    n = cube.n

    def up(c):
        return square(cube, ups, c)

    def down(c):
        return dn[c * n // 4 : (c + 1) * n // 4].reshape(D, D) if cube.tiled else dn[c]

    def pair():
        n1, inv1 = norm_parts(r_ref[0])
        first_norm = n1 * vec(3) + vec(4)
        first_low = first_norm.astype(BF)
        first_ref[here, :] = first_low
        pl.when(first_step)(lambda: wait_load(ups, sems.at[0]))
        output = first_norm + vec(5)
        ahead = dot_nn(first_low, up(0))
        for c in range(4):
            cols = slice(c * D, (c + 1) * D)
            pre = ahead + upb_ref[0:1, cols]
            if c < 3:
                ahead = dot_nn(first_low, up(c + 1))
            active, slope = gelu_parts(pre)
            active = active.astype(BF)
            act_ref[here, cols] = active
            slope_ref[:, cols] = slope
            if c == 0:
                pl.when(first_step)(lambda: wait_load(dn, sems.at[1]))
            output = output + dot_nn(active, down(c))
        n2, inv2 = norm_parts(output)
        result = n2 * vec(6) + vec(7)
        lo_ref[0] = result.astype(BF)
        head = dot_nt(rcot_ref[0], retr_ref[...].reshape(D, -1))
        row = lax.broadcasted_iota(jnp.int32, (seq, 1), 0)
        e = cot_ref[0].astype(F32) + jnp.where(row == 0, head, 0.0)
        top = jnp.where(row[:8] == 0, result[:8], 0.0).astype(BF)
        gretr_ref[...] += dot_tn(top, jnp.broadcast_to(rcot_ref[0], (8, rcot_ref.shape[-1])))
        total = lambda a: jnp.sum(a, axis=0, keepdims=True)
        sums_ref[4:5, 0:D] += total(e * n2)
        sums_ref[5:6, 0:D] += total(e)
        g_second = norm_back(e, n2, inv2, vec(6))
        down_low = g_second.astype(BF)
        down_ref[here, :] = down_low
        sums_ref[3:4, 0:D] += total(down_low.astype(F32))
        g_first = g_second
        ahead = dot_nt(down_low, down(0))
        for c in range(4):
            cols = slice(c * D, (c + 1) * D)
            up_low = (ahead * slope_ref[:, cols]).astype(BF)
            if c < 3:
                ahead = dot_nt(down_low, down(c + 1))
            upl_ref[here, cols] = up_low
            sums_ref[6:7, cols] += total(up_low.astype(F32))
            g_first = g_first + dot_nt(up_low, up(c))
        sums_ref[1:2, 0:D] += total(g_first * n1)
        sums_ref[2:3, 0:D] += total(g_first)
        g_one = norm_back(g_first, n1, inv1, vec(3))
        gone_ref[0] = g_one
        attn_low = g_one.astype(BF)
        attn_ref[0] = attn_low
        sums_ref[0:1, 0:D] += total(attn_low.astype(F32))
        pl.when(first_step)(lambda: wait_load(wo, sems.at[2]))
        gctx_ref[0] = dot_nt(attn_low, wo[...].reshape(D, D)).astype(BF)

    if not cube.tiled:
        pair()
        return
    pl.when(step < pairs)(pair)

    stage, acc_ref, tmp, out_sems = refs[9:13], *refs[13:16]
    me, core = meta[0], meta[1]
    per = n // 4

    def cols(block):
        return pl.ds(pl.multiple_of(block * D, D), D)

    wide = [slice(0, FEW), slice(0, MANY)] * 2
    down_copies = [
        pltpu.make_async_copy(stage[k].at[:, wide[k]], outs[k].at[:, wide[k]], out_sems.at[k]) for k in range(4)
    ]
    up_copies = unit_copies(stage, outs, out_sems, 4, 1, 2)

    @pl.when((step >= pairs) & (step < pairs + 4))
    def _():
        block = step - pairs
        acc_ref[...] = dot_tn(act_ref[:, cols(block)], down_ref[...]).astype(BF).reshape(acc_ref.shape)
        for half in range(2):

            @pl.when(core == half)
            def _(half=half):
                for i in range(per):
                    owner = (i >> cube.core_bit) & 1
                    out = stage[2:4] if owner == half else stage[0:2]
                    distance = lax.bitwise_xor(me, block * per + i ^ (0 if owner == half else cube.core))
                    slots = [meta[layout.slot + (2 * owner + role) * n + distance] for role in range(2)]
                    for k in range(4):
                        put_unit(out, slots, k, acc_ref.at[4 * i + k], 0)

        @pl.when(block == 3)
        def _():
            for copy in down_copies:
                copy.start()

    @pl.when(step >= pairs + 4)
    def _():
        unit = step - pairs - 4
        acc_ref[...] = dot_tn(first_ref[...], upl_ref[:, cols(unit)]).astype(BF).reshape(acc_ref.shape)
        emit_unit(cube, layout, meta, unit, acc_ref, stage, 1)
        for half in range(2):

            @pl.when((unit == 0) & (core == half))
            def _(half=half):
                rows = cube.rows
                tmp[...] = jnp.zeros_like(tmp)
                for i in range(n):
                    near, slot = small_slot(cube, layout, meta, half, i)
                    out = stage[3 if near else 1]
                    tmp[2:8, 0:rows] = sums_ref[0:6, i * rows : (i + 1) * rows]
                    tmp[0:1, 128 : 128 + 4 * rows] = sums_ref[6:7, i * 4 * rows : (i + 1) * 4 * rows]
                    out[slot, 2 * MANY] = tmp[...].astype(BF)
                    block = gretr_ref[i * rows : (i + 1) * rows, :].astype(BF).reshape(GROUPS, cube.sub, 128)
                    parts = [block[k] for k in range(GROUPS)] + [jnp.zeros((cube.sub, D - 128 * GROUPS), BF)]
                    out[slot, 2 * MANY + 1] = jnp.concatenate(parts, axis=1)

        start_and_end(unit, up_copies, down_copies)


def unit_copies(stage, outs, sems, first, at, small):
    copies = []
    for unit in range(4):
        lo, hi = unit * GROUPS, (unit + 1) * GROUPS
        ranges = []
        if lo < FEW:
            ranges += [(k, at * FEW + lo, at * FEW + min(hi, FEW)) for k in (0, 2)]
        if hi > FEW:
            ranges += [(k, at * MANY + max(lo, FEW) - FEW, at * MANY + hi - FEW) for k in (1, 3)]
        if unit == 0:
            ranges += [(k, (at + 1) * MANY, (at + 1) * MANY + small) for k in (1, 3)]
        each = []
        for k, i, j in ranges:
            each.append(pltpu.make_async_copy(stage[k].at[:, i:j], outs[k].at[:, i:j], sems.at[first]))
            first += 1
        copies.append(each)
    return copies


def start_and_end(unit, copies, before):
    for k in range(4):

        @pl.when(unit == k)
        def _(k=k):
            for copy in copies[k]:
                copy.start()

    @pl.when(unit == 3)
    def _():
        for copy in sum(copies, list(before)):
            copy.wait()


def put_unit(out, slots, unit, block, at):
    first = unit * GROUPS
    few = min(max(FEW - first, 0), GROUPS)
    if few:
        out[0][slots[0], at * FEW + first : at * FEW + first + few] = block[0:few]
    if few < GROUPS:
        start = at * MANY + first + few - FEW
        out[1][slots[1], start : start + GROUPS - few] = block[few:GROUPS]


def emit_unit(cube, layout, meta, unit, acc_ref, outs, at):
    me, core = meta[0], meta[1]
    for k in range(4):

        @pl.when(unit == k)
        def _(k=k):
            for side, base, whose in ((outs[0:2], lax.bitwise_xor(me, cube.core), 1 - core), (outs[2:4], me, core)):
                for role in range(2):
                    if (role == 0 and k * GROUPS >= FEW) or (role == 1 and (k + 1) * GROUPS <= FEW):
                        continue
                    first = k * GROUPS
                    few = min(max(FEW - first, 0), GROUPS)
                    for s in range(cube.slots):
                        owner = lax.bitwise_xor(base, meta[layout.dist + (2 * whose + role) * cube.slots + s])
                        if role == 0:
                            side[0][s, at * FEW + first : at * FEW + first + few] = acc_ref[owner, 0:few]
                        else:
                            start = at * MANY + first + few - FEW
                            side[1][s, start : start + GROUPS - few] = acc_ref[owner, few:GROUPS]


def feed_forward(cube, layout, meta, r, cot, rcot, vecs, upb, retr, b_weights, a_weights):
    pairs, seq, _ = r.shape
    ff = 4 * D
    n, sub = cube.n, cube.sub
    wide = lambda k, t: jax.ShapeDtypeStruct((pairs, seq, k), t)
    at = lambda *shape: pl.BlockSpec((1,) + shape, lambda p, *_: (jnp.minimum(p, pairs - 1),) + (0,) * len(shape))
    if cube.tiled:
        square_shape = (n, GROUPS, sub, D)
        buffers = [(n, BLOCKS, sub, D), (n, BLOCKS, sub, D), square_shape]
        terms = grad_shapes(cube, 2, 2)
        term_specs = any_specs(4)
        total = pairs * seq
        more = [pltpu.VMEM((total, k), BF) for k in (D, ff, D, ff)]
        more += [pltpu.VMEM(t.shape, BF) for t in terms]
        more += [pltpu.VMEM(square_shape, BF), pltpu.VMEM((8, D), F32), pltpu.SemaphoreType.DMA((16,))]
    else:
        buffers = [(4, D, D), (4, D, D), (D, D)]
        terms = [wide(k, BF) for k in (D, ff, D, ff)]
        term_specs = [at(seq, k) for k in (D, ff, D, ff)]
        more = []
    return pl.pallas_call(
        functools.partial(ffn_kernel, cube, layout, pairs, b_weights, a_weights),
        out_shape=[
            wide(D, BF),
            wide(D, BF),
            wide(D, F32),
            wide(D, BF),
            jax.ShapeDtypeStruct((8, ff), F32),
            jax.ShapeDtypeStruct((D, rcot.shape[-1]), F32),
        ]
        + terms,
        grid_spec=pltpu.PrefetchScalarGridSpec(
            num_scalar_prefetch=1,
            grid=(pairs + 8 if cube.tiled else pairs,),
            in_specs=[
                at(seq, D),
                at(seq, D),
                at(1, rcot.shape[-1]),
                full_spec(*vecs.shape),
                full_spec(*upb.shape),
                full_spec(*retr.shape),
            ]
            + any_specs(len(b_weights.arrays) + len(a_weights.arrays)),
            out_specs=[
                at(seq, D),
                at(seq, D),
                at(seq, D),
                at(seq, D),
                full_spec(8, ff),
                full_spec(D, rcot.shape[-1]),
            ]
            + term_specs,
            scratch_shapes=[pltpu.VMEM(b, BF) for b in buffers]
            + [pltpu.VMEM((seq, ff), F32), pltpu.SemaphoreType.DMA((3,))]
            + more,
        ),
        compiler_params=params(),
        cost_estimate=cost(pairs * seq * D * 25 * D, 40 * pairs * seq * D),
        name="feed_forward",
    )(meta, r, cot, rcot, vecs, upb, retr, *b_weights.arrays, *a_weights.arrays)


def attn_bwd_kernel(first, joint_ref, p_ref, gctx_ref, *refs):
    if first:
        gj_ref, sums_ref = refs
        sums = jnp.zeros(sums_ref.shape, F32)
    else:
        _, before_ref, gj_ref, sums_ref = refs
        sums = before_ref[...]

    @pl.when(pl.program_id(0) == 0)
    def _():
        sums_ref[...] = sums

    sides = head_masks()
    for h2 in range(H // 2):
        cut = lambda base: slice(base + h2 * 2 * DH, base + (h2 + 1) * 2 * DH)
        q2 = joint_ref[0, :, cut(0)]
        k2 = joint_ref[0, :, cut(D)]
        v2 = joint_ref[0, :, cut(2 * D)]
        go2 = gctx_ref[0, :, cut(0)]
        seq = q2.shape[0]
        gq = gk = gv = 0.0
        for hh in range(2):
            go = go2 * sides[hh]
            p = p_ref[0, h2, hh * seq : (hh + 1) * seq]
            pf = p.astype(F32)
            t = dot_nt(go, v2) * pf
            gs = (t - pf * jnp.sum(t, axis=-1, keepdims=True)).astype(BF)
            gv = gv + dot_tn(p, go)
            gq = gq + dot_nn(gs, k2 * sides[hh])
            gk = gk + dot_tn(gs, q2 * sides[hh])
        gj_ref[0, :, cut(0)] = (gq * SCALE).astype(BF)
        gj_ref[0, :, cut(D)] = (gk * SCALE).astype(BF)
        gj_ref[0, :, cut(2 * D)] = gv.astype(BF)
    for row, j in ((0, 0), (1, 2)):
        part = gj_ref[0, :, j * D : (j + 1) * D].astype(F32)
        sums_ref[row : row + 1, :] += jnp.sum(part, axis=0, keepdims=True)


def attention_backward(joint, probs, gctx, at, count, before=None):
    pairs, seq, _ = joint.shape
    in_specs = [
        pair_spec(seq, 3 * D, first=at),
        pair_spec(H // 2, 2 * seq, seq, first=at),
        pair_spec(seq, D, first=at),
    ]
    args = [joint, probs, gctx]
    aliases = {}
    if before is not None:
        in_specs += any_specs(1) + [full_spec(8, D)]
        args += list(before)
        aliases = {3: 0}
    return pl.pallas_call(
        functools.partial(attn_bwd_kernel, before is None),
        out_shape=(jax.ShapeDtypeStruct((pairs, seq, 3 * D), BF), jax.ShapeDtypeStruct((8, D), F32)),
        grid=(count,),
        in_specs=in_specs,
        out_specs=(pair_spec(seq, 3 * D, first=at), full_spec(8, D)),
        input_output_aliases=aliases,
        compiler_params=params(),
        cost_estimate=cost(count * seq * D * 16 * seq, 40 * count * seq * D),
        name="attention_backward",
    )(*args)


def token_grad_kernel(cube, weights, meta, gj_ref, gone_ref, *refs):
    count = len(weights.arrays)
    pieces, refs = refs[:count], refs[count:]
    gt_ref, blocks, sem = refs

    @pl.when(pl.program_id(0) == 0)
    def _():
        load_a(cube, weights, meta, pieces, blocks, sem, 3)
        wait_load(blocks, sem)

    acc = gone_ref[...].reshape(-1, D)
    for j in range(3):
        acc = acc + dot_nt(gj_ref[:, :, j * D : (j + 1) * D].reshape(-1, D), square(cube, blocks, j))
    gt_ref[...] = acc.astype(BF).reshape(gt_ref.shape)


def token_grad(cube, meta, g_joint, g_one, weights):
    pairs, seq, _ = g_joint.shape
    per = 2 if pairs % 2 == 0 else 1
    block = lambda width: pl.BlockSpec((per, seq, width), lambda p, *_: (p, 0, 0))
    return pl.pallas_call(
        functools.partial(token_grad_kernel, cube, weights),
        out_shape=jax.ShapeDtypeStruct((pairs, seq, D), BF),
        grid_spec=pltpu.PrefetchScalarGridSpec(
            num_scalar_prefetch=1,
            grid=(pairs // per,),
            in_specs=[block(3 * D), block(D)] + any_specs(len(weights.arrays)),
            out_specs=block(D),
            scratch_shapes=[a_buffer(cube, 3), pltpu.SemaphoreType.DMA],
        ),
        compiler_params=params(),
        cost_estimate=cost(pairs * seq * D * 3 * D, 12 * pairs * seq * D),
        name="token_grad",
    )(meta, g_joint, g_one, *weights.arrays)


def small_slot(cube, layout, meta, half, i):
    owner = (i >> cube.core_bit) & 1
    distance = lax.bitwise_xor(meta[0], i ^ (0 if owner == half else cube.core))
    return owner == half, meta[layout.slot + (2 * owner + 1) * cube.n + distance]


def unit_grad_kernel(cube, layout, meta, a_ref, b_ref, qv_ref, a2_ref, b2_ref, *refs):
    outs, acc_ref, tmp, left2, right2, sems = refs[0:4], *refs[4:9]
    stage = refs[9:13]
    unit = pl.program_id(0)
    core = meta[1]
    late = [pltpu.make_async_copy(a2_ref, left2, sems.at[0]), pltpu.make_async_copy(b2_ref, right2, sems.at[1])]

    def make(left, right):
        acc_ref[...] = dot_tn(left[...], right[...]).astype(BF).reshape(acc_ref.shape)

    @pl.when(unit == 0)
    def _():
        for copy in late:
            copy.start()

    pl.when(unit < 3)(lambda: make(a_ref, b_ref))

    @pl.when(unit == 3)
    def _():
        for copy in late:
            copy.wait()
        make(left2, right2)

    emit_unit(cube, layout, meta, unit, acc_ref, stage, 0)
    for half in range(2):

        @pl.when((unit == 0) & (core == half))
        def _(half=half):
            tmp[...] = jnp.zeros_like(tmp)
            for i in range(cube.n):
                near, slot = small_slot(cube, layout, meta, half, i)
                tmp[0:2, 0 : cube.rows] = qv_ref[0:2, i * cube.rows : (i + 1) * cube.rows]
                stage[3 if near else 1][slot, MANY] = tmp[...].astype(BF)

    start_and_end(unit, unit_copies(stage, outs, sems, 2, 0, 1), [])


def by_distance(cube, meta, units):
    me, core = meta[0], meta[1]
    dist = jnp.asarray([cube.dist(p) for p in range(4)], jnp.int32)
    blocks = jnp.concatenate([u.reshape(cube.n, GROUPS, cube.sub, D) for u in units], axis=1)
    parts = [blocks[:, :FEW], blocks[:, FEW:]]
    out = []
    for whose in (1, 0):
        base = me ^ (cube.core * whose)
        out.append([jnp.take(parts[role], base ^ dist[2 * (core ^ whose) + role], axis=0) for role in range(2)])
    return out


def grad_plain_kernel(a_ref, b_ref, out_ref):
    out_ref[...] = dot_tn(a_ref[...], b_ref[...]).astype(BF)


def plain_grad(a, b):
    return pl.pallas_call(
        grad_plain_kernel,
        out_shape=jax.ShapeDtypeStruct((D, D), BF),
        grid=(1,),
        in_specs=[full_spec(*a.shape), full_spec(*b.shape)],
        out_specs=full_spec(D, D),
        compiler_params=params(),
        name="plain_grad",
    )(a, b)


def grad_shapes(cube, sets, small):
    few = (cube.slots, sets * FEW, cube.sub, D)
    many = (cube.slots, sets * MANY + small, cube.sub, D)
    return [jax.ShapeDtypeStruct(s, BF) for s in (few, many, few, many)]


def plain_terms(cube, meta, sums, gretr, first_low, active, down_low, up_low):
    n = cube.n
    blocks = [plain_grad(active[:, j * D : (j + 1) * D], down_low) for j in range(4)]
    whole = jnp.concatenate(blocks, axis=0).reshape(n, 4, -1, D)
    down = sum(by_distance(cube, meta, [whole[:, j] for j in range(4)]), [])
    ups = [plain_grad(first_low, up_low[:, j * D : (j + 1) * D]).reshape(n, -1, D) for j in range(4)]
    up = sum(by_distance(cube, meta, ups), [])
    terms = [jnp.concatenate(pair, axis=1) for pair in zip(down, up)]
    small = small_by_distance(cube, meta, jnp.zeros((2, D), F32), sums, gretr)
    for k in range(2):
        terms[2 * k + 1] = jnp.concatenate([terms[2 * k + 1], small[k]], axis=1)
    return terms


def unit_grads(cube, layout, meta, a, b, tail):
    n = cube.n
    total = a.shape[0]
    if not cube.tiled:
        pairs = [(a, b[:, j * D : (j + 1) * D]) for j in range(b.shape[1] // D)] + [tail[:2]]
        send, keep = by_distance(cube, meta, [plain_grad(x, y).reshape(n, -1, D) for x, y in pairs])
        small = small_by_distance(cube, meta, tail[2], None, None)
        send[1] = jnp.concatenate([send[1], small[0]], axis=1)
        keep[1] = jnp.concatenate([keep[1], small[1]], axis=1)
        return send + keep
    top = b.shape[1] // D - 1
    args = [a, b]
    in_specs = [
        full_spec(total, D),
        pl.BlockSpec((total, D), lambda s, *_: (0, jnp.minimum(s, top))),
    ]
    args += [tail[2], tail[0], tail[1]]
    in_specs += [full_spec(*tail[2].shape)] + any_specs(2)
    return pl.pallas_call(
        functools.partial(unit_grad_kernel, cube, layout),
        out_shape=grad_shapes(cube, 1, 1),
        grid_spec=pltpu.PrefetchScalarGridSpec(
            num_scalar_prefetch=1,
            grid=(4,),
            in_specs=in_specs,
            out_specs=any_specs(4),
            scratch_shapes=[pltpu.VMEM((n, GROUPS, cube.sub, D), BF), pltpu.VMEM((8, D), F32)]
            + [pltpu.VMEM((total, D), BF)] * 2
            + [pltpu.SemaphoreType.DMA((14,))]
            + [pltpu.VMEM(t.shape, BF) for t in grad_shapes(cube, 1, 1)],
        ),
        compiler_params=params(),
        cost_estimate=cost(total * D * 4 * D, 40 * D * D),
        name="unit_grads",
    )(meta, *args)


class Reduce:
    def __init__(self, cube, terms):
        self.cube = cube
        self.terms = terms[2:]
        self.flight = [cube.swap_core(s) for s in terms[:2]]
        self.r = cube.rounds

    @staticmethod
    def add(a, b):
        return a.astype(F32) + b.astype(F32)

    def tie(self, *values):
        out, self.flight = lax.optimization_barrier((values, self.flight))
        return out[0] if len(out) == 1 else out

    def step(self, other=None):
        self.r -= 1
        pairs = list(zip(self.terms, self.flight))
        half = self.terms[0].shape[0] // 2
        away = [self.add(a[half:], b[half:]).astype(BF) for a, b in pairs]
        self.terms = [self.add(a[:half], b[:half]).astype(BF) for a, b in pairs]
        if other is not None:
            away, other.flight = lax.optimization_barrier((away, other.flight))
        self.flight = [self.cube.swap(away[role], role, self.r) for role in range(2)]

    def finish(self):
        self.r = 0
        pairs = list(zip(self.terms, self.flight))
        away = [[self.add(a[s : s + 1], b[s : s + 1]).astype(BF) for s in (3, 2, 1)] for a, b in pairs]
        self.terms = [self.add(a[:1], b[:1]) for a, b in pairs]
        self.flight = [
            [self.cube.swap_rounds(x, role, r) for x, r in zip(away[role], ((0, 1), (1,), (0,)))]
            for role in reversed(range(2))
        ][::-1]

    def result(self):
        shards = []
        for term, got in zip(self.terms, self.flight):
            total = term.astype(F32)
            for g in got if isinstance(got, list) else [got]:
                total = total + g.astype(F32)
            shards.append(total[0])
        return shards


def small_by_distance(cube, meta, sums_qv, sums, gretr):
    n, rows = cube.n, cube.rows
    me, core = meta[0], meta[1]
    wide = cube.small * cube.sub
    vec = jnp.zeros((6, D), F32) if sums is None else sums[:6, :D]
    upb = jnp.zeros((4 * D,), F32) if sums is None else sums[6]
    vec = jnp.concatenate([sums_qv[:2], vec], axis=0)
    vec = jnp.pad(vec.reshape(8, n, rows).transpose(1, 0, 2), ((0, 0), (0, wide - 8), (0, 128 - rows)))
    upb = jnp.pad(upb.reshape(n, 1, 4 * rows), ((0, 0), (0, wide - 1), (0, D - 128 - 4 * rows)))
    block = jnp.concatenate([vec, upb], axis=2)
    if gretr is not None:
        more = jnp.pad(gretr.reshape(n, 1, -1), ((0, 0), (0, wide - 1), (0, D - rows * gretr.shape[1])))
        block = jnp.concatenate([block, more], axis=1)
    dist = jnp.asarray([cube.dist(1), cube.dist(3)], jnp.int32)
    out = []
    for whose in (1, 0):
        part = jnp.take(block.astype(BF), (me ^ (cube.core * whose)) ^ dist[core ^ whose], axis=0)
        out.append(part.reshape(cube.slots, -1, cube.sub, D))
    return out


def per_device(cube, tokens, pair_lengths, out_cotangent, retr_cotangent, *weights):
    (
        qkv_weight,
        query_bias,
        value_bias,
        out_weight,
        out_bias,
        first_gain,
        first_shift,
        up_weight,
        up_bias,
        down_weight,
        down_bias,
        second_gain,
        second_shift,
        retr_weight,
    ) = weights
    me = (lax.axis_index("dp") * lax.axis_size("fsdp") + lax.axis_index("fsdp")).astype(jnp.int32)
    n, rows = cube.n, cube.rows
    core = (me >> cube.core_bit) & 1
    pairs, seq, _ = tokens.shape
    proj = retr_weight.shape[1]
    layout = Meta(cube, pairs)
    meta = Meta.build(cube, me, core, pair_lengths)

    own_vec = jnp.stack(
        [query_bias, value_bias, out_bias, first_gain, first_shift, down_bias, second_gain, second_shift]
    )
    own = pack_own(cube, qkv_weight, out_weight, up_weight, down_weight, retr_weight, own_vec, up_bias[None])
    gather = Gather(cube, own)
    pieces_a = gather.side_a()
    rcot = retr_cotangent[:, None, :]
    if cube.tiled:
        a_weights = Weights(cube, layout, pieces_a)
        odd_weights = Weights(cube, layout, [p for p in pieces_a if p[1] == 1])
        joint, probs, ctx, r, vecs, upb, retr = attention_forward(cube, layout, meta, tokens, a_weights)
        r, pieces_b = gather.side_b(r)
        b_weights = Weights(cube, layout, pieces_b)
    else:
        few, many = natural_blocks(cube, me, core, pieces_a)
        natural = four_units(cube, jnp.concatenate([few, many[:, :MANY]], axis=1))
        natural = [u.reshape(D, D) for u in natural]
        tiny, retr = [
            many[:, at : at + cube.small].reshape(n, -1, D) for at in (MANY, MANY + cube.small)
        ]
        tiny = tiny.astype(F32)
        vecs = tiny[:, :8, :rows].transpose(1, 0, 2).reshape(8, D)
        upb = tiny[:, 0, 128 : 128 + 4 * rows].reshape(1, 4 * D)
        retr = retr[:, 0, : rows * proj].reshape(D, proj)
        a_weights = Weights(cube, layout, natural=natural)
        odd_weights = Weights(cube, layout, natural=natural[3:])
        joint, probs, ctx, r = attention_forward(cube, layout, meta, tokens, a_weights, vecs)
        r, pieces_b = gather.side_b(r)
        few, many = natural_blocks(cube, me, core, pieces_b)
        ups = four_units(cube, jnp.concatenate([few[:, :FEW], many[:, :MANY]], axis=1))
        ups = jnp.stack([u.reshape(D, D) for u in ups])
        downs = jnp.concatenate([few[:, FEW:], many[:, MANY:]], axis=1).reshape(4, D, D)
        b_weights = Weights(cube, layout, natural=[ups, downs])

    layer_output, attn_low, g_one, g_ctx, sums, g_retr, *terms = feed_forward(
        cube, layout, meta, r, out_cotangent, rcot, vecs, upb, retr, b_weights, odd_weights
    )
    flat = lambda a: a.reshape(pairs * seq, a.shape[-1])
    if not cube.tiled:
        terms = plain_terms(cube, meta, sums, g_retr, *[flat(t) for t in terms])
    g_ctx, terms = lax.optimization_barrier((g_ctx, terms))
    ffn = Reduce(cube, terms)

    calls = [1, pairs - 1]
    state, at = None, 0
    for count in calls:
        state = ffn.tie(attention_backward(joint, probs, g_ctx, at, count, state))
        at += count
        if ffn.r:
            ffn.step()
    g_joint, sums_qv = state
    tail_args = (flat(ctx), flat(attn_low), sums_qv)
    terms = unit_grads(cube, layout, meta, flat(tokens), flat(g_joint), tail_args)
    terms = ffn.tie(terms)
    tail = Reduce(cube, terms)
    ffn.step()
    g_joint = tail.tie(g_joint)
    tail.step()
    grad_tokens = token_grad(cube, meta, g_joint, g_one, a_weights)
    grad_tokens = tail.tie(grad_tokens)
    ffn.flight = tail.tie(ffn.flight)
    tail.step(ffn)
    ffn.step()
    while tail.r > 2:
        tail.step()
    ffn.flight = tail.tie(ffn.flight)
    tail.finish()
    while ffn.r:
        ffn.step()

    few, many = tail.result()
    grad_q, grad_k, grad_v, grad_o = jnp.concatenate([few, many[:MANY]], axis=0).reshape(4, rows, D)
    own_qv = many[MANY:].reshape(-1, D)
    few, many = ffn.result()
    grad_down = jnp.concatenate([few[:FEW], many[:MANY]], axis=0).reshape(4 * rows, D)
    ups = jnp.concatenate([few[FEW:], many[MANY : 2 * MANY]], axis=0).reshape(4, rows, D)
    own_vec, own_retr = many[2 * MANY :].reshape(2, -1, D)
    take = lambda i: own_vec[i, :rows]
    if cube.tiled:
        own_retr = own_retr[:8, : GROUPS * proj].reshape(8, GROUPS, proj).transpose(1, 0, 2).reshape(rows, proj)
    else:
        own_retr = own_retr[0, : rows * proj].reshape(rows, proj)
    return (
        layer_output,
        grad_tokens,
        jnp.concatenate([grad_q, grad_k, grad_v], axis=1),
        own_qv[0, :rows],
        own_qv[1, :rows],
        grad_o,
        take(2),
        take(3),
        take(4),
        jnp.concatenate(list(ups), axis=1),
        own_vec[0, 128 : 128 + 4 * rows],
        grad_down,
        take(5),
        take(6),
        take(7),
        own_retr,
    )


def solution(mesh):
    row = P(AXES)
    return jax.shard_map(
        functools.partial(per_device, Cube(mesh)),
        mesh=mesh,
        in_specs=(row,) * 18,
        out_specs=(row,) * 16,
        check_vma=False,
    )
```

```python
import functools

import jax
import jax.numpy as jnp
from jax import lax
from jax.experimental import pallas as pl
from jax.experimental.pallas import tpu as pltpu
from jax.sharding import PartitionSpec as P

H = 12
DH = 64
D = H * DH
EPSILON = 1e-12
SCALE = 0.125
LOG2E = 1.4426950408889634
AXES = ("dp", "fsdp")
GROUPS = 3
FEW, MANY = 4, 8
BLOCKS = FEW + MANY
VMEM_LIMIT = 60 * 1024 * 1024
BF = jnp.bfloat16
F32 = jnp.float32


def xor_masks(size, unit):
    return [(2 * (1 << b) - 1) * unit for b in range(size.bit_length() - 1)]


class Cube:
    def __init__(self, mesh):
        dp, fsdp = mesh.shape["dp"], mesh.shape["fsdp"]
        side = 1 << ((fsdp.bit_length() - 1) // 2)
        self.n = dp * fsdp
        self.core = fsdp
        self.core_bit = fsdp.bit_length() - 1
        self.x, self.y = xor_masks(side, 1), xor_masks(fsdp // side, side)
        self.z = xor_masks(dp // 2, 2 * fsdp)
        self.rounds = len(self.x + self.y + self.z)
        self.rows = D // self.n
        self.sub = self.rows // GROUPS
        self.slots = self.n // 2
        self.small = -(-8 // self.sub)
        self.tiled = self.sub % 8 == 0 and self.n // 4 % (2 * self.core) == 0

    def order(self, part):
        turn = -1 if part >= 2 else 1
        flat, deep = (self.x + self.y)[::turn], self.z[::turn]
        return deep + flat if part % 2 else flat + deep

    def dist(self, part):
        out = [0]
        for mask in self.order(part):
            out = out + [s ^ mask for s in out]
        return out

    def slot(self, part):
        table = [0] * self.n
        for at, d in enumerate(self.dist(part)):
            table[d] = at
        return table

    def swap_core(self, x):
        return lax.ppermute(x, AXES, [(i, i ^ self.core) for i in range(self.n)])

    def swap(self, x, role, r):
        return self.swap_rounds(x, role, [r])

    def swap_rounds(self, x, role, rounds):
        pairs = []
        for i in range(self.n):
            order = self.order(2 * ((i >> self.core_bit) & 1) + role)
            to = i
            for r in rounds:
                to ^= order[r]
            pairs.append((i, to))
        return lax.ppermute(x, AXES, pairs)


class Gather:
    def __init__(self, cube, own):
        self.cube = cube
        known = list(own)
        first = [FEW, MANY + 2 * cube.small]
        for r in range(cube.rounds - 1):
            got = [cube.swap(known[role], role, r) for role in range(2)]
            known, got = lax.optimization_barrier((known, got))
            if r < cube.rounds - 2:
                known = [jnp.concatenate([a, b], axis=0) for a, b in zip(known, got)]
        self.near_a = [jnp.concatenate([a[:, :f], b[:, :f]], axis=0) for a, b, f in zip(known, got, first)]
        self.rest = [(a[:, f:], b[:, f:]) for a, b, f in zip(known, got, first)]

    def link(self, near):
        return [self.cube.swap(near[role], role, self.cube.rounds - 1) for role in range(2)]

    def pieces(self, near, far, near_other, far_other):
        half = self.cube.slots // 2
        out = []
        for role in range(2):
            out += [(near[role], role, 0, 0), (far[role], role, 0, half)]
            out += [(near_other[role], role, 1, 0), (far_other[role], role, 1, half)]
        return out

    def side_a(self):
        core = self.cube.swap_core
        near_a = self.near_a
        far = self.link(near_a)
        near_b = [jnp.concatenate(pair, axis=0) for pair in self.rest]
        near_a, far, near_b = lax.optimization_barrier((near_a, far, near_b))
        self.near_b = near_b
        out = self.pieces(near_a, far, [core(x) for x in near_a], [core(x) for x in far])
        self.far_b = self.link(near_b)
        self.near_b_other = [core(x) for x in near_b]
        return out

    def side_b(self, after):
        after, self.far_b = lax.optimization_barrier((after, self.far_b))
        other = [self.cube.swap_core(x) for x in self.far_b]
        return after, self.pieces(self.near_b, self.far_b, self.near_b_other, other)


def natural_blocks(cube, me, core, pieces):
    out = []
    at = jnp.arange(cube.n, dtype=jnp.int32)
    for role in range(2):
        arrays = [
            jnp.concatenate([p for p, r, w, _ in pieces if r == role and w == whose], axis=0) for whose in range(2)
        ]
        table = jnp.asarray([cube.slot(role), cube.slot(2 + role)], jnp.int32)
        source = at ^ me
        whose = (source >> cube.core_bit) & 1
        slot = table[core ^ whose, source ^ (whose * cube.core)]
        out.append(jnp.take(jnp.concatenate(arrays, axis=0), slot + whose * cube.slots, axis=0))
    return out


def four_units(cube, blocks):
    return [blocks[:, u * GROUPS : (u + 1) * GROUPS].reshape(cube.n, cube.rows, D) for u in range(4)]


class Meta:
    def __init__(self, cube, pairs):
        self.lengths = 2
        self.dist = 2 + pairs
        self.slot = self.dist + 4 * cube.slots

    @staticmethod
    def build(cube, me, core, pair_lengths):
        tables = [cube.dist(p) for p in range(4)] + [cube.slot(p) for p in range(4)]
        tables = jnp.asarray(sum(tables, []), jnp.int32)
        return jnp.concatenate([me[None], core[None], pair_lengths, tables])


def dot_nn(a, b):
    return jnp.dot(a, b, preferred_element_type=F32)


def dot_nt(a, b):
    return lax.dot_general(a, b, (((1,), (1,)), ((), ())), preferred_element_type=F32)


def dot_tn(a, b):
    return lax.dot_general(a, b, (((0,), (0,)), ((), ())), preferred_element_type=F32)


def params():
    return pltpu.CompilerParams(dimension_semantics=("arbitrary",), vmem_limit_bytes=VMEM_LIMIT)


def cost(macs, moved):
    return pl.CostEstimate(flops=2 * macs, bytes_accessed=moved, transcendentals=0)


def pair_spec(*shape, first=0):
    return pl.BlockSpec((1,) + shape, lambda p, *_: (p + first,) + (0,) * len(shape))


def full_spec(*shape):
    return pl.BlockSpec(shape, lambda p, *_: (0,) * len(shape))


def any_specs(n):
    return [pl.BlockSpec(memory_space=pl.ANY)] * n


class Weights:
    def __init__(self, cube, layout, pieces=(), natural=()):
        self.cube, self.layout = cube, layout
        self.arrays = list(natural) if natural else [p[0] for p in pieces]
        self.what = [p[1:] for p in pieces]

    def copies(self, refs, meta, place):
        cube = self.cube
        me, core = meta[0], meta[1]
        for ref, (role, whose, first) in zip(refs, self.what):
            base = lax.bitwise_xor(me, whose * cube.core)
            table = self.layout.dist + (2 * lax.bitwise_xor(core, whose) + role) * cube.slots + first
            for at in range(ref.shape[0]):
                device = lax.bitwise_xor(base, meta[table + at])
                for source, target, sem in place(ref, at, role, device):
                    pltpu.make_async_copy(source, target, sem).start()


def wait_load(buf, sem):
    pltpu.make_async_copy(buf, buf, sem).wait()


def square(cube, blocks, unit):
    return blocks[:, unit * GROUPS : (unit + 1) * GROUPS].reshape(D, D) if cube.tiled else blocks[unit]


def pack_kernel(cube, qkv, out, up, down, retr, vec, upb, few, many):
    sub, rows = cube.sub, cube.rows
    blocks = [(i // GROUPS, i % GROUPS * sub) for i in range(BLOCKS)]
    for role, chosen in enumerate((blocks[:FEW], blocks[FEW:])):
        at, own = 0, (few, many)[role].at[0]
        for unit, row in chosen:
            part = slice(unit * D, (unit + 1) * D)
            own[at] = qkv[row : row + sub, part] if unit < 3 else out[row : row + sub, :]
            at += 1
        if role:
            own[at] = jnp.zeros((sub, D), BF)
            own[at, 0:8, 0:rows] = vec[...]
            own[at, 0:1, 128 : 128 + 4 * rows] = upb[...]
            own[at + 1] = jnp.zeros((sub, D), BF)
            for i in range(GROUPS):
                own[at + 1, :, 128 * i : 128 * (i + 1)] = retr[i * sub : (i + 1) * sub, :]
            at += 2
        for unit, row in chosen:
            own[at] = up[row : row + sub, unit * D : (unit + 1) * D]
            at += 1
        for unit, row in chosen:
            own[at] = down[unit * rows + row : unit * rows + row + sub, :]
            at += 1


def pack_own(cube, qkv, out, up, down, retr, vec, upb):
    sub, rows = cube.sub, cube.rows
    if cube.tiled:
        args = (qkv, out, up, down, retr, vec, upb)
        shapes = [(1, 3 * FEW, sub, D), (1, 3 * MANY + 2, sub, D)]
        return pl.pallas_call(
            functools.partial(pack_kernel, cube),
            out_shape=[jax.ShapeDtypeStruct(x, BF) for x in shapes],
            grid=(1,),
            in_specs=[full_spec(*a.shape) for a in args],
            out_specs=[full_spec(*x) for x in shapes],
            compiler_params=params(),
            name="pack_own",
        )(*args)
    wide = cube.small * sub
    tiny = jnp.pad(vec, ((0, wide - 8), (0, D - rows)))
    tiny = tiny.at[0, 128 : 128 + 4 * rows].set(upb[0])
    tail = jnp.pad(retr.reshape(1, -1), ((0, wide - 1), (0, D - retr.size)))
    a = jnp.concatenate([qkv[:, j * D : (j + 1) * D] for j in range(3)] + [out])
    b = jnp.concatenate([up[:, j * D : (j + 1) * D] for j in range(4)])
    cut = FEW * sub
    roles = [a[:cut], b[:cut], down[:cut]], [a[cut:], tiny, tail, b[cut:], down[cut:]]
    return [jnp.concatenate(x).reshape(1, -1, sub, D) for x in roles]


def spread_vectors(cube, slabs, width, count):
    n = slabs.shape[0] // 8
    lane = lax.broadcasted_iota(jnp.int32, (128, D), 1).astype(F32)
    row = lax.broadcasted_iota(jnp.int32, (128, D), 0).astype(F32)
    inside = lane - jnp.floor((lane + 0.5) * (1.0 / width)) * width
    pick = jnp.where(jnp.abs(inside - row) < 0.5, 1.0, 0.0).astype(BF)
    full = dot_nn(slabs, pick).reshape(n, 8, D)
    at = lax.broadcasted_iota(jnp.int32, (n, 8, D), 2) - lax.broadcasted_iota(jnp.int32, (n, 8, D), 0) * width
    return jnp.sum(jnp.where((at >= 0) & (at < width), full, 0.0), axis=0)


def head_masks():
    lane = lax.broadcasted_iota(jnp.int32, (1, 2 * DH), 1)
    first = jnp.where(lane < DH, 1.0, 0.0)
    return first.astype(BF), (1.0 - first).astype(BF)


def stack_heads(two, sides):
    return jnp.concatenate([two * sides[0], two * sides[1]], axis=0)


def join_heads(stacked):
    half = stacked.shape[0] // 2
    lane = lax.broadcasted_iota(jnp.int32, (1, 2 * DH), 1)
    return jnp.where(lane < DH, stacked[:half], stacked[half:])


def load_a(cube, weights, meta, refs, blocks, sem, count=4):
    if not cube.tiled:
        for u in range(count):
            pltpu.make_async_copy(refs[u], blocks.at[u], sem).start()
        return

    def place(ref, at, role, device):
        if role == 0:
            return [(ref.at[at], blocks.at[device, 0:FEW], sem)]
        many = ref.shape[1] if count == 4 else count * GROUPS - FEW
        return [(ref.at[at, 0:many], blocks.at[device, FEW : FEW + many], sem)]

    weights.copies(refs, meta, place)


def a_buffer(cube, count=4):
    many = BLOCKS + 2 if count == 4 else count * GROUPS
    return pltpu.VMEM((cube.n, many, cube.sub, D) if cube.tiled else (count, D, D), BF)


def attn_fwd_kernel(cube, weights, layout, meta, x_ref, *refs):
    count = len(weights.arrays)
    if not cube.tiled:
        vec_ref, refs = refs[0], refs[1:]
    pieces, refs = refs[:count], refs[count:]
    joint_ref, p_ref, ctx_ref, r_ref = refs[:4]
    refs = refs[4:]
    if cube.tiled:
        vec_ref, upb_ref, retr_ref = refs[:3]
        refs = refs[3:]
    blocks, sem = refs
    pair = pl.program_id(0)

    @pl.when(pair == 0)
    def _():
        load_a(cube, weights, meta, pieces, blocks, sem)
        wait_load(blocks, sem)
        if cube.tiled:
            n = cube.n
            per = n // 4
            vec_ref[...] = spread_vectors(cube, blocks[:, BLOCKS, :, 0:128].reshape(n * 8, 128), cube.rows, n)
            for c in range(4):
                slabs = blocks[c * per : (c + 1) * per, BLOCKS, :, 128:256].reshape(per * 8, 128)
                upb_ref[0:1, c * D : (c + 1) * D] = spread_vectors(cube, slabs, 4 * cube.rows, per)[0:1, :]
            for i in range(GROUPS):
                retr_ref[:, i] = blocks[:, BLOCKS + 1, :, 128 * i : 128 * (i + 1)]

    weight = lambda u: square(cube, blocks, u)
    x = x_ref[0]
    seq = x.shape[0]
    q = (dot_nn(x, weight(0)) + vec_ref[0:1, :]).astype(BF)
    k = dot_nn(x, weight(1)).astype(BF)
    v = (dot_nn(x, weight(2)) + vec_ref[1:2, :]).astype(BF)
    joint_ref[0, :, 0:D] = q
    joint_ref[0, :, D : 2 * D] = k
    joint_ref[0, :, 2 * D : 3 * D] = v
    length = meta[layout.lengths + pair]
    key = lax.broadcasted_iota(jnp.int32, (seq, 1), 0)
    mask = jnp.where(key < length, 0.0, -1e30)
    sides = head_masks()
    for h2 in range(H // 2):
        cols = slice(h2 * 2 * DH, (h2 + 1) * 2 * DH)
        s = dot_nt(k[:, cols], stack_heads(q[:, cols], sides)) * (SCALE * LOG2E) + mask
        e = jnp.exp2(s - jnp.max(s, axis=0, keepdims=True))
        p = (e * (1.0 / jnp.sum(e, axis=0, keepdims=True))).astype(BF)
        p_ref[0, h2] = p
        ctx_ref[0, :, cols] = join_heads(dot_tn(p, v[:, cols])).astype(BF)
    r_ref[0] = x.astype(F32) + dot_nn(ctx_ref[0], weight(3)) + vec_ref[2:3, :]


def attention_forward(cube, layout, meta, tokens, weights, vecs=None):
    pairs, seq, _ = tokens.shape
    shapes = [
        jax.ShapeDtypeStruct((pairs, seq, 3 * D), BF),
        jax.ShapeDtypeStruct((pairs, H // 2, seq, 2 * seq), BF),
        jax.ShapeDtypeStruct((pairs, seq, D), BF),
        jax.ShapeDtypeStruct((pairs, seq, D), F32),
    ]
    out_specs = [pair_spec(seq, 3 * D), pair_spec(H // 2, seq, 2 * seq), pair_spec(seq, D), pair_spec(seq, D)]
    args = [tokens]
    in_specs = [pair_spec(seq, D)]
    if cube.tiled:
        extra = [((8, D), F32), ((1, 4 * D), F32), ((cube.n, GROUPS, cube.sub, 128), BF)]
        shapes += [jax.ShapeDtypeStruct(s, t) for s, t in extra]
        out_specs += [full_spec(*s) for s, _ in extra]
    else:
        args.append(vecs)
        in_specs.append(full_spec(*vecs.shape))
    return pl.pallas_call(
        functools.partial(attn_fwd_kernel, cube, weights, layout),
        out_shape=shapes,
        grid_spec=pltpu.PrefetchScalarGridSpec(
            num_scalar_prefetch=1,
            grid=(pairs,),
            in_specs=in_specs + any_specs(len(weights.arrays)),
            out_specs=out_specs,
            scratch_shapes=[a_buffer(cube), pltpu.SemaphoreType.DMA],
        ),
        compiler_params=params(),
        cost_estimate=cost(pairs * seq * D * (4 * D + 8 * seq), 30 * pairs * seq * D),
        name="attention_forward",
    )(meta, *args, *weights.arrays)


def norm_parts(r):
    centred = r - jnp.mean(r, axis=-1, keepdims=True)
    inverse = lax.rsqrt(jnp.mean(centred * centred, axis=-1, keepdims=True) + EPSILON)
    return centred * inverse, inverse


def norm_back(e, n, inverse, gain):
    scaled = e * gain
    return inverse * (
        scaled
        - jnp.mean(scaled, axis=-1, keepdims=True)
        - n * jnp.mean(scaled * n, axis=-1, keepdims=True)
    )


def gelu_parts(u):
    gauss = jnp.exp2(u * u * (-0.5 * LOG2E))
    t = 1.0 / (1.0 + (0.3275911 * 0.7071067811865476) * jnp.abs(u))
    poly = t * (
        0.5 * 0.254829592
        + t * (-0.5 * 0.284496736 + t * (0.5 * 1.421413741 + t * (-0.5 * 1.453152027 + t * (0.5 * 1.061405429))))
    )
    tail = poly * gauss
    phi = jnp.where(u >= 0.0, 1.0 - tail, tail)
    return u * phi, phi + u * gauss * 0.3989422804014327


def load_b(cube, b_weights, b_refs, a_weights, a_refs, meta, ups, dn, wo, sems):
    if not cube.tiled:
        pltpu.make_async_copy(b_refs[0], ups, sems.at[0]).start()
        pltpu.make_async_copy(b_refs[1], dn, sems.at[1]).start()
        pltpu.make_async_copy(a_refs[0], wo, sems.at[2]).start()
        return

    def place_b(kind, ref, at, role, device):
        count, first = ((FEW, 0), (MANY, FEW))[role]
        source = ref.at[at, kind * count : (kind + 1) * count]
        return [(source, (ups, dn)[kind].at[device, first : first + count], sems.at[kind])]

    def place_a(ref, at, role, device):
        last = 3 * GROUPS - FEW
        return [(ref.at[at, last : last + GROUPS], wo.at[device], sems.at[2])]

    b_weights.copies(b_refs, meta, functools.partial(place_b, 0))
    b_weights.copies(b_refs, meta, functools.partial(place_b, 1))
    a_weights.copies(a_refs, meta, place_a)


def ffn_kernel(
    cube, layout, pairs, b_weights, a_weights, meta, r_ref, cot_ref, rcot_ref, vec_ref, upb_ref, retr_ref, *refs
):
    nb, na = len(b_weights.arrays), len(a_weights.arrays)
    b_refs, a_refs, refs = refs[:nb], refs[nb : nb + na], refs[nb + na :]
    lo_ref, attn_ref, gctx_ref, sums_ref, gretr_ref = refs[:5]
    outs, refs = refs[5:9], refs[9:]
    ups, dn, wo, slope_ref, sems = refs[:5]
    step = pl.program_id(0)
    seq = r_ref.shape[1]
    if cube.tiled:
        first_ref, act_ref, down_ref, upl_ref = refs[5:9]
        here = pl.ds(pl.multiple_of(step * seq, seq), seq)
    else:
        first_ref, act_ref, down_ref, upl_ref = [o.at[0] for o in outs]
        here = slice(0, seq)
    first_step = step == 0

    @pl.when(first_step)
    def _():
        load_b(cube, b_weights, b_refs, a_weights, a_refs, meta, ups, dn, wo, sems)
        sums_ref[...] = jnp.zeros_like(sums_ref)
        gretr_ref[...] = jnp.zeros_like(gretr_ref)

    vec = lambda i: vec_ref[i : i + 1, :]
    n = cube.n

    def up(c):
        return square(cube, ups, c)

    def down(c):
        return dn[c * n // 4 : (c + 1) * n // 4].reshape(D, D) if cube.tiled else dn[c]

    def pair():
        n1, inv1 = norm_parts(r_ref[0])
        first_norm = n1 * vec(3) + vec(4)
        first_low = first_norm.astype(BF)
        first_ref[here, :] = first_low
        pl.when(first_step)(lambda: wait_load(ups, sems.at[0]))
        output = first_norm + vec(5)
        ahead = dot_nn(first_low, up(0))
        for c in range(4):
            cols = slice(c * D, (c + 1) * D)
            pre = ahead + upb_ref[0:1, cols]
            if c < 3:
                ahead = dot_nn(first_low, up(c + 1))
            active, slope = gelu_parts(pre)
            active = active.astype(BF)
            act_ref[here, cols] = active
            slope_ref[:, cols] = slope
            if c == 0:
                pl.when(first_step)(lambda: wait_load(dn, sems.at[1]))
            output = output + dot_nn(active, down(c))
        n2, inv2 = norm_parts(output)
        result = n2 * vec(6) + vec(7)
        lo_ref[0] = result.astype(BF)
        head = dot_nt(rcot_ref[0], retr_ref[...].reshape(D, -1))
        row = lax.broadcasted_iota(jnp.int32, (seq, 1), 0)
        e = cot_ref[0].astype(F32) + jnp.where(row == 0, head, 0.0)
        top = jnp.where(row[:8] == 0, result[:8], 0.0).astype(BF)
        gretr_ref[...] += dot_tn(top, jnp.broadcast_to(rcot_ref[0], (8, rcot_ref.shape[-1])))
        total = lambda a: jnp.sum(a, axis=0, keepdims=True)
        sums_ref[4:5, 0:D] += total(e * n2)
        sums_ref[5:6, 0:D] += total(e)
        g_second = norm_back(e, n2, inv2, vec(6))
        down_low = g_second.astype(BF)
        down_ref[here, :] = down_low
        sums_ref[3:4, 0:D] += total(down_low.astype(F32))
        g_first = g_second
        ahead = dot_nt(down_low, down(0))
        for c in range(4):
            cols = slice(c * D, (c + 1) * D)
            up_low = (ahead * slope_ref[:, cols]).astype(BF)
            if c < 3:
                ahead = dot_nt(down_low, down(c + 1))
            upl_ref[here, cols] = up_low
            sums_ref[6:7, cols] += total(up_low.astype(F32))
            g_first = g_first + dot_nt(up_low, up(c))
        sums_ref[1:2, 0:D] += total(g_first * n1)
        sums_ref[2:3, 0:D] += total(g_first)
        g_one = norm_back(g_first, n1, inv1, vec(3))
        attn_low = g_one.astype(BF)
        attn_ref[0] = attn_low
        sums_ref[0:1, 0:D] += total(attn_low.astype(F32))
        pl.when(first_step)(lambda: wait_load(wo, sems.at[2]))
        gctx_ref[0] = dot_nt(attn_low, wo[...].reshape(D, D)).astype(BF)

    if not cube.tiled:
        pair()
        return
    pl.when(step < pairs)(pair)

    stage, acc_ref, tmp, out_sems = refs[9:13], *refs[13:16]
    me, core = meta[0], meta[1]
    per = n // 4

    def cols(block):
        return pl.ds(pl.multiple_of(block * D, D), D)

    wide = [slice(0, FEW), slice(0, MANY)] * 2
    down_copies = [
        pltpu.make_async_copy(stage[k].at[:, wide[k]], outs[k].at[:, wide[k]], out_sems.at[k]) for k in range(4)
    ]
    up_copies = unit_copies(stage, outs, out_sems, 4, 1, 2)

    @pl.when((step >= pairs) & (step < pairs + 4))
    def _():
        block = step - pairs
        acc_ref[...] = dot_tn(act_ref[:, cols(block)], down_ref[...]).astype(BF).reshape(acc_ref.shape)
        for half in range(2):

            @pl.when(core == half)
            def _(half=half):
                for i in range(per):
                    owner = (i >> cube.core_bit) & 1
                    out = stage[2:4] if owner == half else stage[0:2]
                    distance = lax.bitwise_xor(me, block * per + i ^ (0 if owner == half else cube.core))
                    slots = [meta[layout.slot + (2 * owner + role) * n + distance] for role in range(2)]
                    for k in range(4):
                        put_unit(out, slots, k, acc_ref.at[4 * i + k], 0)

        @pl.when(block == 3)
        def _():
            for copy in down_copies:
                copy.start()

    @pl.when(step >= pairs + 4)
    def _():
        unit = step - pairs - 4
        acc_ref[...] = dot_tn(first_ref[...], upl_ref[:, cols(unit)]).astype(BF).reshape(acc_ref.shape)
        emit_unit(cube, layout, meta, unit, acc_ref, stage, 1)
        for half in range(2):

            @pl.when((unit == 0) & (core == half))
            def _(half=half):
                rows = cube.rows
                tmp[...] = jnp.zeros_like(tmp)
                for i in range(n):
                    near, slot = small_slot(cube, layout, meta, half, i)
                    out = stage[3 if near else 1]
                    tmp[2:8, 0:rows] = sums_ref[0:6, i * rows : (i + 1) * rows]
                    tmp[0:1, 128 : 128 + 4 * rows] = sums_ref[6:7, i * 4 * rows : (i + 1) * 4 * rows]
                    out[slot, 2 * MANY] = tmp[...].astype(BF)
                    block = gretr_ref[i * rows : (i + 1) * rows, :].astype(BF).reshape(GROUPS, cube.sub, 128)
                    parts = [block[k] for k in range(GROUPS)] + [jnp.zeros((cube.sub, D - 128 * GROUPS), BF)]
                    out[slot, 2 * MANY + 1] = jnp.concatenate(parts, axis=1)

        start_and_end(unit, up_copies, down_copies)


def unit_copies(stage, outs, sems, first, at, small):
    copies = []
    for unit in range(4):
        lo, hi = unit * GROUPS, (unit + 1) * GROUPS
        ranges = []
        if lo < FEW:
            ranges += [(k, at * FEW + lo, at * FEW + min(hi, FEW)) for k in (0, 2)]
        if hi > FEW:
            ranges += [(k, at * MANY + max(lo, FEW) - FEW, at * MANY + hi - FEW) for k in (1, 3)]
        if unit == 0:
            ranges += [(k, (at + 1) * MANY, (at + 1) * MANY + small) for k in (1, 3)]
        each = []
        for k, i, j in ranges:
            each.append(pltpu.make_async_copy(stage[k].at[:, i:j], outs[k].at[:, i:j], sems.at[first]))
            first += 1
        copies.append(each)
    return copies


def start_and_end(unit, copies, before):
    for k in range(4):

        @pl.when(unit == k)
        def _(k=k):
            for copy in copies[k]:
                copy.start()

    @pl.when(unit == 3)
    def _():
        for copy in sum(copies, list(before)):
            copy.wait()


def put_unit(out, slots, unit, block, at):
    first = unit * GROUPS
    few = min(max(FEW - first, 0), GROUPS)
    if few:
        out[0][slots[0], at * FEW + first : at * FEW + first + few] = block[0:few]
    if few < GROUPS:
        start = at * MANY + first + few - FEW
        out[1][slots[1], start : start + GROUPS - few] = block[few:GROUPS]


def emit_unit(cube, layout, meta, unit, acc_ref, outs, at):
    me, core = meta[0], meta[1]
    for k in range(4):

        @pl.when(unit == k)
        def _(k=k):
            for side, base, whose in ((outs[0:2], lax.bitwise_xor(me, cube.core), 1 - core), (outs[2:4], me, core)):
                for role in range(2):
                    if (role == 0 and k * GROUPS >= FEW) or (role == 1 and (k + 1) * GROUPS <= FEW):
                        continue
                    first = k * GROUPS
                    few = min(max(FEW - first, 0), GROUPS)
                    for s in range(cube.slots):
                        owner = lax.bitwise_xor(base, meta[layout.dist + (2 * whose + role) * cube.slots + s])
                        if role == 0:
                            side[0][s, at * FEW + first : at * FEW + first + few] = acc_ref[owner, 0:few]
                        else:
                            start = at * MANY + first + few - FEW
                            side[1][s, start : start + GROUPS - few] = acc_ref[owner, few:GROUPS]


def feed_forward(cube, layout, meta, r, cot, rcot, vecs, upb, retr, b_weights, a_weights):
    pairs, seq, _ = r.shape
    ff = 4 * D
    n, sub = cube.n, cube.sub
    wide = lambda k, t: jax.ShapeDtypeStruct((pairs, seq, k), t)
    at = lambda *shape: pl.BlockSpec((1,) + shape, lambda p, *_: (jnp.minimum(p, pairs - 1),) + (0,) * len(shape))
    if cube.tiled:
        square_shape = (n, GROUPS, sub, D)
        buffers = [(n, BLOCKS, sub, D), (n, BLOCKS, sub, D), square_shape]
        terms = grad_shapes(cube, 2, 2)
        term_specs = any_specs(4)
        total = pairs * seq
        more = [pltpu.VMEM((total, k), BF) for k in (D, ff, D, ff)]
        more += [pltpu.VMEM(t.shape, BF) for t in terms]
        more += [pltpu.VMEM(square_shape, BF), pltpu.VMEM((8, D), F32), pltpu.SemaphoreType.DMA((16,))]
    else:
        buffers = [(4, D, D), (4, D, D), (D, D)]
        terms = [wide(k, BF) for k in (D, ff, D, ff)]
        term_specs = [at(seq, k) for k in (D, ff, D, ff)]
        more = []
    return pl.pallas_call(
        functools.partial(ffn_kernel, cube, layout, pairs, b_weights, a_weights),
        out_shape=[
            wide(D, BF),
            wide(D, BF),
            wide(D, BF),
            jax.ShapeDtypeStruct((8, ff), F32),
            jax.ShapeDtypeStruct((D, rcot.shape[-1]), F32),
        ]
        + terms,
        grid_spec=pltpu.PrefetchScalarGridSpec(
            num_scalar_prefetch=1,
            grid=(pairs + 8 if cube.tiled else pairs,),
            in_specs=[
                at(seq, D),
                at(seq, D),
                at(1, rcot.shape[-1]),
                full_spec(*vecs.shape),
                full_spec(*upb.shape),
                full_spec(*retr.shape),
            ]
            + any_specs(len(b_weights.arrays) + len(a_weights.arrays)),
            out_specs=[
                at(seq, D),
                at(seq, D),
                at(seq, D),
                full_spec(8, ff),
                full_spec(D, rcot.shape[-1]),
            ]
            + term_specs,
            scratch_shapes=[pltpu.VMEM(b, BF) for b in buffers]
            + [pltpu.VMEM((seq, ff), F32), pltpu.SemaphoreType.DMA((3,))]
            + more,
        ),
        compiler_params=params(),
        cost_estimate=cost(pairs * seq * D * 25 * D, 40 * pairs * seq * D),
        name="feed_forward",
    )(meta, r, cot, rcot, vecs, upb, retr, *b_weights.arrays, *a_weights.arrays)


def attn_bwd_kernel(first, joint_ref, p_ref, gctx_ref, *refs):
    if first:
        gj_ref, sums_ref = refs
        sums = jnp.zeros(sums_ref.shape, F32)
    else:
        _, before_ref, gj_ref, sums_ref = refs
        sums = before_ref[...]

    @pl.when(pl.program_id(0) == 0)
    def _():
        sums_ref[...] = sums

    sides = head_masks()
    for h2 in range(H // 2):
        cut = lambda base: slice(base + h2 * 2 * DH, base + (h2 + 1) * 2 * DH)
        q2 = joint_ref[0, :, cut(0)]
        k2 = joint_ref[0, :, cut(D)]
        v2 = joint_ref[0, :, cut(2 * D)]
        go = stack_heads(gctx_ref[0, :, cut(0)], sides)
        p = p_ref[0, h2]
        pf = p.astype(F32)
        t = dot_nt(v2, go) * pf
        gs = (t - pf * jnp.sum(t, axis=0, keepdims=True)).astype(BF)
        gj_ref[0, :, cut(0)] = (join_heads(dot_tn(gs, k2)) * SCALE).astype(BF)
        gj_ref[0, :, cut(D)] = (dot_nn(gs, stack_heads(q2, sides)) * SCALE).astype(BF)
        gj_ref[0, :, cut(2 * D)] = dot_nn(p, go).astype(BF)
    for row, j in ((0, 0), (1, 2)):
        part = gj_ref[0, :, j * D : (j + 1) * D].astype(F32)
        sums_ref[row : row + 1, :] += jnp.sum(part, axis=0, keepdims=True)


def attention_backward(joint, probs, gctx, at, count, before=None):
    pairs, seq, _ = joint.shape
    in_specs = [
        pair_spec(seq, 3 * D, first=at),
        pair_spec(H // 2, seq, 2 * seq, first=at),
        pair_spec(seq, D, first=at),
    ]
    args = [joint, probs, gctx]
    aliases = {}
    if before is not None:
        in_specs += any_specs(1) + [full_spec(8, D)]
        args += list(before)
        aliases = {3: 0}
    return pl.pallas_call(
        functools.partial(attn_bwd_kernel, before is None),
        out_shape=(jax.ShapeDtypeStruct((pairs, seq, 3 * D), BF), jax.ShapeDtypeStruct((8, D), F32)),
        grid=(count,),
        in_specs=in_specs,
        out_specs=(pair_spec(seq, 3 * D, first=at), full_spec(8, D)),
        input_output_aliases=aliases,
        compiler_params=params(),
        cost_estimate=cost(count * seq * D * 16 * seq, 40 * count * seq * D),
        name="attention_backward",
    )(*args)


def token_grad_kernel(cube, weights, meta, gj_ref, gone_ref, *refs):
    count = len(weights.arrays)
    pieces, refs = refs[:count], refs[count:]
    gt_ref, blocks, sem = refs

    @pl.when(pl.program_id(0) == 0)
    def _():
        load_a(cube, weights, meta, pieces, blocks, sem, 3)
        wait_load(blocks, sem)

    acc = gone_ref[...].reshape(-1, D).astype(F32)
    for j in range(3):
        acc = acc + dot_nt(gj_ref[:, :, j * D : (j + 1) * D].reshape(-1, D), square(cube, blocks, j))
    gt_ref[...] = acc.astype(BF).reshape(gt_ref.shape)


def token_grad(cube, meta, g_joint, g_one, weights):
    pairs, seq, _ = g_joint.shape
    per = 2 if pairs % 2 == 0 else 1
    block = lambda width: pl.BlockSpec((per, seq, width), lambda p, *_: (p, 0, 0))
    return pl.pallas_call(
        functools.partial(token_grad_kernel, cube, weights),
        out_shape=jax.ShapeDtypeStruct((pairs, seq, D), BF),
        grid_spec=pltpu.PrefetchScalarGridSpec(
            num_scalar_prefetch=1,
            grid=(pairs // per,),
            in_specs=[block(3 * D), block(D)] + any_specs(len(weights.arrays)),
            out_specs=block(D),
            scratch_shapes=[a_buffer(cube, 3), pltpu.SemaphoreType.DMA],
        ),
        compiler_params=params(),
        cost_estimate=cost(pairs * seq * D * 3 * D, 12 * pairs * seq * D),
        name="token_grad",
    )(meta, g_joint, g_one, *weights.arrays)


def small_slot(cube, layout, meta, half, i):
    owner = (i >> cube.core_bit) & 1
    distance = lax.bitwise_xor(meta[0], i ^ (0 if owner == half else cube.core))
    return owner == half, meta[layout.slot + (2 * owner + 1) * cube.n + distance]


def unit_grad_kernel(cube, layout, meta, a_ref, b_ref, qv_ref, a2_ref, b2_ref, *refs):
    outs, acc_ref, tmp, left2, right2, sems = refs[0:4], *refs[4:9]
    stage = refs[9:13]
    unit = pl.program_id(0)
    core = meta[1]
    late = [pltpu.make_async_copy(a2_ref, left2, sems.at[0]), pltpu.make_async_copy(b2_ref, right2, sems.at[1])]

    def make(left, right):
        acc_ref[...] = dot_tn(left[...], right[...]).astype(BF).reshape(acc_ref.shape)

    @pl.when(unit == 0)
    def _():
        for copy in late:
            copy.start()

    pl.when(unit < 3)(lambda: make(a_ref, b_ref))

    @pl.when(unit == 3)
    def _():
        for copy in late:
            copy.wait()
        make(left2, right2)

    emit_unit(cube, layout, meta, unit, acc_ref, stage, 0)
    for half in range(2):

        @pl.when((unit == 0) & (core == half))
        def _(half=half):
            tmp[...] = jnp.zeros_like(tmp)
            for i in range(cube.n):
                near, slot = small_slot(cube, layout, meta, half, i)
                tmp[0:2, 0 : cube.rows] = qv_ref[0:2, i * cube.rows : (i + 1) * cube.rows]
                stage[3 if near else 1][slot, MANY] = tmp[...].astype(BF)

    start_and_end(unit, unit_copies(stage, outs, sems, 2, 0, 1), [])


def by_distance(cube, meta, units):
    me, core = meta[0], meta[1]
    dist = jnp.asarray([cube.dist(p) for p in range(4)], jnp.int32)
    blocks = jnp.concatenate([u.reshape(cube.n, GROUPS, cube.sub, D) for u in units], axis=1)
    parts = [blocks[:, :FEW], blocks[:, FEW:]]
    out = []
    for whose in (1, 0):
        base = me ^ (cube.core * whose)
        out.append([jnp.take(parts[role], base ^ dist[2 * (core ^ whose) + role], axis=0) for role in range(2)])
    return out


def grad_plain_kernel(a_ref, b_ref, out_ref):
    out_ref[...] = dot_tn(a_ref[...], b_ref[...]).astype(BF)


def plain_grad(a, b):
    return pl.pallas_call(
        grad_plain_kernel,
        out_shape=jax.ShapeDtypeStruct((D, D), BF),
        grid=(1,),
        in_specs=[full_spec(*a.shape), full_spec(*b.shape)],
        out_specs=full_spec(D, D),
        compiler_params=params(),
        name="plain_grad",
    )(a, b)


def grad_shapes(cube, sets, small):
    few = (cube.slots, sets * FEW, cube.sub, D)
    many = (cube.slots, sets * MANY + small, cube.sub, D)
    return [jax.ShapeDtypeStruct(s, BF) for s in (few, many, few, many)]


def plain_terms(cube, meta, sums, gretr, first_low, active, down_low, up_low):
    n = cube.n
    blocks = [plain_grad(active[:, j * D : (j + 1) * D], down_low) for j in range(4)]
    whole = jnp.concatenate(blocks, axis=0).reshape(n, 4, -1, D)
    down = sum(by_distance(cube, meta, [whole[:, j] for j in range(4)]), [])
    ups = [plain_grad(first_low, up_low[:, j * D : (j + 1) * D]).reshape(n, -1, D) for j in range(4)]
    up = sum(by_distance(cube, meta, ups), [])
    terms = [jnp.concatenate(pair, axis=1) for pair in zip(down, up)]
    small = small_by_distance(cube, meta, jnp.zeros((2, D), F32), sums, gretr)
    for k in range(2):
        terms[2 * k + 1] = jnp.concatenate([terms[2 * k + 1], small[k]], axis=1)
    return terms


def unit_grads(cube, layout, meta, a, b, tail):
    n = cube.n
    total = a.shape[0]
    if not cube.tiled:
        pairs = [(a, b[:, j * D : (j + 1) * D]) for j in range(b.shape[1] // D)] + [tail[:2]]
        send, keep = by_distance(cube, meta, [plain_grad(x, y).reshape(n, -1, D) for x, y in pairs])
        small = small_by_distance(cube, meta, tail[2], None, None)
        send[1] = jnp.concatenate([send[1], small[0]], axis=1)
        keep[1] = jnp.concatenate([keep[1], small[1]], axis=1)
        return send + keep
    top = b.shape[1] // D - 1
    args = [a, b]
    in_specs = [
        full_spec(total, D),
        pl.BlockSpec((total, D), lambda s, *_: (0, jnp.minimum(s, top))),
    ]
    args += [tail[2], tail[0], tail[1]]
    in_specs += [full_spec(*tail[2].shape)] + any_specs(2)
    return pl.pallas_call(
        functools.partial(unit_grad_kernel, cube, layout),
        out_shape=grad_shapes(cube, 1, 1),
        grid_spec=pltpu.PrefetchScalarGridSpec(
            num_scalar_prefetch=1,
            grid=(4,),
            in_specs=in_specs,
            out_specs=any_specs(4),
            scratch_shapes=[pltpu.VMEM((n, GROUPS, cube.sub, D), BF), pltpu.VMEM((8, D), F32)]
            + [pltpu.VMEM((total, D), BF)] * 2
            + [pltpu.SemaphoreType.DMA((14,))]
            + [pltpu.VMEM(t.shape, BF) for t in grad_shapes(cube, 1, 1)],
        ),
        compiler_params=params(),
        cost_estimate=cost(total * D * 4 * D, 40 * D * D),
        name="unit_grads",
    )(meta, *args)


class Reduce:
    def __init__(self, cube, terms):
        self.cube = cube
        self.terms = terms[2:]
        self.flight = [cube.swap_core(s) for s in terms[:2]]
        self.r = cube.rounds

    @staticmethod
    def add(a, b):
        return a.astype(F32) + b.astype(F32)

    def tie(self, *values):
        out, self.flight = lax.optimization_barrier((values, self.flight))
        return out[0] if len(out) == 1 else out

    def step(self, other=None):
        self.r -= 1
        pairs = list(zip(self.terms, self.flight))
        half = self.terms[0].shape[0] // 2
        away = [self.add(a[half:], b[half:]).astype(BF) for a, b in pairs]
        self.terms = [self.add(a[:half], b[:half]).astype(BF) for a, b in pairs]
        if other is not None:
            away, other.flight = lax.optimization_barrier((away, other.flight))
        self.flight = [self.cube.swap(away[role], role, self.r) for role in range(2)]

    def finish(self):
        self.r = 0
        pairs = list(zip(self.terms, self.flight))
        away = [[self.add(a[s : s + 1], b[s : s + 1]).astype(BF) for s in (3, 2, 1)] for a, b in pairs]
        self.terms = [self.add(a[:1], b[:1]) for a, b in pairs]
        self.flight = [
            [self.cube.swap_rounds(x, role, r) for x, r in zip(away[role], ((0, 1), (1,), (0,)))]
            for role in reversed(range(2))
        ][::-1]

    def result(self):
        shards = []
        for term, got in zip(self.terms, self.flight):
            total = term.astype(F32)
            for g in got if isinstance(got, list) else [got]:
                total = total + g.astype(F32)
            shards.append(total[0])
        return shards


def small_by_distance(cube, meta, sums_qv, sums, gretr):
    n, rows = cube.n, cube.rows
    me, core = meta[0], meta[1]
    wide = cube.small * cube.sub
    vec = jnp.zeros((6, D), F32) if sums is None else sums[:6, :D]
    upb = jnp.zeros((4 * D,), F32) if sums is None else sums[6]
    vec = jnp.concatenate([sums_qv[:2], vec], axis=0)
    vec = jnp.pad(vec.reshape(8, n, rows).transpose(1, 0, 2), ((0, 0), (0, wide - 8), (0, 128 - rows)))
    upb = jnp.pad(upb.reshape(n, 1, 4 * rows), ((0, 0), (0, wide - 1), (0, D - 128 - 4 * rows)))
    block = jnp.concatenate([vec, upb], axis=2)
    if gretr is not None:
        more = jnp.pad(gretr.reshape(n, 1, -1), ((0, 0), (0, wide - 1), (0, D - rows * gretr.shape[1])))
        block = jnp.concatenate([block, more], axis=1)
    dist = jnp.asarray([cube.dist(1), cube.dist(3)], jnp.int32)
    out = []
    for whose in (1, 0):
        part = jnp.take(block.astype(BF), (me ^ (cube.core * whose)) ^ dist[core ^ whose], axis=0)
        out.append(part.reshape(cube.slots, -1, cube.sub, D))
    return out


def per_device(cube, tokens, pair_lengths, out_cotangent, retr_cotangent, *weights):
    (
        qkv_weight,
        query_bias,
        value_bias,
        out_weight,
        out_bias,
        first_gain,
        first_shift,
        up_weight,
        up_bias,
        down_weight,
        down_bias,
        second_gain,
        second_shift,
        retr_weight,
    ) = weights
    me = (lax.axis_index("dp") * lax.axis_size("fsdp") + lax.axis_index("fsdp")).astype(jnp.int32)
    n, rows = cube.n, cube.rows
    core = (me >> cube.core_bit) & 1
    pairs, seq, _ = tokens.shape
    proj = retr_weight.shape[1]
    layout = Meta(cube, pairs)
    meta = Meta.build(cube, me, core, pair_lengths)

    own_vec = jnp.stack(
        [query_bias, value_bias, out_bias, first_gain, first_shift, down_bias, second_gain, second_shift]
    )
    own = pack_own(cube, qkv_weight, out_weight, up_weight, down_weight, retr_weight, own_vec, up_bias[None])
    gather = Gather(cube, own)
    pieces_a = gather.side_a()
    rcot = retr_cotangent[:, None, :]
    if cube.tiled:
        a_weights = Weights(cube, layout, pieces_a)
        odd_weights = Weights(cube, layout, [p for p in pieces_a if p[1] == 1])
        joint, probs, ctx, r, vecs, upb, retr = attention_forward(cube, layout, meta, tokens, a_weights)
        r, pieces_b = gather.side_b(r)
        b_weights = Weights(cube, layout, pieces_b)
    else:
        few, many = natural_blocks(cube, me, core, pieces_a)
        natural = four_units(cube, jnp.concatenate([few, many[:, :MANY]], axis=1))
        natural = [u.reshape(D, D) for u in natural]
        tiny, retr = [
            many[:, at : at + cube.small].reshape(n, -1, D) for at in (MANY, MANY + cube.small)
        ]
        tiny = tiny.astype(F32)
        vecs = tiny[:, :8, :rows].transpose(1, 0, 2).reshape(8, D)
        upb = tiny[:, 0, 128 : 128 + 4 * rows].reshape(1, 4 * D)
        retr = retr[:, 0, : rows * proj].reshape(D, proj)
        a_weights = Weights(cube, layout, natural=natural)
        odd_weights = Weights(cube, layout, natural=natural[3:])
        joint, probs, ctx, r = attention_forward(cube, layout, meta, tokens, a_weights, vecs)
        r, pieces_b = gather.side_b(r)
        few, many = natural_blocks(cube, me, core, pieces_b)
        ups = four_units(cube, jnp.concatenate([few[:, :FEW], many[:, :MANY]], axis=1))
        ups = jnp.stack([u.reshape(D, D) for u in ups])
        downs = jnp.concatenate([few[:, FEW:], many[:, MANY:]], axis=1).reshape(4, D, D)
        b_weights = Weights(cube, layout, natural=[ups, downs])

    layer_output, attn_low, g_ctx, sums, g_retr, *terms = feed_forward(
        cube, layout, meta, r, out_cotangent, rcot, vecs, upb, retr, b_weights, odd_weights
    )
    flat = lambda a: a.reshape(pairs * seq, a.shape[-1])
    if not cube.tiled:
        terms = plain_terms(cube, meta, sums, g_retr, *[flat(t) for t in terms])
    g_ctx, terms = lax.optimization_barrier((g_ctx, terms))
    ffn = Reduce(cube, terms)

    calls = [1, pairs - 1]
    state, at = None, 0
    for count in calls:
        state = ffn.tie(attention_backward(joint, probs, g_ctx, at, count, state))
        at += count
        if ffn.r:
            ffn.step()
    g_joint, sums_qv = state
    tail_args = (flat(ctx), flat(attn_low), sums_qv)
    terms = unit_grads(cube, layout, meta, flat(tokens), flat(g_joint), tail_args)
    terms = ffn.tie(terms)
    tail = Reduce(cube, terms)
    ffn.step()
    g_joint = tail.tie(g_joint)
    tail.step()
    grad_tokens = token_grad(cube, meta, g_joint, attn_low, a_weights)
    grad_tokens = tail.tie(grad_tokens)
    ffn.flight = tail.tie(ffn.flight)
    tail.step(ffn)
    ffn.step()
    while tail.r > 2:
        tail.step()
    ffn.flight = tail.tie(ffn.flight)
    tail.finish()
    while ffn.r:
        ffn.step()

    few, many = tail.result()
    grad_q, grad_k, grad_v, grad_o = jnp.concatenate([few, many[:MANY]], axis=0).reshape(4, rows, D)
    own_qv = many[MANY:].reshape(-1, D)
    few, many = ffn.result()
    grad_down = jnp.concatenate([few[:FEW], many[:MANY]], axis=0).reshape(4 * rows, D)
    ups = jnp.concatenate([few[FEW:], many[MANY : 2 * MANY]], axis=0).reshape(4, rows, D)
    own_vec, own_retr = many[2 * MANY :].reshape(2, -1, D)
    take = lambda i: own_vec[i, :rows]
    if cube.tiled:
        own_retr = own_retr[:8, : GROUPS * proj].reshape(8, GROUPS, proj).transpose(1, 0, 2).reshape(rows, proj)
    else:
        own_retr = own_retr[0, : rows * proj].reshape(rows, proj)
    return (
        layer_output,
        grad_tokens,
        jnp.concatenate([grad_q, grad_k, grad_v], axis=1),
        own_qv[0, :rows],
        own_qv[1, :rows],
        grad_o,
        take(2),
        take(3),
        take(4),
        jnp.concatenate(list(ups), axis=1),
        own_vec[0, 128 : 128 + 4 * rows],
        grad_down,
        take(5),
        take(6),
        take(7),
        own_retr,
    )


def solution(mesh):
    row = P(AXES)
    return jax.shard_map(
        functools.partial(per_device, Cube(mesh)),
        mesh=mesh,
        in_specs=(row,) * 18,
        out_specs=(row,) * 16,
        check_vma=False,
    )
```
